32 devices in a mesh: cube: 32 (over z, y, x, core).
Axes of the slice: x: 2, y: 2, z: 4, core: 2. Of those that a mesh axis runs over, the one named last changes fastest.
Arguments:
- vectors: bfloat16 [131072, 768], P('cube'), may hold values from -40 to 40
- child_labels: int32 [2, 131072], P(None, 'cube'), may hold values from 0 to 1, as said below
Outputs:
- held: bfloat16 [229376, 768], P('cube')
- margin_one: float32 [196608], P('cube')
- margin_two: float32 [229376], P('cube')
- centroids: float32 [6, 768], replicated
The draws below stay inside these ranges and needn't reach their ends.
Inputs may be any that keep to these rules, and one draw needn't show every extreme that they name: `child_labels`: per device, the vectors leaving at the first level number from 1024 to 2048, and 2048 on some device in every draw. `child_labels`: per device, the second-level leavers among its vectors that stay at the first level number at most 512, and among the vectors it sends away at the first level at most 512; in every draw some device holds 512 second-level leavers of each kind (its own stayers and those received at the first level), so its second-level send buffer is full.
All inputs are finite; a program needn't handle non-finite values.
Results may differ from the reference program's by a relative error of at most 0.0011.
Values may be sent and summed in bfloat16 or wider, within the bound.
No kernel may reach another device: no remote copies, remote signals or barrier semaphores. Data moves between devices by JAX's collectives and lax.ppermute only.
A program may use at most 128 MiB of HBM per device.

```python
from functools import partial
import jax
import jax.numpy as jnp

D = 768
ROWS = 4096
N_CUBE = 32


def label_plan(key):
    ways = N_CUBE
    levels = ways.bit_length() - 1
    cap_one = ROWS // 2
    cap_two = ROWS // 4
    device = jnp.arange(ways, dtype=jnp.int32)
    bit_one = device >> levels - 1 & 1
    bit_two = device >> levels - 2 & 1
    keys = jax.random.split(key, 5)
    orders = jax.vmap(lambda k: jax.random.permutation(k, ROWS))(jax.random.split(keys[0], ways))
    rank = jnp.argsort(orders, axis=1).astype(jnp.int32)
    hot = jax.random.randint(keys[1], (), 0, ways)
    sends = jax.random.randint(keys[2], (ways,), cap_one // 2, cap_one + 1)
    sends = jnp.where(device == hot, cap_one, sends)
    stays_out = jax.random.randint(keys[3], (ways,), cap_two // 4, cap_two // 2 + 1)
    stays_out = jnp.where(device == hot, cap_two // 2, stays_out)
    sent_out = jax.random.randint(keys[4], (ways,), cap_two // 4, cap_two // 2 + 1)
    sent_out = jnp.where(device == hot ^ 1 << levels - 1, cap_two // 2, sent_out)
    miss_one = rank < sends[:, None]
    miss_two = jnp.where(miss_one, rank < sent_out[:, None], rank - sends[:, None] < stays_out[:, None])
    first = bit_one[:, None] ^ miss_one.astype(jnp.int32)
    later = bit_two[:, None] ^ miss_two.astype(jnp.int32)
    return (first.reshape(-1), later.reshape(-1))


def draw_child_labels(key, part):
    first, later = label_plan(key)
    return jnp.stack([first, later]).astype(jnp.int32)


def draw_vectors(key, part):
    first, later = label_plan(key)
    key = jax.random.fold_in(key, 7)
    keys = jax.random.split(key, 3)
    ways = N_CUBE
    device = jnp.arange(ways * ROWS) // ROWS
    spread = 3.0 ** (device.astype(jnp.float32) / (ways - 1))
    axis_one = jax.random.normal(keys[0], (D,), jnp.float32)
    axis_two = jax.random.normal(keys[1], (D,), jnp.float32)
    noise = jax.random.normal(keys[2], (ways * ROWS, D), jnp.float32)
    sign_one = (2 * first - 1).astype(jnp.float32)[:, None]
    sign_two = (2 * later - 1).astype(jnp.float32)[:, None]
    signal = 0.6 * spread[:, None] * (sign_one * axis_one[None] + sign_two * axis_two[None])
    return jnp.clip(noise + signal, -40.0, 40.0).astype(jnp.bfloat16)


def setup_inputs(seed: int = 0) -> dict:
    seeds = jax.random.split(jax.random.key(seed), 3)
    vectors = draw_vectors(jax.random.fold_in(seeds[2], 71), 0)
    child_labels = draw_child_labels(jax.random.fold_in(seeds[2], 71), 0)
    return dict(vectors=vectors, child_labels=child_labels)


def compact(mask, rows, cap, fill):
    place = jnp.cumsum(mask.astype(jnp.int32)) - 1
    index = jnp.where(mask, place, cap).astype(jnp.int32)
    base = jnp.full((cap + 1,) + rows.shape[1:], fill, rows.dtype)
    return base.at[index].set(rows)[:cap]


def split_margin(held_rows, live, pair):
    scores = jnp.dot(held_rows, pair.astype(jnp.bfloat16).T, preferred_element_type=jnp.float32)
    offset = 0.5 * (jnp.sum(pair[1] * pair[1]) - jnp.sum(pair[0] * pair[0]))
    return jnp.where(live, (scores[:, 1] - scores[:, 0] - offset) / D, jnp.float32(0.0))


def group_sum(values, group, count):
    return jnp.stack([jnp.sum(jnp.where((group == g)[:, None], values, jnp.float32(0.0)), axis=0) for g in range(count)])


def reference(vectors, child_labels):
    ways = N_CUBE
    levels = ways.bit_length() - 1
    device = jnp.arange(ways, dtype=jnp.int32)
    bit_one = (device >> (levels - 1)) & 1
    bit_two = (device >> (levels - 2)) & 1
    rows = vectors.reshape(ways, ROWS, D)
    first = child_labels[0].reshape(ways, ROWS)
    later = child_labels[1].reshape(ways, ROWS)
    cap_one = ROWS // 2
    cap_two = ROWS // 4
    leave = first != bit_one[:, None]
    stay = jnp.logical_not(leave)
    send_rows = jax.vmap(partial(compact, cap=cap_one, fill=0))(leave, rows)
    send_tags = jax.vmap(partial(compact, cap=cap_one, fill=-1))(leave, later)
    partner = device ^ (1 << (levels - 1))
    held_one = jnp.concatenate([jnp.where(stay[..., None], rows, jnp.zeros((), jnp.bfloat16)), send_rows[partner]], axis=1)
    tags = jnp.concatenate([jnp.where(stay, later, -1), send_tags[partner]], axis=1)
    live_one = tags >= 0
    sum_one = jnp.sum(held_one, axis=1, dtype=jnp.float32)
    count_one = jnp.sum(live_one, axis=1).astype(jnp.float32)
    centre_one = group_sum(sum_one, bit_one, 2) / group_sum(count_one[:, None], bit_one, 2)
    margin_one = jax.vmap(split_margin, in_axes=(0, 0, None))(held_one, live_one, centre_one)
    moving = live_one & (tags != bit_two[:, None])
    out_rows = jax.vmap(partial(compact, cap=cap_two, fill=0))(moving, held_one)
    out_tags = jax.vmap(partial(compact, cap=cap_two, fill=-1))(moving, tags)
    other = device ^ (1 << (levels - 2))
    held_two = jnp.concatenate([jnp.where(moving[..., None], jnp.zeros((), jnp.bfloat16), held_one), out_rows[other]], axis=1)
    live_two = jnp.concatenate([live_one & jnp.logical_not(moving), out_tags[other] >= 0], axis=1)
    group = 2 * bit_one + bit_two
    sum_two = jnp.sum(held_two, axis=1, dtype=jnp.float32)
    count_two = jnp.sum(live_two, axis=1).astype(jnp.float32)
    centre_two = group_sum(sum_two, group, 4) / group_sum(count_two[:, None], group, 4)
    pairs = centre_two.reshape(2, 2, D)[bit_one]
    margin_two = jax.vmap(split_margin)(held_two, live_two, pairs)
    centroids = jnp.concatenate([centre_one, centre_two], axis=0)
    return (held_two.reshape(ways * (ROWS + cap_one + cap_two), D), margin_one.reshape(-1), margin_two.reshape(-1), centroids)
```

```python
import functools
import jax
import jax.numpy as jnp
from jax import lax
from jax.experimental import pallas as pl
from jax.experimental.pallas import tpu as pltpu
from jax.sharding import PartitionSpec as P

BF = jnp.bfloat16
F32 = jnp.float32
I32 = jnp.int32
BLK = 256
PARTS = 4
VMEM_BYTES = 48 * 1024 * 1024


def swap(x, bits):
    return lax.ppermute(x, "cube", [(i, i ^ bits) for i in range(lax.axis_size("cube"))])


def dot(a, b):
    return lax.dot_general(a, b, (((1,), (0,)), ((), ())), preferred_element_type=F32)


def dot_t(a, b):
    return lax.dot_general(a, b, (((1,), (1,)), ((), ())), preferred_element_type=F32)


def iota(shape, dim):
    return lax.broadcasted_iota(I32, shape, dim)


def as_bf(mask):
    return jnp.where(mask, jnp.float32(1), jnp.float32(0)).astype(BF)


def pack(sums, counts, width):
    high = sums.astype(BF).astype(F32)
    middle = (sums - high).astype(BF).astype(F32)
    low = sums - high - middle
    spare = width - 128 * len(counts)
    counts = jnp.concatenate(counts + ([jnp.zeros((1, spare), I32)] if spare else []), axis=1)
    upper, lower = (counts >> 8).astype(F32), (counts & 255).astype(F32)
    return jnp.concatenate([high, middle, low, upper, lower, jnp.zeros((2, width), F32)], axis=0).astype(BF)


def unpack(extra):
    extra = extra.astype(F32)
    sums = extra[0:4] + extra[4:8] + extra[8:12]
    return sums, extra[12:13] * 256.0 + extra[13:14]


def count_at(extra, k):
    extra = extra[12:14, 128 * k : 128 * k + 1].astype(F32)
    return (extra[0:1] * 256.0 + extra[1:2]).astype(I32)


def spec(memory):
    return pl.BlockSpec(memory_space=memory)


def params():
    return pltpu.CompilerParams(vmem_limit_bytes=VMEM_BYTES)


def sort_kernel(here, labels, x_hbm, *refs):
    outs, (pos_ref, off_ref, x, buf, tail, sem_in, sem_out) = refs[:PARTS], refs[PARTS:]
    rows = labels.shape[1]
    blocks = rows // BLK
    cap = rows // 2
    step = rows // PARTS
    loads = [
        pltpu.make_async_copy(x_hbm.at[pl.ds(k * step, step)], x.at[pl.ds(k * step, step)], sem_in.at[k])
        for k in range(PARTS)
    ]
    for load in loads:
        load.start()
    buf[...] = jnp.zeros_like(buf)
    leave = labels[0:1, :] != here[0]
    miss = labels[1:2, :] != here[1]
    code = jnp.where(leave, jnp.where(miss, 0, 1), jnp.where(miss, 2, 3))
    code = jnp.concatenate(
        [jnp.broadcast_to(code[:, b * BLK : (b + 1) * BLK], (8, BLK)) for b in range(blocks)], axis=0
    )
    tall = 8 * blocks
    kind = iota((tall, BLK), 0) & 7
    mask = (code == kind) | ((kind == 4) & (code <= 1))
    maskb = as_bf(mask)
    upper = as_bf(iota((BLK, BLK), 0) <= iota((BLK, BLK), 1))
    before = dot(maskb, upper)
    total = dot(maskb, jnp.ones((BLK, BLK), BF)).astype(BF)
    r, c = iota((tall, tall), 0), iota((tall, tall), 1)
    same = ((r ^ c) & 7) == 0
    earlier = as_bf((same & (c < r)) | (((r & 7) == 1) & ((c & 7) == 0)))
    off = dot(earlier, total)
    pos_ref[...] = jnp.where(mask, (before + off).astype(I32) - 1, -1)
    off_ref[...] = off[:, :128].astype(I32)
    r8, c8 = iota((8, tall), 0), iota((8, tall), 1)
    every = dot(as_bf(r8 == (c8 & 7)), total)[:, :128].astype(I32)
    group = 2 * labels[0:1, :] + labels[1:2, :]
    wide = BLK + 16
    slot = iota((wide, BLK), 0)
    sums = jnp.zeros((4, x.shape[1]), F32)
    for b in range(blocks):
        if b % (step // BLK) == 0:
            loads[b // (step // BLK)].wait()
        hot = []
        bases = []
        for kind in (0, 1):
            base = off_ref[8 * b + kind : 8 * b + kind + 1, 0:1]
            base = jnp.minimum((base[0, 0] // 16) * 16, cap)
            place = pos_ref[8 * b + kind : 8 * b + kind + 1, :]
            hot.append(as_bf(slot == place - base))
            bases.append(pl.multiple_of(base, 16))
        hot.append(as_bf((iota((16, BLK), 0) & 3) == group[:, b * BLK : (b + 1) * BLK]))
        got = dot(jnp.concatenate(hot, axis=0), x[b * BLK : (b + 1) * BLK, :])
        for kind in (0, 1):
            buf[pl.ds(bases[kind], wide), :] += got[kind * wide : (kind + 1) * wide].astype(BF)
        sums += got[2 * wide : 2 * wide + 4]
    one, two = here[0], here[1]
    kinds = [every[k : k + 1] for k in range(4)]
    counts = []
    for g in range(4):
        away, miss = jnp.int32(g >> 1) != one, jnp.int32(g & 1) != two
        counts.append(jnp.where(away, jnp.where(miss, kinds[0], kinds[1]), jnp.where(miss, kinds[2], kinds[3])))
    tail[...] = pack(sums, counts + [kinds[0], kinds[2]], x.shape[1])
    part = cap // PARTS
    stores = [
        pltpu.make_async_copy(buf.at[pl.ds(k * part, part)], outs[k].at[pl.ds(0, part)], sem_out.at[k])
        for k in range(PARTS)
    ]
    stores.append(pltpu.make_async_copy(tail, outs[0].at[pl.ds(part, 16)], sem_out.at[PARTS]))
    for store in stores:
        store.start()
    for store in stores:
        store.wait()


def sort_call(here, labels, vectors):
    rows, width = vectors.shape
    tall = 8 * rows // BLK
    part = rows // 2 // PARTS
    return pl.pallas_call(
        sort_kernel,
        out_shape=[jax.ShapeDtypeStruct((part + (0 if k else 16), width), BF) for k in range(PARTS)]
        + [
            jax.ShapeDtypeStruct((tall, BLK), I32),
            jax.ShapeDtypeStruct((tall, 128), I32),
        ],
        in_specs=[spec(pltpu.SMEM), spec(pltpu.VMEM), spec(pl.ANY)],
        out_specs=[spec(pl.ANY)] * PARTS + [spec(pltpu.VMEM)] * 2,
        scratch_shapes=[
            pltpu.VMEM((rows, width), BF),
            pltpu.VMEM((rows // 2 + BLK + 16, width), BF),
            pltpu.VMEM((16, width), BF),
            pltpu.SemaphoreType.DMA((PARTS,)),
            pltpu.SemaphoreType.DMA((PARTS + 1,)),
        ],
        compiler_params=params(),
        cost_estimate=pl.CostEstimate(flops=8 * 10**9, bytes_accessed=10 * 10**6, transcendentals=0),
        name="sort_leavers",
    )(here, labels, vectors)


def stay_kernel(off, pos, extra, x_ref, held, second, meta, buf, ranks):
    b = pl.program_id(0)

    @pl.when(b == 0)
    def _():
        buf[...] = jnp.zeros_like(buf)
        ranks[...] = jnp.zeros_like(ranks)

    x = x_ref[...]
    half = second.shape[0] - 16
    cap = 4 * half
    stays = pos[3:4, :] >= 0
    diag = as_bf((iota((BLK, BLK), 0) == iota((BLK, BLK), 1)) & stays)
    base = jnp.minimum((off[8 * b + 2, 0] // 16) * 16, half)
    wide = BLK + 16
    hot = as_bf(iota((wide, BLK), 0) == pos[2:3, :] - base)
    got = dot(jnp.concatenate([diag, hot], axis=0), x)
    held[...] = got[:BLK].astype(BF)
    buf[pl.ds(pl.multiple_of(base, 16), wide), :] += got[BLK:].astype(BF)
    rank = pos[4:5, :]
    line = iota((16, BLK), 0)
    value = jnp.where(line == 0, rank >> 8, jnp.where(line == 1, rank & 255, 1))
    value = jnp.where(rank >= 0, value, 0).astype(F32).astype(BF)
    for kind in (0, 1):
        base = pl.multiple_of(jnp.minimum((off[8 * b + kind, 0] // 128) * 128, cap), 128)
        hot = as_bf(iota((BLK + 128, BLK), 0) == pos[kind : kind + 1, :] - base)
        ranks[:, pl.ds(base, BLK + 128)] += dot_t(value, hot)[:8]

    @pl.when(b == pl.num_programs(0) - 1)
    def _():
        second[0:half, :] = buf[0:half, :]
        second[half:, :] = extra[...]
        seen = ranks[2:3, :cap] > 0.5
        rank = (ranks[0:1, :cap] * 256.0 + ranks[1:2, :cap]).astype(I32)
        goal = jnp.where(seen, rank, 1 << 20)
        line = cap // 8
        for k in range(8):
            meta[k : k + 1, :] = goal[:, k * line : (k + 1) * line]


def stay_call(off, pos, first, vectors):
    rows, width = vectors.shape
    cap = rows // 2
    half = rows // 8
    return pl.pallas_call(
        stay_kernel,
        grid=(rows // BLK,),
        out_shape=[
            jax.ShapeDtypeStruct((rows + cap + cap // 2, width), BF),
            jax.ShapeDtypeStruct((half + 16, width), BF),
            jax.ShapeDtypeStruct((8, cap // 8), I32),
        ],
        in_specs=[
            spec(pltpu.SMEM),
            pl.BlockSpec((8, BLK), lambda b: (b, 0)),
            pl.BlockSpec((16, width), lambda b: (half // 16, 0)),
            pl.BlockSpec((BLK, width), lambda b: (b, 0)),
        ],
        out_specs=[
            pl.BlockSpec((BLK, width), lambda b: (b, 0)),
            pl.BlockSpec((half + 16, width), lambda b: (0, 0)),
            pl.BlockSpec((8, cap // 8), lambda b: (0, 0)),
        ],
        scratch_shapes=[pltpu.VMEM((half + BLK + 16, width), BF), pltpu.VMEM((8, cap + BLK + 128), F32)],
        compiler_params=params(),
        cost_estimate=pl.CostEstimate(flops=6 * 10**9, bytes_accessed=14 * 10**6, transcendentals=0),
        name="own_slots",
    )(off, pos, first, vectors)


def margins(score, shift, first, width):
    return (score[first + 1 : first + 2] - score[first : first + 1] - shift) / width


def put_lines(ref, start, values):
    for k in range(values.shape[1] // 128):
        ref[start + k : start + k + 1, :] = values[:, 128 * k : 128 * (k + 1)]


def centre_kernel(here, total, labels, x_ref, cents, centres, shifts, one, two):
    width = x_ref.shape[1]

    @pl.when(pl.program_id(0) == 0)
    def _():
        sums, counts = total[0:4, :], total[4:8, :]
        low = (sums[0:1] + sums[1:2]) / (counts[0:1] + counts[1:2])
        high = (sums[2:3] + sums[3:4]) / (counts[2:3] + counts[3:4])
        groups = sums / counts
        cents[0:1, :] = low
        cents[1:2, :] = high
        cents[2:6, :] = groups
        top = here[0] == 1
        left = jnp.where(top, groups[2:3], groups[0:1])
        right = jnp.where(top, groups[3:4], groups[1:2])
        centres[...] = jnp.concatenate([low, high, left, right, jnp.zeros((12, width), F32)], axis=0).astype(BF)
        for k, (a, b) in enumerate(((low, high), (left, right))):
            shift = 0.5 * (jnp.sum(b * b, axis=1, keepdims=True) - jnp.sum(a * a, axis=1, keepdims=True))
            shifts[k : k + 1, :] = jnp.broadcast_to(shift, (1, 128))

    score = dot_t(centres[...], x_ref[...])
    stay = labels[0:1, :] == here[0]
    keep = stay & (labels[1:2, :] == here[1])
    put_lines(one, 0, jnp.where(stay, margins(score, shifts[0:1, 0:1], 0, width), 0.0))
    put_lines(two, 0, jnp.where(keep, margins(score, shifts[1:2, 0:1], 2, width), 0.0))


def centre_call(here, total, labels, vectors):
    rows, width = vectors.shape
    cap = rows // 2
    return pl.pallas_call(
        centre_kernel,
        grid=(rows // 1024,),
        out_shape=[
            jax.ShapeDtypeStruct((6, width), F32),
            jax.ShapeDtypeStruct((16, width), BF),
            jax.ShapeDtypeStruct((8, 128), F32),
            jax.ShapeDtypeStruct(((rows + cap) // 128, 128), F32),
            jax.ShapeDtypeStruct(((rows + cap + cap // 2) // 128, 128), F32),
        ],
        in_specs=[
            spec(pltpu.SMEM),
            pl.BlockSpec((8, width), lambda b: (0, 0)),
            pl.BlockSpec((2, 1024), lambda b: (0, b)),
            pl.BlockSpec((1024, width), lambda b: (b, 0)),
        ],
        out_specs=[
            pl.BlockSpec((6, width), lambda b: (0, 0)),
            pl.BlockSpec((16, width), lambda b: (0, 0)),
            pl.BlockSpec((8, 128), lambda b: (0, 0)),
            pl.BlockSpec((8, 128), lambda b: (b, 0)),
            pl.BlockSpec((8, 128), lambda b: (b, 0)),
        ],
        compiler_params=params(),
        cost_estimate=pl.CostEstimate(flops=2 * 10**9, bytes_accessed=7 * 10**6, transcendentals=0),
        name="own_margins",
    )(here, total, labels, vectors)


def second_kernel(centres, shifts, second, relay, first, meta, held_in, two_in, held, two, again, start, goals):
    del held_in, two_in
    half = second.shape[0] - 16
    slots = held.shape[0]
    cap = 2 * slots
    have = count_at(second[half:, :], 5)
    more = count_at(relay[half:, :], 4)
    both = count_at(first[half:, :], 4)
    lane = iota((1, half), 1)
    goal = jnp.where(lane < more, lane + have, -1)
    moved = dot(as_bf(iota((slots, half), 0) == goal), relay[0:half, :]).astype(BF)
    held[0:half, :] = moved[0:half] + second[0:half, :]
    held[half:, :] = moved[half:]
    score = dot_t(centres[...], held[...])
    width = held.shape[1]
    live = iota((1, slots), 1) < have + more
    put_lines(two, 0, jnp.where(live, margins(score, shifts[1:2, 0:1], 2, width), 0.0))

    score = dot_t(centres[...], first[0:half, :])
    value = jnp.where(lane < both, margins(score, shifts[0:1, 0:1], 0, width), 0.0)
    high = value.astype(BF).astype(F32)
    middle = (value - high).astype(BF).astype(F32)
    low = value - high - middle
    value = jnp.concatenate([high, middle, low, jnp.zeros((13, half), F32)], axis=0).astype(BF)
    place = jnp.concatenate([meta[k : k + 1, :] for k in range(8)], axis=1)
    goal = jnp.where(lane < both, place[:, :half], -1)
    for k in range(cap // BLK):
        hot = as_bf(iota((BLK, half), 0) + k * BLK == goal)
        got = dot_t(value, hot)
        put_lines(again, k * BLK // 128, got[0:1] + got[1:2] + got[2:3])
    lane = iota((8, cap), 1)
    earlier = (lane < both) | (place < BLK * iota((8, cap), 0))
    begin = jnp.sum(jnp.where(earlier, 1.0, 0.0), axis=1, keepdims=True).astype(I32)
    begin = jnp.minimum((begin >> 7) << 7, cap - BLK - 128)
    start[...] = jnp.broadcast_to(begin, start.shape)
    goals[...] = jnp.broadcast_to(jnp.where(iota((1, cap), 1) < both, -1, place), goals.shape)


def second_call(centres, shifts, second, relay, first, meta, held, two):
    half, width = second.shape
    half -= 16
    cap = 4 * half
    slots = cap // 2
    return pl.pallas_call(
        second_kernel,
        grid=(1,),
        out_shape=[
            jax.ShapeDtypeStruct(held.shape, BF),
            jax.ShapeDtypeStruct(two.shape, F32),
            jax.ShapeDtypeStruct((cap // 128, 128), F32),
            jax.ShapeDtypeStruct((8, 128), I32),
            jax.ShapeDtypeStruct((8, cap), I32),
        ],
        in_specs=[spec(pltpu.VMEM)] * 6 + [spec(pl.ANY)] * 2,
        out_specs=[
            pl.BlockSpec((slots, width), lambda b: (held.shape[0] // slots - 1, 0)),
            pl.BlockSpec((slots // 128, 128), lambda b: (held.shape[0] // slots - 1, 0)),
            pl.BlockSpec((cap // 128, 128), lambda b: (0, 0)),
            pl.BlockSpec((8, 128), lambda b: (0, 0)),
            pl.BlockSpec((8, cap), lambda b: (0, 0)),
        ],
        input_output_aliases={6: 0, 7: 1},
        compiler_params=params(),
        cost_estimate=pl.CostEstimate(flops=3 * 10**9, bytes_accessed=6 * 10**6, transcendentals=0),
        name="second_slots",
    )(centres, shifts, second, relay, first, meta, held, two)


def column_kernel(own, a, b, c, out):
    sums, counts = unpack(own[...])
    for other in (a, b, c):
        s, n = unpack(other[...])
        sums, counts = sums + s, counts + n
    out[0:4, :] = sums
    width = out.shape[1]
    for g in range(4):
        out[4 + g : 5 + g, :] = jnp.broadcast_to(counts[:, 128 * g : 128 * g + 1], (1, width))


def column_call(*pieces):
    rows, width = pieces[0].shape
    return pl.pallas_call(
        column_kernel,
        grid=(1,),
        out_shape=jax.ShapeDtypeStruct((8, width), F32),
        in_specs=[pl.BlockSpec((16, width), lambda b: (rows // 16 - 1, 0))] * 4,
        out_specs=pl.BlockSpec((8, width), lambda b: (0, 0)),
        compiler_params=params(),
        name="column_sums",
    )(*pieces)


def first_kernel(start, centres, shifts, goals, again, *refs):
    pieces, (held_in, one_in, two_in, held, one, two, x, sem) = refs[:PARTS], refs[PARTS:]
    del held_in, one_in, two_in
    k = pl.program_id(0)
    part, width = pieces[1].shape

    @pl.when(k == 0)
    def _():
        loads = [
            pltpu.make_async_copy(pieces[i].at[pl.ds(0, part)], x.at[pl.ds(i * part, part)], sem.at[i])
            for i in range(PARTS)
        ]
        for load in loads:
            load.start()
        for load in loads:
            load.wait()

    span = BLK + 128
    begin = pl.multiple_of(start[k, 0], 128)
    goal = goals[0:1, pl.ds(begin, span)] - k * BLK
    hot = as_bf(iota((BLK, span), 0) == goal)
    rows = dot(hot, x[pl.ds(begin, span), :]).astype(BF)
    held[...] = rows
    score = dot_t(centres[...], rows)
    live = dot_t(jnp.ones((16, span), BF), hot)[0:1] > 0.5
    m_one = margins(score, shifts[0:1, 0:1], 0, width)
    m_two = margins(score, shifts[1:2, 0:1], 2, width)
    for i in range(BLK // 128):
        line = k * (BLK // 128) + i
        part_live = live[:, 128 * i : 128 * (i + 1)]
        one[pl.ds(line, 1), :] = jnp.where(part_live, m_one[:, 128 * i : 128 * (i + 1)], again[pl.ds(line, 1), :])
        two[pl.ds(line, 1), :] = jnp.where(part_live, m_two[:, 128 * i : 128 * (i + 1)], 0.0)


def first_call(start, centres, shifts, goals, again, pieces, held, one, two):
    width = held.shape[1]
    cap = goals.shape[1]
    base = 2 * cap // BLK
    lines = cap // 128
    return pl.pallas_call(
        first_kernel,
        grid=(cap // BLK,),
        out_shape=[
            jax.ShapeDtypeStruct(held.shape, BF),
            jax.ShapeDtypeStruct(one.shape, F32),
            jax.ShapeDtypeStruct(two.shape, F32),
        ],
        in_specs=[spec(pltpu.SMEM)] + [spec(pltpu.VMEM)] * 4 + [spec(pl.ANY)] * (PARTS + 3),
        out_specs=[
            pl.BlockSpec((BLK, width), lambda k: (base + k, 0)),
            pl.BlockSpec((lines, 128), lambda k: (2, 0)),
            pl.BlockSpec((lines, 128), lambda k: (2, 0)),
        ],
        scratch_shapes=[pltpu.VMEM((cap, width), BF), pltpu.SemaphoreType.DMA((PARTS,))],
        input_output_aliases={5 + PARTS: 0, 6 + PARTS: 1, 7 + PARTS: 2},
        compiler_params=params(),
        cost_estimate=pl.CostEstimate(flops=3 * 10**9, bytes_accessed=7 * 10**6, transcendentals=0),
        name="first_slots",
    )(start, centres, shifts, goals, again, *pieces, held, one, two)


def local(vectors, child_labels):
    ways = lax.axis_size("cube")
    top = ways // 2
    nxt = ways // 4
    me = lax.axis_index("cube")
    here = jnp.stack([(me // top) & 1, (me // nxt) & 1]).astype(I32)
    *pieces, pos, off = sort_call(here, child_labels, vectors)
    got = []
    for k, piece in enumerate(pieces):
        if k >= 2:
            piece, got[k - 2] = lax.optimization_barrier((piece, got[k - 2]))
        got.append(swap(piece, top))
    held, second, meta = stay_call(off, pos, pieces[0], vectors)
    second_in = swap(second, nxt)
    meta_in = swap(meta, top)
    relay = swap(got[0], nxt)
    total = column_call(pieces[0], second_in, got[0], relay)
    bit = 1
    while bit < nxt:
        total = total + swap(total, bit)
        bit *= 2
    cents, centres, shifts, one, two = centre_call(here, total, child_labels, vectors)
    held, two, again, start, goals = second_call(centres, shifts, second_in, relay, got[0], meta_in, held, two)
    held, one, two = first_call(start, centres, shifts, goals, again, got, held, one, two)
    return held, one.reshape(-1), two.reshape(-1), cents


def solution(mesh):
    return jax.shard_map(
        local,
        mesh=mesh,
        in_specs=(P("cube", None), P(None, "cube")),
        out_specs=(P("cube", None), P("cube"), P("cube"), P()),
        check_vma=False,
    )
```

```python
import functools
import jax
import jax.numpy as jnp
from jax import lax
from jax.experimental import pallas as pl
from jax.experimental.pallas import tpu as pltpu
from jax.sharding import PartitionSpec as P

BF = jnp.bfloat16
F32 = jnp.float32
I32 = jnp.int32
BLK = 256
HANDS = 8
VMEM_BYTES = 48 * 1024 * 1024


def swap(x, bits):
    return lax.ppermute(x, "cube", [(i, i ^ bits) for i in range(lax.axis_size("cube"))])


def dot(a, b):
    return lax.dot_general(a, b, (((1,), (0,)), ((), ())), preferred_element_type=F32)


def dot_t(a, b):
    return lax.dot_general(a, b, (((1,), (1,)), ((), ())), preferred_element_type=F32)


def iota(shape, dim):
    return lax.broadcasted_iota(I32, shape, dim)


def as_bf(mask):
    return jnp.where(mask, jnp.float32(1), jnp.float32(0)).astype(BF)


def pack(sums, counts, width):
    high = sums.astype(BF).astype(F32)
    middle = (sums - high).astype(BF).astype(F32)
    low = sums - high - middle
    spare = width - 128 * len(counts)
    counts = jnp.concatenate(counts + ([jnp.zeros((1, spare), I32)] if spare else []), axis=1)
    upper, lower = (counts >> 8).astype(F32), (counts & 255).astype(F32)
    return jnp.concatenate([high, middle, low, upper, lower, jnp.zeros((2, width), F32)], axis=0).astype(BF)


def unpack(extra):
    extra = extra.astype(F32)
    sums = extra[0:4] + extra[4:8] + extra[8:12]
    return sums, extra[12:13] * 256.0 + extra[13:14]


def count_at(extra, k):
    extra = extra[12:14, 128 * k : 128 * k + 1].astype(F32)
    return (extra[0:1] * 256.0 + extra[1:2]).astype(I32)


def spec(memory):
    return pl.BlockSpec(memory_space=memory)


def params():
    return pltpu.CompilerParams(vmem_limit_bytes=VMEM_BYTES)


def plan_kernel(here, labels, pos, off_ref, every, leavers):
    rows = labels.shape[1]
    blocks = rows // BLK
    leave = labels[0:1, :] != here[0]
    miss = labels[1:2, :] != here[1]
    code = jnp.where(leave, jnp.where(miss, 0, 1), jnp.where(miss, 2, 3))
    code = jnp.concatenate(
        [jnp.broadcast_to(code[:, b * BLK : (b + 1) * BLK], (8, BLK)) for b in range(blocks)], axis=0
    )
    tall = 8 * blocks
    kind = iota((tall, BLK), 0) & 7
    mask = (code == kind) | ((kind == 4) & (code <= 1))
    maskb = as_bf(mask)
    upper = as_bf(iota((BLK, BLK), 0) <= iota((BLK, BLK), 1))
    before = dot(maskb, upper)
    total = dot(maskb, jnp.ones((BLK, BLK), BF)).astype(BF)
    r, c = iota((tall, tall), 0), iota((tall, tall), 1)
    same = ((r ^ c) & 7) == 0
    earlier = as_bf((same & (c < r)) | (((r & 7) == 1) & ((c & 7) == 0)))
    off = dot(earlier, total)
    pos[...] = jnp.where(mask, (before + off).astype(I32) - 1, -1)
    off_ref[...] = off[:, :128].astype(I32)
    r8, c8 = iota((8, tall), 0), iota((8, tall), 1)
    count = dot(as_bf(r8 == (c8 & 7)), total)[:, :128].astype(I32)
    every[...] = count
    leavers[...] = jnp.broadcast_to(count[4:5], leavers.shape)


def plan_call(here, labels):
    rows = labels.shape[1]
    tall = 8 * rows // BLK
    return pl.pallas_call(
        plan_kernel,
        out_shape=[
            jax.ShapeDtypeStruct((tall, BLK), I32),
            jax.ShapeDtypeStruct((tall, 128), I32),
            jax.ShapeDtypeStruct((8, 128), I32),
            jax.ShapeDtypeStruct((8, 128), I32),
        ],
        in_specs=[spec(pltpu.SMEM), spec(pltpu.VMEM)],
        out_specs=[spec(pltpu.VMEM)] * 4,
        compiler_params=params(),
        cost_estimate=pl.CostEstimate(flops=10**8, bytes_accessed=10**5, transcendentals=0),
        name="plan_places",
    )(here, labels)


def sort_kernel(here, labels, pos_ref, off_ref, every, x_hbm, first, middle, rest, x, buf, tail, sem_in, sem_out):
    rows = labels.shape[1]
    blocks = rows // BLK
    cap = rows // 2
    step = rows // 4
    loads = [
        pltpu.make_async_copy(x_hbm.at[pl.ds(k * step, step)], x.at[pl.ds(k * step, step)], sem_in.at[k])
        for k in range(4)
    ]
    for load in loads:
        load.start()
    buf[...] = jnp.zeros_like(buf)
    group = 2 * labels[0:1, :] + labels[1:2, :]
    wide = BLK + 16
    slot = iota((wide, BLK), 0)
    sums = jnp.zeros((4, x.shape[1]), F32)
    for b in range(blocks):
        if b % (step // BLK) == 0:
            loads[b // (step // BLK)].wait()
        hot = []
        bases = []
        for kind in (0, 1):
            base = off_ref[8 * b + kind : 8 * b + kind + 1, 0:1]
            base = jnp.minimum((base[0, 0] // 16) * 16, cap)
            place = pos_ref[8 * b + kind : 8 * b + kind + 1, :]
            hot.append(as_bf(slot == place - base))
            bases.append(pl.multiple_of(base, 16))
        hot.append(as_bf((iota((16, BLK), 0) & 3) == group[:, b * BLK : (b + 1) * BLK]))
        got = dot(jnp.concatenate(hot, axis=0), x[b * BLK : (b + 1) * BLK, :])
        for kind in (0, 1):
            buf[pl.ds(bases[kind], wide), :] += got[kind * wide : (kind + 1) * wide].astype(BF)
        sums += got[2 * wide : 2 * wide + 4]
    one, two = here[0], here[1]
    kinds = [every[k : k + 1] for k in range(4)]
    counts = []
    for g in range(4):
        away, miss = jnp.int32(g >> 1) != one, jnp.int32(g & 1) != two
        counts.append(jnp.where(away, jnp.where(miss, kinds[0], kinds[1]), jnp.where(miss, kinds[2], kinds[3])))
    tail[...] = pack(sums, counts + [kinds[0], kinds[2]], x.shape[1])
    part = cap // 4
    stores = [
        pltpu.make_async_copy(buf.at[pl.ds(0, part)], first.at[pl.ds(0, part)], sem_out.at[0]),
        pltpu.make_async_copy(buf.at[pl.ds(part, part)], middle, sem_out.at[1]),
        pltpu.make_async_copy(buf.at[pl.ds(2 * part, 2 * part)], rest, sem_out.at[2]),
        pltpu.make_async_copy(tail, first.at[pl.ds(part, 16)], sem_out.at[3]),
    ]
    for store in stores:
        store.start()
    for store in stores:
        store.wait()


def sort_call(here, labels, pos, off, every, vectors):
    rows, width = vectors.shape
    part = rows // 8
    return pl.pallas_call(
        sort_kernel,
        out_shape=[
            jax.ShapeDtypeStruct((part + 16, width), BF),
            jax.ShapeDtypeStruct((part, width), BF),
            jax.ShapeDtypeStruct((2 * part, width), BF),
        ],
        in_specs=[spec(pltpu.SMEM)] + [spec(pltpu.VMEM)] * 4 + [spec(pl.ANY)],
        out_specs=[spec(pl.ANY)] * 3,
        scratch_shapes=[
            pltpu.VMEM((rows, width), BF),
            pltpu.VMEM((rows // 2 + BLK + 16, width), BF),
            pltpu.VMEM((16, width), BF),
            pltpu.SemaphoreType.DMA((4,)),
            pltpu.SemaphoreType.DMA((4,)),
        ],
        compiler_params=params(),
        cost_estimate=pl.CostEstimate(flops=8 * 10**9, bytes_accessed=10 * 10**6, transcendentals=0),
        name="sort_leavers",
    )(here, labels, pos, off, every, vectors)


def deal_kernel(rest, own, near, top, far, *refs):
    hands, (tail, sem) = refs[:HANDS], refs[HANDS:]
    rows, width = rest.shape
    turns = rows // 16 // HANDS
    counts = jnp.concatenate([ref[0:1, :] for ref in (own, near, top, far)], axis=1)
    counts = jnp.concatenate([counts, jnp.zeros((1, width - 512), I32)], axis=1)
    upper, lower = (counts >> 8).astype(F32), (counts & 255).astype(F32)
    tail[...] = jnp.concatenate([upper, lower, jnp.zeros((14, width), F32)], axis=0).astype(BF)
    copies = []
    for h, hand in enumerate(hands):
        for turn in range(turns):
            block = rest.at[pl.ds(16 * (h + HANDS * turn), 16)]
            copies.append(pltpu.make_async_copy(block, hand.at[pl.ds(16 * turn, 16)], sem.at[h, turn]))
        copies.append(pltpu.make_async_copy(tail, hand.at[pl.ds(16 * turns, 16)], sem.at[h, turns]))
    for copy in copies:
        copy.start()
    for copy in copies:
        copy.wait()


def deal_call(rest, *counts):
    rows, width = rest.shape
    turns = rows // 16 // HANDS
    return pl.pallas_call(
        deal_kernel,
        out_shape=[jax.ShapeDtypeStruct((16 * turns + 16, width), BF)] * HANDS,
        in_specs=[spec(pl.ANY)] + [spec(pltpu.VMEM)] * 4,
        out_specs=[spec(pl.ANY)] * HANDS,
        scratch_shapes=[pltpu.VMEM((16, width), BF), pltpu.SemaphoreType.DMA((HANDS, turns + 1))],
        compiler_params=params(),
        cost_estimate=pl.CostEstimate(flops=0, bytes_accessed=3 * 10**6, transcendentals=0),
        name="deal_rest",
    )(rest, *counts)


def pack_kernel(step, *refs):
    hands, (out, longest, begins) = refs[:HANDS], refs[HANDS:]
    rows = hands[0].shape[0] - 16
    out[...] = jnp.zeros_like(out)
    full = []
    for hand in hands:
        count = hand[rows : rows + 2, 0:512].astype(F32)
        count = (count[0:1] * 256.0 + count[1:2]).astype(I32)
        full.append((jnp.maximum(count - rows * HANDS, 0) + 15) >> 4)
    place = jnp.zeros((1, 512), I32)
    for h, hand in enumerate(hands):
        base = pl.multiple_of(place[0, 0] * 16, 16)
        out[pl.ds(base, rows), :] = hand[0:rows, :]
        begins[h : h + 1, :] = place[:, 256:384] * 16
        place = jnp.minimum(place + ((full[h] + (HANDS - 1 - h)) >> 3), (h + 1) * (rows // 16))
    most = jnp.zeros((1, 512), I32)
    for other in range(HANDS):
        size = jnp.zeros((1, 512), I32)
        for h in range(HANDS):
            size = size + ((full[other ^ h] + (HANDS - 1 - h)) >> 3)
        most = jnp.maximum(most, size)
    most = jnp.max(most.astype(F32), axis=1, keepdims=True).astype(I32)
    per = step // 16
    longest[...] = jnp.broadcast_to(jnp.minimum(most + per - 1, out.shape[0] // 16) // per, longest.shape)


def pack_call(step, hands):
    rows, width = hands[0].shape
    rows -= 16
    return pl.pallas_call(
        functools.partial(pack_kernel, step),
        out_shape=[
            jax.ShapeDtypeStruct((rows * HANDS, width), BF),
            jax.ShapeDtypeStruct((8, 128), I32),
            jax.ShapeDtypeStruct((8, 128), I32),
        ],
        in_specs=[spec(pltpu.VMEM)] * HANDS,
        out_specs=[spec(pltpu.VMEM)] * 3,
        compiler_params=params(),
        cost_estimate=pl.CostEstimate(flops=0, bytes_accessed=3 * 10**6, transcendentals=0),
        name="pack_hands",
    )(*hands)


def part_kernel(begins, pack_in, *refs):
    hands, sem = refs[:HANDS], refs[HANDS]
    rows = hands[0].shape[0]
    copies = []
    for h, hand in enumerate(hands):
        base = pl.multiple_of((begins[h, 0] // 16) * 16, 16)
        copies.append(pltpu.make_async_copy(pack_in.at[pl.ds(base, rows)], hand, sem.at[h]))
    for copy in copies:
        copy.start()
    for copy in copies:
        copy.wait()


def part_call(begins, pack_in):
    rows, width = pack_in.shape
    return pl.pallas_call(
        part_kernel,
        out_shape=[jax.ShapeDtypeStruct((rows // HANDS, width), BF)] * HANDS,
        in_specs=[spec(pltpu.SMEM), spec(pl.ANY)],
        out_specs=[spec(pl.ANY)] * HANDS,
        scratch_shapes=[pltpu.SemaphoreType.DMA((HANDS,))],
        compiler_params=params(),
        cost_estimate=pl.CostEstimate(flops=0, bytes_accessed=3 * 10**6, transcendentals=0),
        name="part_pack",
    )(begins, pack_in)


def stay_kernel(off, pos, extra, x_ref, held, second, meta, buf, ranks):
    b = pl.program_id(0)

    @pl.when(b == 0)
    def _():
        buf[...] = jnp.zeros_like(buf)
        ranks[...] = jnp.zeros_like(ranks)

    x = x_ref[...]
    half = second.shape[0] - 16
    cap = 4 * half
    stays = pos[3:4, :] >= 0
    diag = as_bf((iota((BLK, BLK), 0) == iota((BLK, BLK), 1)) & stays)
    base = jnp.minimum((off[8 * b + 2, 0] // 16) * 16, half)
    wide = BLK + 16
    hot = as_bf(iota((wide, BLK), 0) == pos[2:3, :] - base)
    got = dot(jnp.concatenate([diag, hot], axis=0), x)
    held[...] = got[:BLK].astype(BF)
    buf[pl.ds(pl.multiple_of(base, 16), wide), :] += got[BLK:].astype(BF)
    rank = pos[4:5, :]
    line = iota((16, BLK), 0)
    value = jnp.where(line == 0, rank >> 8, jnp.where(line == 1, rank & 255, 1))
    value = jnp.where(rank >= 0, value, 0).astype(F32).astype(BF)
    for kind in (0, 1):
        base = pl.multiple_of(jnp.minimum((off[8 * b + kind, 0] // 128) * 128, cap), 128)
        hot = as_bf(iota((BLK + 128, BLK), 0) == pos[kind : kind + 1, :] - base)
        ranks[:, pl.ds(base, BLK + 128)] += dot_t(value, hot)[:8]

    @pl.when(b == pl.num_programs(0) - 1)
    def _():
        second[0:half, :] = buf[0:half, :]
        second[half:, :] = extra[...]
        seen = ranks[2:3, :cap] > 0.5
        rank = (ranks[0:1, :cap] * 256.0 + ranks[1:2, :cap]).astype(I32)
        goal = jnp.where(seen, rank, 1 << 20)
        line = cap // 8
        for k in range(8):
            meta[k : k + 1, :] = goal[:, k * line : (k + 1) * line]


def stay_call(off, pos, first, vectors):
    rows, width = vectors.shape
    cap = rows // 2
    half = rows // 8
    return pl.pallas_call(
        stay_kernel,
        grid=(rows // BLK,),
        out_shape=[
            jax.ShapeDtypeStruct((rows + cap + cap // 2, width), BF),
            jax.ShapeDtypeStruct((half + 16, width), BF),
            jax.ShapeDtypeStruct((8, cap // 8), I32),
        ],
        in_specs=[
            spec(pltpu.SMEM),
            pl.BlockSpec((8, BLK), lambda b: (b, 0)),
            pl.BlockSpec((16, width), lambda b: (half // 16, 0)),
            pl.BlockSpec((BLK, width), lambda b: (b, 0)),
        ],
        out_specs=[
            pl.BlockSpec((BLK, width), lambda b: (b, 0)),
            pl.BlockSpec((half + 16, width), lambda b: (0, 0)),
            pl.BlockSpec((8, cap // 8), lambda b: (0, 0)),
        ],
        scratch_shapes=[pltpu.VMEM((half + BLK + 16, width), BF), pltpu.VMEM((8, cap + BLK + 128), F32)],
        compiler_params=params(),
        cost_estimate=pl.CostEstimate(flops=6 * 10**9, bytes_accessed=14 * 10**6, transcendentals=0),
        name="own_slots",
    )(off, pos, first, vectors)


def margins(score, shift, first, width):
    return (score[first + 1 : first + 2] - score[first : first + 1] - shift) / width


def put_lines(ref, start, values):
    for k in range(values.shape[1] // 128):
        ref[start + k : start + k + 1, :] = values[:, 128 * k : 128 * (k + 1)]


def centre_kernel(here, total, labels, x_ref, cents, centres, shifts, one, two):
    width = x_ref.shape[1]

    @pl.when(pl.program_id(0) == 0)
    def _():
        sums, counts = total[0:4, :], total[4:8, :]
        low = (sums[0:1] + sums[1:2]) / (counts[0:1] + counts[1:2])
        high = (sums[2:3] + sums[3:4]) / (counts[2:3] + counts[3:4])
        groups = sums / counts
        cents[0:1, :] = low
        cents[1:2, :] = high
        cents[2:6, :] = groups
        top = here[0] == 1
        left = jnp.where(top, groups[2:3], groups[0:1])
        right = jnp.where(top, groups[3:4], groups[1:2])
        centres[...] = jnp.concatenate([low, high, left, right, jnp.zeros((12, width), F32)], axis=0).astype(BF)
        for k, (a, b) in enumerate(((low, high), (left, right))):
            shift = 0.5 * (jnp.sum(b * b, axis=1, keepdims=True) - jnp.sum(a * a, axis=1, keepdims=True))
            shifts[k : k + 1, :] = jnp.broadcast_to(shift, (1, 128))

    score = dot_t(centres[...], x_ref[...])
    stay = labels[0:1, :] == here[0]
    keep = stay & (labels[1:2, :] == here[1])
    put_lines(one, 0, jnp.where(stay, margins(score, shifts[0:1, 0:1], 0, width), 0.0))
    put_lines(two, 0, jnp.where(keep, margins(score, shifts[1:2, 0:1], 2, width), 0.0))


def centre_call(here, total, labels, vectors):
    rows, width = vectors.shape
    cap = rows // 2
    return pl.pallas_call(
        centre_kernel,
        grid=(rows // 1024,),
        out_shape=[
            jax.ShapeDtypeStruct((6, width), F32),
            jax.ShapeDtypeStruct((16, width), BF),
            jax.ShapeDtypeStruct((8, 128), F32),
            jax.ShapeDtypeStruct(((rows + cap) // 128, 128), F32),
            jax.ShapeDtypeStruct(((rows + cap + cap // 2) // 128, 128), F32),
        ],
        in_specs=[
            spec(pltpu.SMEM),
            pl.BlockSpec((8, width), lambda b: (0, 0)),
            pl.BlockSpec((2, 1024), lambda b: (0, b)),
            pl.BlockSpec((1024, width), lambda b: (b, 0)),
        ],
        out_specs=[
            pl.BlockSpec((6, width), lambda b: (0, 0)),
            pl.BlockSpec((16, width), lambda b: (0, 0)),
            pl.BlockSpec((8, 128), lambda b: (0, 0)),
            pl.BlockSpec((8, 128), lambda b: (b, 0)),
            pl.BlockSpec((8, 128), lambda b: (b, 0)),
        ],
        compiler_params=params(),
        cost_estimate=pl.CostEstimate(flops=2 * 10**9, bytes_accessed=7 * 10**6, transcendentals=0),
        name="own_margins",
    )(here, total, labels, vectors)


def second_kernel(centres, shifts, second, relay, first, meta, held_in, two_in, held, two, again, start, goals):
    del held_in, two_in
    half = second.shape[0] - 16
    slots = held.shape[0]
    cap = 2 * slots
    have = count_at(second[half:, :], 5)
    more = count_at(relay[half:, :], 4)
    both = count_at(first[half:, :], 4)
    lane = iota((1, half), 1)
    goal = jnp.where(lane < more, lane + have, -1)
    moved = dot(as_bf(iota((slots, half), 0) == goal), relay[0:half, :]).astype(BF)
    held[0:half, :] = moved[0:half] + second[0:half, :]
    held[half:, :] = moved[half:]
    score = dot_t(centres[...], held[...])
    width = held.shape[1]
    live = iota((1, slots), 1) < have + more
    put_lines(two, 0, jnp.where(live, margins(score, shifts[1:2, 0:1], 2, width), 0.0))

    score = dot_t(centres[...], first[0:half, :])
    value = jnp.where(lane < both, margins(score, shifts[0:1, 0:1], 0, width), 0.0)
    high = value.astype(BF).astype(F32)
    middle = (value - high).astype(BF).astype(F32)
    low = value - high - middle
    value = jnp.concatenate([high, middle, low, jnp.zeros((13, half), F32)], axis=0).astype(BF)
    place = jnp.concatenate([meta[k : k + 1, :] for k in range(8)], axis=1)
    goal = jnp.where(lane < both, place[:, :half], -1)
    for k in range(cap // BLK):
        hot = as_bf(iota((BLK, half), 0) + k * BLK == goal)
        got = dot_t(value, hot)
        put_lines(again, k * BLK // 128, got[0:1] + got[1:2] + got[2:3])
    lane = iota((8, cap), 1)
    earlier = (lane < both) | (place < BLK * iota((8, cap), 0))
    begin = jnp.sum(jnp.where(earlier, 1.0, 0.0), axis=1, keepdims=True).astype(I32)
    begin = jnp.minimum((begin >> 7) << 7, cap - BLK - 128)
    start[...] = jnp.broadcast_to(begin, start.shape)
    goals[...] = jnp.broadcast_to(jnp.where(iota((1, cap), 1) < both, -1, place), goals.shape)


def second_call(centres, shifts, second, relay, first, meta, held, two):
    half, width = second.shape
    half -= 16
    cap = 4 * half
    slots = cap // 2
    return pl.pallas_call(
        second_kernel,
        grid=(1,),
        out_shape=[
            jax.ShapeDtypeStruct(held.shape, BF),
            jax.ShapeDtypeStruct(two.shape, F32),
            jax.ShapeDtypeStruct((cap // 128, 128), F32),
            jax.ShapeDtypeStruct((8, 128), I32),
            jax.ShapeDtypeStruct((8, cap), I32),
        ],
        in_specs=[spec(pltpu.VMEM)] * 6 + [spec(pl.ANY)] * 2,
        out_specs=[
            pl.BlockSpec((slots, width), lambda b: (held.shape[0] // slots - 1, 0)),
            pl.BlockSpec((slots // 128, 128), lambda b: (held.shape[0] // slots - 1, 0)),
            pl.BlockSpec((cap // 128, 128), lambda b: (0, 0)),
            pl.BlockSpec((8, 128), lambda b: (0, 0)),
            pl.BlockSpec((8, cap), lambda b: (0, 0)),
        ],
        input_output_aliases={6: 0, 7: 1},
        compiler_params=params(),
        cost_estimate=pl.CostEstimate(flops=3 * 10**9, bytes_accessed=6 * 10**6, transcendentals=0),
        name="second_slots",
    )(centres, shifts, second, relay, first, meta, held, two)


def column_kernel(own, a, b, c, out):
    sums, counts = unpack(own[...])
    for other in (a, b, c):
        s, n = unpack(other[...])
        sums, counts = sums + s, counts + n
    out[0:4, :] = sums
    width = out.shape[1]
    for g in range(4):
        out[4 + g : 5 + g, :] = jnp.broadcast_to(counts[:, 128 * g : 128 * g + 1], (1, width))


def column_call(*pieces):
    width = pieces[0].shape[1]
    return pl.pallas_call(
        column_kernel,
        grid=(1,),
        out_shape=jax.ShapeDtypeStruct((8, width), F32),
        in_specs=[pl.BlockSpec((16, width), functools.partial(lambda last, b: (last, 0), p.shape[0] // 16 - 1)) for p in pieces],
        out_specs=pl.BlockSpec((8, width), lambda b: (0, 0)),
        compiler_params=params(),
        name="column_sums",
    )(*pieces)


def first_kernel(start, centres, shifts, goals, again, first, middle, *refs):
    hands, (held_in, one_in, two_in, held, one, two, x, sem) = refs[:HANDS], refs[HANDS:]
    del held_in, one_in, two_in
    k = pl.program_id(0)
    part, width = middle.shape

    @pl.when(k == 0)
    def _():
        turns = hands[0].shape[0] // 16
        loads = [
            pltpu.make_async_copy(first.at[pl.ds(0, part)], x.at[pl.ds(0, part)], sem.at[HANDS, 0]),
            pltpu.make_async_copy(middle, x.at[pl.ds(part, part)], sem.at[HANDS, 1]),
        ]
        for h, hand in enumerate(hands):
            for turn in range(turns):
                block = x.at[pl.ds(2 * part + 16 * (h + HANDS * turn), 16)]
                loads.append(pltpu.make_async_copy(hand.at[pl.ds(16 * turn, 16)], block, sem.at[h, turn]))
        for load in loads:
            load.start()
        for load in loads:
            load.wait()

    span = BLK + 128
    begin = pl.multiple_of(start[k, 0], 128)
    goal = goals[0:1, pl.ds(begin, span)] - k * BLK
    hot = as_bf(iota((BLK, span), 0) == goal)
    rows = dot(hot, x[pl.ds(begin, span), :]).astype(BF)
    held[...] = rows
    score = dot_t(centres[...], rows)
    live = dot_t(jnp.ones((16, span), BF), hot)[0:1] > 0.5
    m_one = margins(score, shifts[0:1, 0:1], 0, width)
    m_two = margins(score, shifts[1:2, 0:1], 2, width)
    for i in range(BLK // 128):
        line = k * (BLK // 128) + i
        part_live = live[:, 128 * i : 128 * (i + 1)]
        one[pl.ds(line, 1), :] = jnp.where(part_live, m_one[:, 128 * i : 128 * (i + 1)], again[pl.ds(line, 1), :])
        two[pl.ds(line, 1), :] = jnp.where(part_live, m_two[:, 128 * i : 128 * (i + 1)], 0.0)


def first_call(start, centres, shifts, goals, again, first, middle, hands, held, one, two):
    width = held.shape[1]
    cap = goals.shape[1]
    base = 2 * cap // BLK
    lines = cap // 128
    return pl.pallas_call(
        first_kernel,
        grid=(cap // BLK,),
        out_shape=[
            jax.ShapeDtypeStruct(held.shape, BF),
            jax.ShapeDtypeStruct(one.shape, F32),
            jax.ShapeDtypeStruct(two.shape, F32),
        ],
        in_specs=[spec(pltpu.SMEM)] + [spec(pltpu.VMEM)] * 4 + [spec(pl.ANY)] * (HANDS + 5),
        out_specs=[
            pl.BlockSpec((BLK, width), lambda k: (base + k, 0)),
            pl.BlockSpec((lines, 128), lambda k: (2, 0)),
            pl.BlockSpec((lines, 128), lambda k: (2, 0)),
        ],
        scratch_shapes=[pltpu.VMEM((cap, width), BF), pltpu.SemaphoreType.DMA((HANDS + 1, cap // 32 // HANDS))],
        input_output_aliases={7 + HANDS: 0, 8 + HANDS: 1, 9 + HANDS: 2},
        compiler_params=params(),
        cost_estimate=pl.CostEstimate(flops=3 * 10**9, bytes_accessed=7 * 10**6, transcendentals=0),
        name="first_slots",
    )(start, centres, shifts, goals, again, first, middle, *hands, held, one, two)


def local(vectors, child_labels):
    ways = lax.axis_size("cube")
    top = ways // 2
    nxt = ways // 4
    me = lax.axis_index("cube")
    here = jnp.stack([(me // top) & 1, (me // nxt) & 1]).astype(I32)
    after = lax.optimization_barrier
    pos, off, every, leavers = plan_call(here, child_labels)
    counts = [leavers] + [swap(leavers, bits) for bits in (nxt, top, top | nxt)]
    first, middle, rest = sort_call(here, child_labels, pos, off, every, vectors)
    first_in = swap(first, top)
    own, *hands = deal_call(rest, *counts)
    pos, own = after((pos, own))
    hands = [own] + [swap(hand, h + 1) for h, hand in enumerate(hands)]
    sums = first[-16:]
    held, second, meta = stay_call(off, pos, first, vectors)
    second_in = swap(second, nxt)
    limit = rest.shape[0]
    step = limit // 16
    packed, longest, begins = pack_call(step, hands)
    bit = HANDS
    while bit < nxt:
        longest = jnp.maximum(longest, swap(longest, bit))
        bit *= 2

    def cross(size):
        def branch(rows, sums, meta):
            got = jnp.pad(swap(rows[:size], top), ((0, limit - size), (0, 0))) if size else jnp.zeros_like(rows)
            return got, swap(sums, top | nxt), swap(meta, top)

        return branch

    sizes = range(0, limit + 1, step)
    packed_in, far_sums, meta_in = lax.switch(longest[0, 0], [cross(size) for size in sizes], packed, sums, meta)
    middle, first_in, packed_in = after((middle, first_in, packed_in))
    middle_in = swap(middle, top)
    own, *hands = part_call(begins, packed_in)
    own, second_in = after((own, second_in))
    hands = [own] + [swap(hand, h + 1) for h, hand in enumerate(hands)]
    relay = swap(first_in, nxt)
    total = column_call(first, second_in, first_in, far_sums)
    bit = 1
    while bit < nxt:
        total = total + swap(total, bit)
        bit *= 2
    cents, centres, shifts, one, two = centre_call(here, total, child_labels, vectors)
    held, two, again, start, goals = second_call(centres, shifts, second_in, relay, first_in, meta_in, held, two)
    held, one, two = first_call(start, centres, shifts, goals, again, first_in, middle_in, hands, held, one, two)
    return held, one.reshape(-1), two.reshape(-1), cents


def solution(mesh):
    return jax.shard_map(
        local,
        mesh=mesh,
        in_specs=(P("cube", None), P(None, "cube")),
        out_specs=(P("cube", None), P("cube"), P("cube"), P()),
        check_vma=False,
    )
```

```python
import functools
import jax
import jax.numpy as jnp
from jax import lax
from jax.experimental import pallas as pl
from jax.experimental.pallas import tpu as pltpu
from jax.sharding import PartitionSpec as P

BF = jnp.bfloat16
F32 = jnp.float32
I32 = jnp.int32
BLK = 256
HANDS = 8
VMEM_BYTES = 48 * 1024 * 1024


def swap(x, bits):
    return lax.ppermute(x, "cube", [(i, i ^ bits) for i in range(lax.axis_size("cube"))])


def dot(a, b):
    return lax.dot_general(a, b, (((1,), (0,)), ((), ())), preferred_element_type=F32)


def dot_t(a, b):
    return lax.dot_general(a, b, (((1,), (1,)), ((), ())), preferred_element_type=F32)


def iota(shape, dim):
    return lax.broadcasted_iota(I32, shape, dim)


def as_bf(mask):
    return jnp.where(mask, jnp.float32(1), jnp.float32(0)).astype(BF)


def pack(sums, counts, width):
    high = sums.astype(BF).astype(F32)
    middle = (sums - high).astype(BF).astype(F32)
    low = sums - high - middle
    spare = width - 128 * len(counts)
    counts = jnp.concatenate(counts + ([jnp.zeros((1, spare), I32)] if spare else []), axis=1)
    upper, lower = (counts >> 8).astype(F32), (counts & 255).astype(F32)
    return jnp.concatenate([high, middle, low, upper, lower, jnp.zeros((2, width), F32)], axis=0).astype(BF)


def unpack(extra):
    extra = extra.astype(F32)
    sums = extra[0:4] + extra[4:8] + extra[8:12]
    return sums, extra[12:13] * 256.0 + extra[13:14]


def count_at(extra, k):
    extra = extra[12:14, 128 * k : 128 * k + 1].astype(F32)
    return (extra[0:1] * 256.0 + extra[1:2]).astype(I32)


def spec(memory):
    return pl.BlockSpec(memory_space=memory)


def params():
    return pltpu.CompilerParams(vmem_limit_bytes=VMEM_BYTES)


def plan_kernel(here, labels, pos, off_ref, every, leavers):
    rows = labels.shape[1]
    blocks = rows // BLK
    leave = labels[0:1, :] != here[0]
    miss = labels[1:2, :] != here[1]
    code = jnp.where(leave, jnp.where(miss, 0, 1), jnp.where(miss, 2, 3))
    code = jnp.concatenate(
        [jnp.broadcast_to(code[:, b * BLK : (b + 1) * BLK], (8, BLK)) for b in range(blocks)], axis=0
    )
    tall = 8 * blocks
    kind = iota((tall, BLK), 0) & 7
    mask = (code == kind) | ((kind == 4) & (code <= 1))
    maskb = as_bf(mask)
    upper = as_bf(iota((BLK, BLK), 0) <= iota((BLK, BLK), 1))
    before = dot(maskb, upper)
    total = dot(maskb, jnp.ones((BLK, BLK), BF)).astype(BF)
    r, c = iota((tall, tall), 0), iota((tall, tall), 1)
    same = ((r ^ c) & 7) == 0
    earlier = as_bf((same & (c < r)) | (((r & 7) == 1) & ((c & 7) == 0)))
    off = dot(earlier, total)
    pos[...] = jnp.where(mask, (before + off).astype(I32) - 1, -1)
    off_ref[...] = off[:, :128].astype(I32)
    r8, c8 = iota((8, tall), 0), iota((8, tall), 1)
    count = dot(as_bf(r8 == (c8 & 7)), total)[:, :128].astype(I32)
    every[...] = count
    leavers[...] = jnp.broadcast_to(count[4:5], leavers.shape)


def plan_call(here, labels):
    rows = labels.shape[1]
    tall = 8 * rows // BLK
    return pl.pallas_call(
        plan_kernel,
        out_shape=[
            jax.ShapeDtypeStruct((tall, BLK), I32),
            jax.ShapeDtypeStruct((tall, 128), I32),
            jax.ShapeDtypeStruct((8, 128), I32),
            jax.ShapeDtypeStruct((8, 128), I32),
        ],
        in_specs=[spec(pltpu.SMEM), spec(pltpu.VMEM)],
        out_specs=[spec(pltpu.VMEM)] * 4,
        compiler_params=params(),
        cost_estimate=pl.CostEstimate(flops=10**8, bytes_accessed=10**5, transcendentals=0),
        name="plan_places",
    )(here, labels)


def sort_kernel(here, labels, pos_ref, off_ref, every, x_hbm, first, middle, rest, x, buf, tail, sem_in, sem_out):
    rows = labels.shape[1]
    blocks = rows // BLK
    cap = rows // 2
    step = rows // 4
    loads = [
        pltpu.make_async_copy(x_hbm.at[pl.ds(k * step, step)], x.at[pl.ds(k * step, step)], sem_in.at[k])
        for k in range(4)
    ]
    for load in loads:
        load.start()
    buf[...] = jnp.zeros_like(buf)
    group = 2 * labels[0:1, :] + labels[1:2, :]
    wide = BLK + 16
    slot = iota((wide, BLK), 0)
    sums = jnp.zeros((4, x.shape[1]), F32)
    for b in range(blocks):
        if b % (step // BLK) == 0:
            loads[b // (step // BLK)].wait()
        hot = []
        bases = []
        for kind in (0, 1):
            base = off_ref[8 * b + kind : 8 * b + kind + 1, 0:1]
            base = jnp.minimum((base[0, 0] // 16) * 16, cap)
            place = pos_ref[8 * b + kind : 8 * b + kind + 1, :]
            hot.append(as_bf(slot == place - base))
            bases.append(pl.multiple_of(base, 16))
        hot.append(as_bf((iota((16, BLK), 0) & 3) == group[:, b * BLK : (b + 1) * BLK]))
        got = dot(jnp.concatenate(hot, axis=0), x[b * BLK : (b + 1) * BLK, :])
        for kind in (0, 1):
            buf[pl.ds(bases[kind], wide), :] += got[kind * wide : (kind + 1) * wide].astype(BF)
        sums += got[2 * wide : 2 * wide + 4]
    one, two = here[0], here[1]
    kinds = [every[k : k + 1] for k in range(4)]
    counts = []
    for g in range(4):
        away, miss = jnp.int32(g >> 1) != one, jnp.int32(g & 1) != two
        counts.append(jnp.where(away, jnp.where(miss, kinds[0], kinds[1]), jnp.where(miss, kinds[2], kinds[3])))
    tail[...] = pack(sums, counts + [kinds[0], kinds[2]], x.shape[1])
    part = cap // 4
    stores = [
        pltpu.make_async_copy(buf.at[pl.ds(0, part)], first.at[pl.ds(0, part)], sem_out.at[0]),
        pltpu.make_async_copy(buf.at[pl.ds(part, part)], middle, sem_out.at[1]),
        pltpu.make_async_copy(buf.at[pl.ds(2 * part, 2 * part)], rest, sem_out.at[2]),
        pltpu.make_async_copy(tail, first.at[pl.ds(part, 16)], sem_out.at[3]),
    ]
    for store in stores:
        store.start()
    for store in stores:
        store.wait()


def sort_call(here, labels, pos, off, every, vectors):
    rows, width = vectors.shape
    part = rows // 8
    return pl.pallas_call(
        sort_kernel,
        out_shape=[
            jax.ShapeDtypeStruct((part + 16, width), BF),
            jax.ShapeDtypeStruct((part, width), BF),
            jax.ShapeDtypeStruct((2 * part, width), BF),
        ],
        in_specs=[spec(pltpu.SMEM)] + [spec(pltpu.VMEM)] * 4 + [spec(pl.ANY)],
        out_specs=[spec(pl.ANY), spec(pltpu.HBM), spec(pl.ANY)],
        scratch_shapes=[
            pltpu.VMEM((rows, width), BF),
            pltpu.VMEM((rows // 2 + BLK + 16, width), BF),
            pltpu.VMEM((16, width), BF),
            pltpu.SemaphoreType.DMA((4,)),
            pltpu.SemaphoreType.DMA((4,)),
        ],
        compiler_params=params(),
        cost_estimate=pl.CostEstimate(flops=8 * 10**9, bytes_accessed=10 * 10**6, transcendentals=0),
        name="sort_leavers",
    )(here, labels, pos, off, every, vectors)


def deal_kernel(rest, own, near, top, far, *refs):
    hands, (tail, sem) = refs[:HANDS], refs[HANDS:]
    rows, width = rest.shape
    turns = rows // 16 // HANDS
    counts = jnp.concatenate([ref[0:1, :] for ref in (own, near, top, far)], axis=1)
    counts = jnp.concatenate([counts, jnp.zeros((1, width - 512), I32)], axis=1)
    upper, lower = (counts >> 8).astype(F32), (counts & 255).astype(F32)
    tail[...] = jnp.concatenate([upper, lower, jnp.zeros((14, width), F32)], axis=0).astype(BF)
    copies = []
    for h, hand in enumerate(hands):
        for turn in range(turns):
            block = rest.at[pl.ds(16 * (h + HANDS * turn), 16)]
            copies.append(pltpu.make_async_copy(block, hand.at[pl.ds(16 * turn, 16)], sem.at[h, turn]))
        copies.append(pltpu.make_async_copy(tail, hand.at[pl.ds(16 * turns, 16)], sem.at[h, turns]))
    for copy in copies:
        copy.start()
    for copy in copies:
        copy.wait()


def deal_call(rest, *counts):
    rows, width = rest.shape
    turns = rows // 16 // HANDS
    return pl.pallas_call(
        deal_kernel,
        out_shape=[jax.ShapeDtypeStruct((16 * turns + 16, width), BF)] * HANDS,
        in_specs=[spec(pl.ANY)] + [spec(pltpu.VMEM)] * 4,
        out_specs=[spec(pl.ANY)] * HANDS,
        scratch_shapes=[pltpu.VMEM((16, width), BF), pltpu.SemaphoreType.DMA((HANDS, turns + 1))],
        compiler_params=params(),
        cost_estimate=pl.CostEstimate(flops=0, bytes_accessed=3 * 10**6, transcendentals=0),
        name="deal_rest",
    )(rest, *counts)


def pack_kernel(step, *refs):
    hands, (out, longest, begins) = refs[:HANDS], refs[HANDS:]
    rows = hands[0].shape[0] - 16
    out[...] = jnp.zeros_like(out)
    full = []
    for hand in hands:
        count = hand[rows : rows + 2, 0:512].astype(F32)
        count = (count[0:1] * 256.0 + count[1:2]).astype(I32)
        full.append((jnp.maximum(count - rows * HANDS, 0) + 15) >> 4)
    place = jnp.zeros((1, 512), I32)
    for h, hand in enumerate(hands):
        base = pl.multiple_of(place[0, 0] * 16, 16)
        out[pl.ds(base, rows), :] = hand[0:rows, :]
        begins[h : h + 1, :] = place[:, 256:384] * 16
        place = jnp.minimum(place + ((full[h] + (HANDS - 1 - h)) >> 3), (h + 1) * (rows // 16))
    most = jnp.zeros((1, 512), I32)
    for other in range(HANDS):
        size = jnp.zeros((1, 512), I32)
        for h in range(HANDS):
            size = size + ((full[other ^ h] + (HANDS - 1 - h)) >> 3)
        most = jnp.maximum(most, size)
    most = jnp.max(most.astype(F32), axis=1, keepdims=True).astype(I32)
    per = step // 16
    longest[...] = jnp.broadcast_to(jnp.minimum(most + per - 1, out.shape[0] // 16) // per, longest.shape)


def pack_call(step, hands):
    rows, width = hands[0].shape
    rows -= 16
    return pl.pallas_call(
        functools.partial(pack_kernel, step),
        out_shape=[
            jax.ShapeDtypeStruct((rows * HANDS, width), BF),
            jax.ShapeDtypeStruct((8, 128), I32),
            jax.ShapeDtypeStruct((8, 128), I32),
        ],
        in_specs=[spec(pltpu.VMEM)] * HANDS,
        out_specs=[spec(pltpu.VMEM)] * 3,
        compiler_params=params(),
        cost_estimate=pl.CostEstimate(flops=0, bytes_accessed=3 * 10**6, transcendentals=0),
        name="pack_hands",
    )(*hands)


def part_kernel(begins, pack_in, *refs):
    hands, sem = refs[:HANDS], refs[HANDS]
    rows = hands[0].shape[0]
    copies = []
    for h, hand in enumerate(hands):
        base = pl.multiple_of((begins[h, 0] // 16) * 16, 16)
        copies.append(pltpu.make_async_copy(pack_in.at[pl.ds(base, rows)], hand, sem.at[h]))
    for copy in copies:
        copy.start()
    for copy in copies:
        copy.wait()


def part_call(begins, pack_in):
    rows, width = pack_in.shape
    return pl.pallas_call(
        part_kernel,
        out_shape=[jax.ShapeDtypeStruct((rows // HANDS, width), BF)] * HANDS,
        in_specs=[spec(pltpu.SMEM), spec(pl.ANY)],
        out_specs=[spec(pl.ANY)] * HANDS,
        scratch_shapes=[pltpu.SemaphoreType.DMA((HANDS,))],
        compiler_params=params(),
        cost_estimate=pl.CostEstimate(flops=0, bytes_accessed=3 * 10**6, transcendentals=0),
        name="part_pack",
    )(begins, pack_in)


def second_send_kernel(off, pos, extra, x_ref, second, meta, buf, ranks):
    step = pl.program_id(0)

    @pl.when(step == 0)
    def _():
        buf[...] = jnp.zeros_like(buf)
        ranks[...] = jnp.zeros_like(ranks)

    half = second.shape[0] - 16
    cap = 4 * half
    wide = BLK + 16
    blocks = x_ref.shape[0] // BLK
    line = iota((16, BLK), 0)
    for sub in range(blocks):
        b = step * blocks + sub
        place = pos[8 * sub : 8 * sub + 8, :]
        base = jnp.minimum((off[8 * b + 2, 0] // 16) * 16, half)
        hot = as_bf(iota((wide, BLK), 0) == place[2:3, :] - base)
        got = dot(hot, x_ref[sub * BLK : (sub + 1) * BLK, :])
        buf[pl.ds(pl.multiple_of(base, 16), wide), :] += got.astype(BF)
        rank = place[4:5, :]
        value = jnp.where(line == 0, rank >> 8, jnp.where(line == 1, rank & 255, 1))
        value = jnp.where(rank >= 0, value, 0).astype(F32).astype(BF)
        for kind in (0, 1):
            base = pl.multiple_of(jnp.minimum((off[8 * b + kind, 0] // 128) * 128, cap), 128)
            hot = as_bf(iota((BLK + 128, BLK), 0) == place[kind : kind + 1, :] - base)
            ranks[:, pl.ds(base, BLK + 128)] += dot_t(value, hot)[:8]

    @pl.when(step == pl.num_programs(0) - 1)
    def _():
        second[0:half, :] = buf[0:half, :]
        second[half:, :] = extra[...]
        seen = ranks[2:3, :cap] > 0.5
        rank = (ranks[0:1, :cap] * 256.0 + ranks[1:2, :cap]).astype(I32)
        goal = jnp.where(seen, rank, 1 << 20)
        line = cap // 8
        for k in range(8):
            meta[k : k + 1, :] = goal[:, k * line : (k + 1) * line]


def second_send_call(off, pos, first, vectors):
    rows, width = vectors.shape
    cap = rows // 2
    half = rows // 8
    return pl.pallas_call(
        second_send_kernel,
        grid=(rows // 1024,),
        out_shape=[
            jax.ShapeDtypeStruct((half + 16, width), BF),
            jax.ShapeDtypeStruct((8, cap // 8), I32),
        ],
        in_specs=[
            spec(pltpu.SMEM),
            pl.BlockSpec((8 * 1024 // BLK, BLK), lambda b: (b, 0)),
            pl.BlockSpec((16, width), lambda b: (half // 16, 0)),
            pl.BlockSpec((1024, width), lambda b: (b, 0)),
        ],
        out_specs=[
            pl.BlockSpec((half + 16, width), lambda b: (0, 0)),
            pl.BlockSpec((8, cap // 8), lambda b: (0, 0)),
        ],
        scratch_shapes=[pltpu.VMEM((half + BLK + 16, width), BF), pltpu.VMEM((8, cap + BLK + 128), F32)],
        compiler_params=params(),
        cost_estimate=pl.CostEstimate(flops=6 * 10**9, bytes_accessed=8 * 10**6, transcendentals=0),
        name="second_send",
    )(off, pos, first, vectors)


def own_kernel(pos, x_ref, held):
    same = iota((BLK, BLK), 0) == iota((BLK, BLK), 1)
    for sub in range(x_ref.shape[0] // BLK):
        lines = slice(sub * BLK, (sub + 1) * BLK)
        held[lines, :] = dot(as_bf(same & (pos[8 * sub + 3 : 8 * sub + 4, :] >= 0)), x_ref[lines, :]).astype(BF)


def own_call(pos, vectors):
    rows, width = vectors.shape
    return pl.pallas_call(
        own_kernel,
        grid=(rows // 1024,),
        out_shape=jax.ShapeDtypeStruct((rows + rows // 2 + rows // 4, width), BF),
        in_specs=[
            pl.BlockSpec((8 * 1024 // BLK, BLK), lambda b: (b, 0)),
            pl.BlockSpec((1024, width), lambda b: (b, 0)),
        ],
        out_specs=pl.BlockSpec((1024, width), lambda b: (b, 0)),
        compiler_params=params(),
        cost_estimate=pl.CostEstimate(flops=2 * 10**9, bytes_accessed=13 * 10**6, transcendentals=0),
        name="own_slots",
    )(pos, vectors)


def margins(score, shift, first, width):
    return (score[first + 1 : first + 2] - score[first : first + 1] - shift) / width


def put_lines(ref, start, values):
    for k in range(values.shape[1] // 128):
        ref[start + k : start + k + 1, :] = values[:, 128 * k : 128 * (k + 1)]


def centre_kernel(here, total, labels, x_ref, cents, centres, shifts, one, two):
    width = x_ref.shape[1]

    @pl.when(pl.program_id(0) == 0)
    def _():
        sums, counts = total[0:4, :], total[4:8, :]
        low = (sums[0:1] + sums[1:2]) / (counts[0:1] + counts[1:2])
        high = (sums[2:3] + sums[3:4]) / (counts[2:3] + counts[3:4])
        groups = sums / counts
        cents[0:1, :] = low
        cents[1:2, :] = high
        cents[2:6, :] = groups
        top = here[0] == 1
        left = jnp.where(top, groups[2:3], groups[0:1])
        right = jnp.where(top, groups[3:4], groups[1:2])
        centres[...] = jnp.concatenate([low, high, left, right, jnp.zeros((12, width), F32)], axis=0).astype(BF)
        for k, (a, b) in enumerate(((low, high), (left, right))):
            shift = 0.5 * (jnp.sum(b * b, axis=1, keepdims=True) - jnp.sum(a * a, axis=1, keepdims=True))
            shifts[k : k + 1, :] = jnp.broadcast_to(shift, (1, 128))

    score = dot_t(centres[...], x_ref[...])
    stay = labels[0:1, :] == here[0]
    keep = stay & (labels[1:2, :] == here[1])
    put_lines(one, 0, jnp.where(stay, margins(score, shifts[0:1, 0:1], 0, width), 0.0))
    put_lines(two, 0, jnp.where(keep, margins(score, shifts[1:2, 0:1], 2, width), 0.0))


def centre_call(here, total, labels, vectors):
    rows, width = vectors.shape
    cap = rows // 2
    return pl.pallas_call(
        centre_kernel,
        grid=(rows // 1024,),
        out_shape=[
            jax.ShapeDtypeStruct((6, width), F32),
            jax.ShapeDtypeStruct((16, width), BF),
            jax.ShapeDtypeStruct((8, 128), F32),
            jax.ShapeDtypeStruct(((rows + cap) // 128, 128), F32),
            jax.ShapeDtypeStruct(((rows + cap + cap // 2) // 128, 128), F32),
        ],
        in_specs=[
            spec(pltpu.SMEM),
            pl.BlockSpec((8, width), lambda b: (0, 0)),
            pl.BlockSpec((2, 1024), lambda b: (0, b)),
            pl.BlockSpec((1024, width), lambda b: (b, 0)),
        ],
        out_specs=[
            pl.BlockSpec((6, width), lambda b: (0, 0)),
            pl.BlockSpec((16, width), lambda b: (0, 0)),
            pl.BlockSpec((8, 128), lambda b: (0, 0)),
            pl.BlockSpec((8, 128), lambda b: (b, 0)),
            pl.BlockSpec((8, 128), lambda b: (b, 0)),
        ],
        compiler_params=params(),
        cost_estimate=pl.CostEstimate(flops=2 * 10**9, bytes_accessed=7 * 10**6, transcendentals=0),
        name="own_margins",
    )(here, total, labels, vectors)


def second_kernel(centres, shifts, second, relay, first, meta, leavers, held_in, two_in, held, two, again, alone, start, goals):
    del held_in, two_in
    half = second.shape[0] - 16
    slots = held.shape[0]
    cap = 2 * slots
    have = count_at(second[half:, :], 5)
    more = count_at(relay[half:, :], 4)
    both = count_at(first[half:, :], 4)
    lane = iota((1, half), 1)
    goal = jnp.where(lane < more, lane + have, -1)
    moved = dot(as_bf(iota((slots, half), 0) == goal), relay[0:half, :]).astype(BF)
    held[0:half, :] = moved[0:half] + second[0:half, :]
    held[half:, :] = moved[half:]
    score = dot_t(centres[...], held[...])
    width = held.shape[1]
    live = iota((1, slots), 1) < have + more
    put_lines(two, 0, jnp.where(live, margins(score, shifts[1:2, 0:1], 2, width), 0.0))

    score = dot_t(centres[...], first[0:half, :])
    value = jnp.where(lane < both, margins(score, shifts[0:1, 0:1], 0, width), 0.0)
    high = value.astype(BF).astype(F32)
    middle = (value - high).astype(BF).astype(F32)
    low = value - high - middle
    value = jnp.concatenate([high, middle, low, jnp.ones((1, half), F32), jnp.zeros((12, half), F32)], axis=0).astype(BF)
    place = jnp.concatenate([meta[k : k + 1, :] for k in range(8)], axis=1)
    goal = jnp.where(lane < both, place[:, :half], -1)
    for k in range(cap // BLK):
        hot = as_bf(iota((BLK, half), 0) + k * BLK == goal)
        got = dot_t(value, hot)
        put_lines(again, k * BLK // 128, got[0:1] + got[1:2] + got[2:3])
        free = (iota((1, BLK), 1) + k * BLK < leavers[0:1, 0:1]) & (got[3:4] < 0.5)
        put_lines(alone, k * BLK // 128, jnp.where(free, 1.0, 0.0))
    lane = iota((8, cap), 1)
    earlier = (lane < both) | (place < BLK * iota((8, cap), 0))
    begin = jnp.sum(jnp.where(earlier, 1.0, 0.0), axis=1, keepdims=True).astype(I32)
    begin = jnp.minimum((begin >> 7) << 7, cap - BLK - 128)
    start[...] = jnp.broadcast_to(begin, start.shape)
    goals[...] = jnp.broadcast_to(jnp.where(iota((1, cap), 1) < both, -1, place), goals.shape)


def second_call(centres, shifts, second, relay, first, meta, leavers, held, two):
    half, width = second.shape
    half -= 16
    cap = 4 * half
    slots = cap // 2
    return pl.pallas_call(
        second_kernel,
        grid=(1,),
        out_shape=[
            jax.ShapeDtypeStruct(held.shape, BF),
            jax.ShapeDtypeStruct(two.shape, F32),
            jax.ShapeDtypeStruct((cap // 128, 128), F32),
            jax.ShapeDtypeStruct((cap // 128, 128), F32),
            jax.ShapeDtypeStruct((8, 128), I32),
            jax.ShapeDtypeStruct((8, cap), I32),
        ],
        in_specs=[spec(pltpu.VMEM)] * 7 + [spec(pl.ANY)] * 2,
        out_specs=[
            pl.BlockSpec((slots, width), lambda b: (held.shape[0] // slots - 1, 0)),
            pl.BlockSpec((slots // 128, 128), lambda b: (held.shape[0] // slots - 1, 0)),
            pl.BlockSpec((cap // 128, 128), lambda b: (0, 0)),
            pl.BlockSpec((cap // 128, 128), lambda b: (0, 0)),
            pl.BlockSpec((8, 128), lambda b: (0, 0)),
            pl.BlockSpec((8, cap), lambda b: (0, 0)),
        ],
        input_output_aliases={7: 0, 8: 1},
        compiler_params=params(),
        cost_estimate=pl.CostEstimate(flops=3 * 10**9, bytes_accessed=6 * 10**6, transcendentals=0),
        name="second_slots",
    )(centres, shifts, second, relay, first, meta, leavers, held, two)


def column_kernel(own, a, b, c, out):
    sums, counts = unpack(own[...])
    for other in (a, b, c):
        s, n = unpack(other[...])
        sums, counts = sums + s, counts + n
    out[0:4, :] = sums
    width = out.shape[1]
    for g in range(4):
        out[4 + g : 5 + g, :] = jnp.broadcast_to(counts[:, 128 * g : 128 * g + 1], (1, width))


def column_call(*pieces):
    width = pieces[0].shape[1]
    return pl.pallas_call(
        column_kernel,
        grid=(1,),
        out_shape=jax.ShapeDtypeStruct((8, width), F32),
        in_specs=[pl.BlockSpec((16, width), functools.partial(lambda last, b: (last, 0), p.shape[0] // 16 - 1)) for p in pieces],
        out_specs=pl.BlockSpec((8, width), lambda b: (0, 0)),
        compiler_params=params(),
        name="column_sums",
    )(*pieces)


def first_kernel(start, centres, shifts, goals, again, alone, first, middle, *refs):
    hands, (held_in, one_in, two_in, held, one, two, x, out, sem, sent) = refs[:HANDS], refs[HANDS:]
    del one_in, two_in, held_in
    part, width = middle.shape
    turns = hands[0].shape[0] // 16
    loads = [
        pltpu.make_async_copy(first.at[pl.ds(0, part)], x.at[pl.ds(0, part)], sem.at[HANDS, 0]),
        pltpu.make_async_copy(middle, x.at[pl.ds(part, part)], sem.at[HANDS, 1]),
    ]
    for h, hand in enumerate(hands):
        for turn in range(turns):
            block = x.at[pl.ds(2 * part + 16 * (h + HANDS * turn), 16)]
            loads.append(pltpu.make_async_copy(hand.at[pl.ds(16 * turn, 16)], block, sem.at[h, turn]))
    for load in loads:
        load.start()
    for load in loads:
        load.wait()
    span = BLK + 128
    base = 8 * part
    slot = iota((BLK, span), 0)
    stores = []
    for k in range(4 * part // BLK):
        begin = pl.multiple_of(start[k, 0], 128)
        hot = as_bf(slot == goals[0:1, pl.ds(begin, span)] - k * BLK)
        rows = dot(hot, x[pl.ds(begin, span), :]).astype(BF)
        lines = pl.ds(k * BLK, BLK)
        out[lines, :] = rows
        stores.append(pltpu.make_async_copy(out.at[lines], held.at[pl.ds(base + k * BLK, BLK)], sent.at[k]))
        stores[-1].start()
        score = dot_t(centres[...], rows)
        m_one = margins(score, shifts[0:1, 0:1], 0, width)
        m_two = margins(score, shifts[1:2, 0:1], 2, width)
        for i in range(BLK // 128):
            line = slice(k * (BLK // 128) + i, k * (BLK // 128) + i + 1)
            lanes = slice(128 * i, 128 * (i + 1))
            one[line, :] = jnp.where(alone[line, :] > 0.5, m_one[:, lanes], again[line, :])
            two[line, :] = jnp.where(alone[line, :] > 0.5, m_two[:, lanes], 0.0)
    for store in stores:
        store.wait()


def first_call(start, centres, shifts, goals, again, alone, first, middle, hands, held, one, two):
    width = held.shape[1]
    cap = goals.shape[1]
    lines = cap // 128
    return pl.pallas_call(
        first_kernel,
        grid=(1,),
        out_shape=[
            jax.ShapeDtypeStruct(held.shape, BF),
            jax.ShapeDtypeStruct(one.shape, F32),
            jax.ShapeDtypeStruct(two.shape, F32),
        ],
        in_specs=[spec(pltpu.SMEM)] + [spec(pltpu.VMEM)] * 5 + [spec(pl.ANY)] * (HANDS + 5),
        out_specs=[
            spec(pl.ANY),
            pl.BlockSpec((lines, 128), lambda k: (2, 0)),
            pl.BlockSpec((lines, 128), lambda k: (2, 0)),
        ],
        scratch_shapes=[
            pltpu.VMEM((cap, width), BF),
            pltpu.VMEM((cap, width), BF),
            pltpu.SemaphoreType.DMA((HANDS + 1, cap // 32 // HANDS)),
            pltpu.SemaphoreType.DMA((cap // BLK,)),
        ],
        input_output_aliases={8 + HANDS: 0, 9 + HANDS: 1, 10 + HANDS: 2},
        compiler_params=params(),
        cost_estimate=pl.CostEstimate(flops=3 * 10**9, bytes_accessed=7 * 10**6, transcendentals=0),
        name="first_slots",
    )(start, centres, shifts, goals, again, alone, first, middle, *hands, held, one, two)


def local(vectors, child_labels):
    ways = lax.axis_size("cube")
    top = ways // 2
    nxt = ways // 4
    me = lax.axis_index("cube")
    here = jnp.stack([(me // top) & 1, (me // nxt) & 1]).astype(I32)
    after = lax.optimization_barrier
    pos, off, every, leavers = plan_call(here, child_labels)
    counts = [leavers] + [swap(leavers, bits) for bits in (nxt, top, top | nxt)]
    first, middle, rest = sort_call(here, child_labels, pos, off, every, vectors)
    first_in = swap(first, top)
    own, *hands = deal_call(rest, *counts)
    hands = [own] + [swap(hand, h + 1) for h, hand in enumerate(hands)]
    after_deal, _ = after((pos, own))
    second, meta = second_send_call(off, after_deal, first, vectors)
    second_in = swap(second, nxt)
    after_send, _ = after((after_deal, meta))
    held = own_call(after_send, vectors)
    limit = rest.shape[0]
    step = limit // 16
    packed, longest, begins = pack_call(step, hands)
    bit = HANDS
    while bit < nxt:
        longest = jnp.maximum(longest, swap(longest, bit))
        bit *= 2

    def cross(size):
        def branch(rows, first_in, meta):
            got = jnp.pad(swap(rows[:size], top), ((0, limit - size), (0, 0))) if size else jnp.zeros_like(rows)
            return got, swap(first_in, nxt), swap(meta, top)

        return branch

    sizes = range(0, limit + 1, step)
    packed, held, first_in = after((packed, held, first_in))
    packed_in, relay, meta_in = lax.switch(longest[0, 0], [cross(size) for size in sizes], packed, first_in, meta)
    middle, packed_in = after((middle, packed_in))
    middle_in = swap(middle, top)
    own, *hands = part_call(begins, packed_in)
    hands = [own] + [swap(hand, h + 1) for h, hand in enumerate(hands)]
    second_in, *hands[4:] = after((second_in, *hands[4:]))
    total = column_call(first, second_in, first_in, relay)
    bit = 1
    while bit < nxt:
        total = total + swap(total, bit)
        bit *= 2
    cents, centres, shifts, one, two = centre_call(here, total, child_labels, vectors)
    held, two, again, alone, start, goals = second_call(
        centres, shifts, second_in, relay, first_in, meta_in, counts[2], held, two
    )
    held, one, two = first_call(
        start, centres, shifts, goals, again, alone, first_in, middle_in, hands, held, one, two
    )
    return held, one.reshape(-1), two.reshape(-1), cents


def solution(mesh):
    return jax.shard_map(
        local,
        mesh=mesh,
        in_specs=(P("cube", None), P(None, "cube")),
        out_specs=(P("cube", None), P("cube"), P("cube"), P()),
        check_vma=False,
    )
```

```python
import functools
import jax
import jax.numpy as jnp
from jax import lax
from jax.experimental import pallas as pl
from jax.experimental.pallas import tpu as pltpu
from jax.sharding import PartitionSpec as P

BF = jnp.bfloat16
F32 = jnp.float32
I32 = jnp.int32
BLK = 256
HANDS = 8
WIDE = BLK // 2 + 16
VMEM_BYTES = 48 * 1024 * 1024


def swap(x, bits):
    return lax.ppermute(x, "cube", [(i, i ^ bits) for i in range(lax.axis_size("cube"))])


def dot(a, b):
    return lax.dot_general(a, b, (((1,), (0,)), ((), ())), preferred_element_type=F32)


def dot_t(a, b):
    return lax.dot_general(a, b, (((1,), (1,)), ((), ())), preferred_element_type=F32)


def iota(shape, dim):
    return lax.broadcasted_iota(I32, shape, dim)


def as_bf(mask):
    return jnp.where(mask, jnp.float32(1), jnp.float32(0)).astype(BF)


def pack(sums, counts, width):
    high = sums.astype(BF).astype(F32)
    middle = (sums - high).astype(BF).astype(F32)
    low = sums - high - middle
    spare = width - 128 * len(counts)
    counts = jnp.concatenate(counts + ([jnp.zeros((1, spare), I32)] if spare else []), axis=1)
    upper, lower = (counts >> 8).astype(F32), (counts & 255).astype(F32)
    return jnp.concatenate([high, middle, low, upper, lower, jnp.zeros((2, width), F32)], axis=0).astype(BF)


def unpack(extra):
    extra = extra.astype(F32)
    sums = extra[0:4] + extra[4:8] + extra[8:12]
    return sums, extra[12:13] * 256.0 + extra[13:14]


def count_at(extra, k):
    extra = extra[12:14, 128 * k : 128 * k + 1].astype(F32)
    return (extra[0:1] * 256.0 + extra[1:2]).astype(I32)


def spec(memory):
    return pl.BlockSpec(memory_space=memory)


def params():
    return pltpu.CompilerParams(vmem_limit_bytes=VMEM_BYTES)


def plan_kernel(here, labels, pos, off_ref, every, leavers):
    rows = labels.shape[1]
    blocks = rows // BLK
    leave = labels[0:1, :] != here[0]
    miss = labels[1:2, :] != here[1]
    code = jnp.where(leave, jnp.where(miss, 0, 1), jnp.where(miss, 2, 3))
    code = jnp.concatenate(
        [jnp.broadcast_to(code[:, b * BLK : (b + 1) * BLK], (8, BLK)) for b in range(blocks)], axis=0
    )
    tall = 8 * blocks
    kind = iota((tall, BLK), 0) & 7
    mask = (code == kind) | ((kind == 4) & (code <= 1))
    maskb = as_bf(mask)
    upper = as_bf(iota((BLK, BLK), 0) <= iota((BLK, BLK), 1))
    before = dot(maskb, upper)
    total = dot(maskb, jnp.ones((BLK, BLK), BF)).astype(BF)
    r, c = iota((tall, tall), 0), iota((tall, tall), 1)
    same = ((r ^ c) & 7) == 0
    earlier = as_bf((same & (c < r)) | (((r & 7) == 1) & ((c & 7) == 0)))
    off = dot(earlier, total)
    pos[...] = jnp.where(mask, (before + off).astype(I32) - 1, -1)
    off_ref[...] = (off + jnp.where(iota((tall, BLK), 1) < 64, 0.0, total.astype(F32)))[:, :128].astype(I32)
    r8, c8 = iota((8, tall), 0), iota((8, tall), 1)
    count = dot(as_bf(r8 == (c8 & 7)), total)[:, :128].astype(I32)
    every[...] = count
    leavers[...] = jnp.broadcast_to(count[4:5], leavers.shape)


def plan_call(here, labels):
    rows = labels.shape[1]
    tall = 8 * rows // BLK
    return pl.pallas_call(
        plan_kernel,
        out_shape=[
            jax.ShapeDtypeStruct((tall, BLK), I32),
            jax.ShapeDtypeStruct((tall, 128), I32),
            jax.ShapeDtypeStruct((8, 128), I32),
            jax.ShapeDtypeStruct((8, 128), I32),
        ],
        in_specs=[spec(pltpu.SMEM), spec(pltpu.VMEM)],
        out_specs=[spec(pltpu.VMEM)] * 4,
        compiler_params=params(),
        cost_estimate=pl.CostEstimate(flops=10**8, bytes_accessed=10**5, transcendentals=0),
        name="plan_places",
    )(here, labels)


def sort_kernel(here, labels, pos_ref, off_ref, every, x_hbm, first, middle, rest, x, buf, tail, sums, sem_in, sem_out):
    rows = labels.shape[1]
    blocks = rows // BLK
    cap = rows // 2
    step = rows // 4
    loads = [
        pltpu.make_async_copy(x_hbm.at[pl.ds(k * step, step)], x.at[pl.ds(k * step, step)], sem_in.at[k])
        for k in range(4)
    ]
    for load in loads:
        load.start()
    buf[...] = jnp.zeros_like(buf)
    group = 2 * labels[0:1, :] + labels[1:2, :]
    slot = iota((WIDE, BLK), 0)
    more_slot = iota((BLK + 16 - WIDE, BLK), 0) + WIDE
    sums[...] = jnp.zeros_like(sums)
    for b in range(blocks):
        if b % (step // BLK) == 0:
            loads[b // (step // BLK)].wait()
        vectors = x.at[pl.ds(b * BLK, BLK)]
        hot = [as_bf((iota((16, BLK), 0) & 3) == group[:, b * BLK : (b + 1) * BLK])]
        bases = []
        ends = []
        places = []
        for kind in (0, 1):
            line = slice(8 * b + kind, 8 * b + kind + 1)
            base = pl.multiple_of(jnp.minimum((off_ref[line, 0:1][0, 0] // 16) * 16, cap), 16)
            bases.append(base)
            ends.append(off_ref[line, 64:65][0, 0])
            places.append(pos_ref[line, :] - base)
            hot.append(as_bf(slot == places[kind]))
        got = dot(jnp.concatenate(hot, axis=0), vectors[...])
        sums[...] += got[0:8]
        got = got[16:].astype(BF)
        buf[pl.ds(bases[0], WIDE), :] += got[:WIDE]
        buf[pl.ds(bases[1], 16), :] += got[WIDE : WIDE + 16]
        buf[pl.ds(bases[1] + 16, WIDE - 16), :] = got[WIDE + 16 :]
        for kind in (0, 1):

            @pl.when(ends[kind] - bases[kind] > WIDE)
            def _():
                more = dot(as_bf(more_slot == places[kind]), vectors[...]).astype(BF)
                buf[pl.ds(bases[kind] + WIDE, BLK + 16 - WIDE), :] += more

    one, two = here[0], here[1]
    kinds = [every[k : k + 1] for k in range(4)]
    counts = []
    for g in range(4):
        away, miss = jnp.int32(g >> 1) != one, jnp.int32(g & 1) != two
        counts.append(jnp.where(away, jnp.where(miss, kinds[0], kinds[1]), jnp.where(miss, kinds[2], kinds[3])))
    tail[...] = pack(sums[0:4, :], counts + [kinds[0], kinds[2]], x.shape[1])
    part = cap // 4
    stores = [
        pltpu.make_async_copy(buf.at[pl.ds(0, part)], first.at[pl.ds(0, part)], sem_out.at[0]),
        pltpu.make_async_copy(buf.at[pl.ds(part, part)], middle, sem_out.at[1]),
        pltpu.make_async_copy(buf.at[pl.ds(2 * part, 2 * part)], rest, sem_out.at[2]),
        pltpu.make_async_copy(tail, first.at[pl.ds(part, 16)], sem_out.at[3]),
    ]
    for store in stores:
        store.start()
    for store in stores:
        store.wait()


def sort_call(here, labels, pos, off, every, vectors):
    rows, width = vectors.shape
    part = rows // 8
    return pl.pallas_call(
        sort_kernel,
        out_shape=[
            jax.ShapeDtypeStruct((part + 16, width), BF),
            jax.ShapeDtypeStruct((part, width), BF),
            jax.ShapeDtypeStruct((2 * part, width), BF),
        ],
        in_specs=[spec(pltpu.SMEM)] + [spec(pltpu.VMEM)] * 4 + [spec(pl.ANY)],
        out_specs=[spec(pl.ANY), spec(pltpu.HBM), spec(pl.ANY)],
        scratch_shapes=[
            pltpu.VMEM((rows, width), BF),
            pltpu.VMEM((rows // 2 + BLK + 16, width), BF),
            pltpu.VMEM((16, width), BF),
            pltpu.VMEM((8, width), F32),
            pltpu.SemaphoreType.DMA((4,)),
            pltpu.SemaphoreType.DMA((4,)),
        ],
        compiler_params=params(),
        cost_estimate=pl.CostEstimate(flops=8 * 10**9, bytes_accessed=10 * 10**6, transcendentals=0),
        name="sort_leavers",
    )(here, labels, pos, off, every, vectors)


def deal_kernel(rest, own, near, top, far, *refs):
    hands, (tail, sem) = refs[:HANDS], refs[HANDS:]
    rows, width = rest.shape
    turns = rows // 16 // HANDS
    counts = jnp.concatenate([ref[0:1, :] for ref in (own, near, top, far)], axis=1)
    counts = jnp.concatenate([counts, jnp.zeros((1, width - 512), I32)], axis=1)
    upper, lower = (counts >> 8).astype(F32), (counts & 255).astype(F32)
    tail[...] = jnp.concatenate([upper, lower, jnp.zeros((14, width), F32)], axis=0).astype(BF)
    copies = []
    for h, hand in enumerate(hands):
        for turn in range(turns):
            block = rest.at[pl.ds(16 * (h + HANDS * turn), 16)]
            copies.append(pltpu.make_async_copy(block, hand.at[pl.ds(16 * turn, 16)], sem.at[h, turn]))
        copies.append(pltpu.make_async_copy(tail, hand.at[pl.ds(16 * turns, 16)], sem.at[h, turns]))
    for copy in copies:
        copy.start()
    for copy in copies:
        copy.wait()


def deal_call(rest, *counts):
    rows, width = rest.shape
    turns = rows // 16 // HANDS
    return pl.pallas_call(
        deal_kernel,
        out_shape=[jax.ShapeDtypeStruct((16 * turns + 16, width), BF)] * HANDS,
        in_specs=[spec(pl.ANY)] + [spec(pltpu.VMEM)] * 4,
        out_specs=[spec(pl.ANY)] * HANDS,
        scratch_shapes=[pltpu.VMEM((16, width), BF), pltpu.SemaphoreType.DMA((HANDS, turns + 1))],
        compiler_params=params(),
        cost_estimate=pl.CostEstimate(flops=0, bytes_accessed=3 * 10**6, transcendentals=0),
        name="deal_rest",
    )(rest, *counts)


def pack_kernel(step, *refs):
    hands, (out, longest, begins) = refs[:HANDS], refs[HANDS:]
    rows = hands[0].shape[0] - 16
    out[...] = jnp.zeros_like(out)
    full = []
    for hand in hands:
        count = hand[rows : rows + 2, 0:512].astype(F32)
        count = (count[0:1] * 256.0 + count[1:2]).astype(I32)
        full.append((jnp.maximum(count - rows * HANDS, 0) + 15) >> 4)
    place = jnp.zeros((1, 512), I32)
    for h, hand in enumerate(hands):
        base = pl.multiple_of(place[0, 0] * 16, 16)
        out[pl.ds(base, rows), :] = hand[0:rows, :]
        begins[h : h + 1, :] = place[:, 256:384] * 16
        place = jnp.minimum(place + ((full[h] + (HANDS - 1 - h)) >> 3), (h + 1) * (rows // 16))
    most = jnp.zeros((1, 512), I32)
    for other in range(HANDS):
        size = jnp.zeros((1, 512), I32)
        for h in range(HANDS):
            size = size + ((full[other ^ h] + (HANDS - 1 - h)) >> 3)
        most = jnp.maximum(most, size)
    most = jnp.max(most.astype(F32), axis=1, keepdims=True).astype(I32)
    per = step // 16
    longest[...] = jnp.broadcast_to(jnp.minimum(most + per - 1, out.shape[0] // 16) // per, longest.shape)


def pack_call(step, hands):
    rows, width = hands[0].shape
    rows -= 16
    return pl.pallas_call(
        functools.partial(pack_kernel, step),
        out_shape=[
            jax.ShapeDtypeStruct((rows * HANDS, width), BF),
            jax.ShapeDtypeStruct((8, 128), I32),
            jax.ShapeDtypeStruct((8, 128), I32),
        ],
        in_specs=[spec(pltpu.VMEM)] * HANDS,
        out_specs=[spec(pltpu.VMEM)] * 3,
        compiler_params=params(),
        cost_estimate=pl.CostEstimate(flops=0, bytes_accessed=3 * 10**6, transcendentals=0),
        name="pack_hands",
    )(*hands)


def part_kernel(begins, pack_in, *refs):
    hands, sem = refs[:HANDS], refs[HANDS]
    rows = hands[0].shape[0]
    copies = []
    for h, hand in enumerate(hands):
        base = pl.multiple_of((begins[h, 0] // 16) * 16, 16)
        copies.append(pltpu.make_async_copy(pack_in.at[pl.ds(base, rows)], hand, sem.at[h]))
    for copy in copies:
        copy.start()
    for copy in copies:
        copy.wait()


def part_call(begins, pack_in):
    rows, width = pack_in.shape
    return pl.pallas_call(
        part_kernel,
        out_shape=[jax.ShapeDtypeStruct((rows // HANDS, width), BF)] * HANDS,
        in_specs=[spec(pltpu.SMEM), spec(pl.ANY)],
        out_specs=[spec(pl.ANY)] * HANDS,
        scratch_shapes=[pltpu.SemaphoreType.DMA((HANDS,))],
        compiler_params=params(),
        cost_estimate=pl.CostEstimate(flops=0, bytes_accessed=3 * 10**6, transcendentals=0),
        name="part_pack",
    )(begins, pack_in)


def second_send_kernel(off, pos, extra, x_ref, second, meta, buf, ranks):
    step = pl.program_id(0)

    @pl.when(step == 0)
    def _():
        buf[...] = jnp.zeros_like(buf)
        ranks[...] = jnp.zeros_like(ranks)

    half = second.shape[0] - 16
    cap = 4 * half
    wide = BLK + 16
    blocks = x_ref.shape[0] // BLK
    line = iota((16, BLK), 0)
    for sub in range(blocks):
        b = step * blocks + sub
        place = pos[8 * sub : 8 * sub + 8, :]
        base = jnp.minimum((off[8 * b + 2, 0] // 16) * 16, half)
        hot = as_bf(iota((wide, BLK), 0) == place[2:3, :] - base)
        got = dot(hot, x_ref[sub * BLK : (sub + 1) * BLK, :])
        buf[pl.ds(pl.multiple_of(base, 16), wide), :] += got.astype(BF)
        rank = place[4:5, :]
        value = jnp.where(line == 0, rank >> 8, jnp.where(line == 1, rank & 255, 1))
        value = jnp.where(rank >= 0, value, 0).astype(F32).astype(BF)
        for kind in (0, 1):
            base = pl.multiple_of(jnp.minimum((off[8 * b + kind, 0] // 128) * 128, cap), 128)
            hot = as_bf(iota((BLK + 128, BLK), 0) == place[kind : kind + 1, :] - base)
            ranks[:, pl.ds(base, BLK + 128)] += dot_t(value, hot)[:8]

    @pl.when(step == pl.num_programs(0) - 1)
    def _():
        second[0:half, :] = buf[0:half, :]
        second[half:, :] = extra[...]
        seen = ranks[2:3, :cap] > 0.5
        rank = (ranks[0:1, :cap] * 256.0 + ranks[1:2, :cap]).astype(I32)
        goal = jnp.where(seen, rank, 1 << 20)
        line = cap // 8
        for k in range(8):
            meta[k : k + 1, :] = goal[:, k * line : (k + 1) * line]


def second_send_call(off, pos, first, vectors):
    rows, width = vectors.shape
    cap = rows // 2
    half = rows // 8
    return pl.pallas_call(
        second_send_kernel,
        grid=(rows // 1024,),
        out_shape=[
            jax.ShapeDtypeStruct((half + 16, width), BF),
            jax.ShapeDtypeStruct((8, cap // 8), I32),
        ],
        in_specs=[
            spec(pltpu.SMEM),
            pl.BlockSpec((8 * 1024 // BLK, BLK), lambda b: (b, 0)),
            pl.BlockSpec((16, width), lambda b: (half // 16, 0)),
            pl.BlockSpec((1024, width), lambda b: (b, 0)),
        ],
        out_specs=[
            pl.BlockSpec((half + 16, width), lambda b: (0, 0)),
            pl.BlockSpec((8, cap // 8), lambda b: (0, 0)),
        ],
        scratch_shapes=[pltpu.VMEM((half + BLK + 16, width), BF), pltpu.VMEM((8, cap + BLK + 128), F32)],
        compiler_params=params(),
        cost_estimate=pl.CostEstimate(flops=6 * 10**9, bytes_accessed=8 * 10**6, transcendentals=0),
        name="second_send",
    )(off, pos, first, vectors)


def own_kernel(pos, x_ref, held):
    same = iota((BLK, BLK), 0) == iota((BLK, BLK), 1)
    for sub in range(x_ref.shape[0] // BLK):
        lines = slice(sub * BLK, (sub + 1) * BLK)
        held[lines, :] = dot(as_bf(same & (pos[8 * sub + 3 : 8 * sub + 4, :] >= 0)), x_ref[lines, :]).astype(BF)


def own_call(pos, vectors):
    rows, width = vectors.shape
    return pl.pallas_call(
        own_kernel,
        grid=(rows // 1024,),
        out_shape=jax.ShapeDtypeStruct((rows + rows // 2 + rows // 4, width), BF),
        in_specs=[
            pl.BlockSpec((8 * 1024 // BLK, BLK), lambda b: (b, 0)),
            pl.BlockSpec((1024, width), lambda b: (b, 0)),
        ],
        out_specs=pl.BlockSpec((1024, width), lambda b: (b, 0)),
        compiler_params=params(),
        cost_estimate=pl.CostEstimate(flops=2 * 10**9, bytes_accessed=13 * 10**6, transcendentals=0),
        name="own_slots",
    )(pos, vectors)


def margins(score, shift, first, width):
    return (score[first + 1 : first + 2] - score[first : first + 1] - shift) / width


def put_lines(ref, start, values):
    for k in range(values.shape[1] // 128):
        ref[start + k : start + k + 1, :] = values[:, 128 * k : 128 * (k + 1)]


def centre_kernel(here, total, labels, x_ref, cents, centres, turned, shifts, one, two):
    width = x_ref.shape[1]

    @pl.when(pl.program_id(0) == 0)
    def _():
        sums, counts = total[0:4, :], total[4:8, :]
        low = (sums[0:1] + sums[1:2]) / (counts[0:1] + counts[1:2])
        high = (sums[2:3] + sums[3:4]) / (counts[2:3] + counts[3:4])
        groups = sums / counts
        cents[0:1, :] = low
        cents[1:2, :] = high
        cents[2:6, :] = groups
        top = here[0] == 1
        left = jnp.where(top, groups[2:3], groups[0:1])
        right = jnp.where(top, groups[3:4], groups[1:2])
        rows = jnp.concatenate([low, high, left, right, jnp.zeros((124, width), F32)], axis=0)
        centres[...] = rows[0:16].astype(BF)
        turned[...] = rows.T.astype(BF)
        for k, (a, b) in enumerate(((low, high), (left, right))):
            shift = 0.5 * (jnp.sum(b * b, axis=1, keepdims=True) - jnp.sum(a * a, axis=1, keepdims=True))
            shifts[k : k + 1, :] = jnp.broadcast_to(shift, (1, 128))

    score = dot(x_ref[...], turned[...]).T
    stay = labels[0:1, :] == here[0]
    keep = stay & (labels[1:2, :] == here[1])
    put_lines(one, 0, jnp.where(stay, margins(score, shifts[0:1, 0:1], 0, width), 0.0))
    put_lines(two, 0, jnp.where(keep, margins(score, shifts[1:2, 0:1], 2, width), 0.0))


def centre_call(here, total, labels, vectors):
    rows, width = vectors.shape
    cap = rows // 2
    return pl.pallas_call(
        centre_kernel,
        grid=(rows // 1024,),
        out_shape=[
            jax.ShapeDtypeStruct((6, width), F32),
            jax.ShapeDtypeStruct((16, width), BF),
            jax.ShapeDtypeStruct((width, 128), BF),
            jax.ShapeDtypeStruct((8, 128), F32),
            jax.ShapeDtypeStruct(((rows + cap) // 128, 128), F32),
            jax.ShapeDtypeStruct(((rows + cap + cap // 2) // 128, 128), F32),
        ],
        in_specs=[
            spec(pltpu.SMEM),
            pl.BlockSpec((8, width), lambda b: (0, 0)),
            pl.BlockSpec((2, 1024), lambda b: (0, b)),
            pl.BlockSpec((1024, width), lambda b: (b, 0)),
        ],
        out_specs=[
            pl.BlockSpec((6, width), lambda b: (0, 0)),
            pl.BlockSpec((16, width), lambda b: (0, 0)),
            pl.BlockSpec((width, 128), lambda b: (0, 0)),
            pl.BlockSpec((8, 128), lambda b: (0, 0)),
            pl.BlockSpec((8, 128), lambda b: (b, 0)),
            pl.BlockSpec((8, 128), lambda b: (b, 0)),
        ],
        compiler_params=params(),
        cost_estimate=pl.CostEstimate(flops=2 * 10**9, bytes_accessed=7 * 10**6, transcendentals=0),
        name="own_margins",
    )(here, total, labels, vectors)


def second_kernel(centres, shifts, second, relay, first, meta, leavers, held_in, two_in, held, two, again, alone, start, goals):
    del held_in, two_in
    half = second.shape[0] - 16
    slots = held.shape[0]
    cap = 2 * slots
    have = count_at(second[half:, :], 5)
    more = count_at(relay[half:, :], 4)
    both = count_at(first[half:, :], 4)
    lane = iota((1, half), 1)
    goal = jnp.where(lane < more, lane + have, -1)
    moved = dot(as_bf(iota((slots, half), 0) == goal), relay[0:half, :]).astype(BF)
    held[0:half, :] = moved[0:half] + second[0:half, :]
    held[half:, :] = moved[half:]
    score = dot_t(centres[...], held[...])
    width = held.shape[1]
    live = iota((1, slots), 1) < have + more
    put_lines(two, 0, jnp.where(live, margins(score, shifts[1:2, 0:1], 2, width), 0.0))

    score = dot_t(centres[...], first[0:half, :])
    value = jnp.where(lane < both, margins(score, shifts[0:1, 0:1], 0, width), 0.0)
    high = value.astype(BF).astype(F32)
    middle = (value - high).astype(BF).astype(F32)
    low = value - high - middle
    value = jnp.concatenate([high, middle, low, jnp.ones((1, half), F32), jnp.zeros((12, half), F32)], axis=0).astype(BF)
    place = jnp.concatenate([meta[k : k + 1, :] for k in range(8)], axis=1)
    goal = jnp.where(lane < both, place[:, :half], -1)
    for k in range(cap // BLK):
        hot = as_bf(iota((BLK, half), 0) + k * BLK == goal)
        got = dot_t(value, hot)
        put_lines(again, k * BLK // 128, got[0:1] + got[1:2] + got[2:3])
        free = (iota((1, BLK), 1) + k * BLK < leavers[0:1, 0:1]) & (got[3:4] < 0.5)
        put_lines(alone, k * BLK // 128, jnp.where(free, 1.0, 0.0))
    lane = iota((8, cap), 1)
    earlier = (lane < both) | (place < BLK * iota((8, cap), 0))
    begin = jnp.sum(jnp.where(earlier, 1.0, 0.0), axis=1, keepdims=True).astype(I32)
    begin = jnp.minimum((begin >> 7) << 7, cap - BLK - 128)
    start[...] = jnp.broadcast_to(begin, start.shape)
    goals[...] = jnp.broadcast_to(jnp.where(iota((1, cap), 1) < both, -1, place), goals.shape)


def second_call(centres, shifts, second, relay, first, meta, leavers, held, two):
    half, width = second.shape
    half -= 16
    cap = 4 * half
    slots = cap // 2
    return pl.pallas_call(
        second_kernel,
        grid=(1,),
        out_shape=[
            jax.ShapeDtypeStruct(held.shape, BF),
            jax.ShapeDtypeStruct(two.shape, F32),
            jax.ShapeDtypeStruct((cap // 128, 128), F32),
            jax.ShapeDtypeStruct((cap // 128, 128), F32),
            jax.ShapeDtypeStruct((8, 128), I32),
            jax.ShapeDtypeStruct((8, cap), I32),
        ],
        in_specs=[spec(pltpu.VMEM)] * 7 + [spec(pl.ANY)] * 2,
        out_specs=[
            pl.BlockSpec((slots, width), lambda b: (held.shape[0] // slots - 1, 0)),
            pl.BlockSpec((slots // 128, 128), lambda b: (held.shape[0] // slots - 1, 0)),
            pl.BlockSpec((cap // 128, 128), lambda b: (0, 0)),
            pl.BlockSpec((cap // 128, 128), lambda b: (0, 0)),
            pl.BlockSpec((8, 128), lambda b: (0, 0)),
            pl.BlockSpec((8, cap), lambda b: (0, 0)),
        ],
        input_output_aliases={7: 0, 8: 1},
        compiler_params=params(),
        cost_estimate=pl.CostEstimate(flops=3 * 10**9, bytes_accessed=6 * 10**6, transcendentals=0),
        name="second_slots",
    )(centres, shifts, second, relay, first, meta, leavers, held, two)


def column_kernel(own, a, b, c, out):
    sums, counts = unpack(own[...])
    for other in (a, b, c):
        s, n = unpack(other[...])
        sums, counts = sums + s, counts + n
    out[0:4, :] = sums
    width = out.shape[1]
    for g in range(4):
        out[4 + g : 5 + g, :] = jnp.broadcast_to(counts[:, 128 * g : 128 * g + 1], (1, width))


def column_call(*pieces):
    width = pieces[0].shape[1]
    return pl.pallas_call(
        column_kernel,
        grid=(1,),
        out_shape=jax.ShapeDtypeStruct((8, width), F32),
        in_specs=[pl.BlockSpec((16, width), functools.partial(lambda last, b: (last, 0), p.shape[0] // 16 - 1)) for p in pieces],
        out_specs=pl.BlockSpec((8, width), lambda b: (0, 0)),
        compiler_params=params(),
        name="column_sums",
    )(*pieces)


def first_kernel(start, turned, shifts, goals, again, alone, first, middle, *refs):
    hands, (held_in, one_in, two_in, held, one, two, x, out, sem, sent) = refs[:HANDS], refs[HANDS:]
    del one_in, two_in, held_in
    part, width = middle.shape
    turns = hands[0].shape[0] // 16
    loads = [
        pltpu.make_async_copy(first.at[pl.ds(0, part)], x.at[pl.ds(0, part)], sem.at[HANDS, 0]),
        pltpu.make_async_copy(middle, x.at[pl.ds(part, part)], sem.at[HANDS, 1]),
    ]
    for h, hand in enumerate(hands):
        for turn in range(turns):
            block = x.at[pl.ds(2 * part + 16 * (h + HANDS * turn), 16)]
            loads.append(pltpu.make_async_copy(hand.at[pl.ds(16 * turn, 16)], block, sem.at[h, turn]))
    for load in loads:
        load.start()
    for load in loads:
        load.wait()
    span = BLK + 128
    base = 8 * part
    slot = iota((BLK, span), 0)
    stores = []
    for k in range(4 * part // BLK):
        begin = pl.multiple_of(start[k, 0], 128)
        hot = as_bf(slot == goals[0:1, pl.ds(begin, span)] - k * BLK)
        rows = dot(hot, x[pl.ds(begin, span), :]).astype(BF)
        lines = pl.ds(k * BLK, BLK)
        out[lines, :] = rows
        stores.append(pltpu.make_async_copy(out.at[lines], held.at[pl.ds(base + k * BLK, BLK)], sent.at[k]))
        stores[-1].start()
        score = dot(rows, turned[...]).T
        m_one = margins(score, shifts[0:1, 0:1], 0, width)
        m_two = margins(score, shifts[1:2, 0:1], 2, width)
        for i in range(BLK // 128):
            line = slice(k * (BLK // 128) + i, k * (BLK // 128) + i + 1)
            lanes = slice(128 * i, 128 * (i + 1))
            one[line, :] = jnp.where(alone[line, :] > 0.5, m_one[:, lanes], again[line, :])
            two[line, :] = jnp.where(alone[line, :] > 0.5, m_two[:, lanes], 0.0)
    for store in stores:
        store.wait()


def first_call(start, turned, shifts, goals, again, alone, first, middle, hands, held, one, two):
    width = held.shape[1]
    cap = goals.shape[1]
    lines = cap // 128
    return pl.pallas_call(
        first_kernel,
        grid=(1,),
        out_shape=[
            jax.ShapeDtypeStruct(held.shape, BF),
            jax.ShapeDtypeStruct(one.shape, F32),
            jax.ShapeDtypeStruct(two.shape, F32),
        ],
        in_specs=[spec(pltpu.SMEM)] + [spec(pltpu.VMEM)] * 5 + [spec(pl.ANY)] * (HANDS + 5),
        out_specs=[
            spec(pl.ANY),
            pl.BlockSpec((lines, 128), lambda k: (2, 0)),
            pl.BlockSpec((lines, 128), lambda k: (2, 0)),
        ],
        scratch_shapes=[
            pltpu.VMEM((cap, width), BF),
            pltpu.VMEM((cap, width), BF),
            pltpu.SemaphoreType.DMA((HANDS + 1, cap // 32 // HANDS)),
            pltpu.SemaphoreType.DMA((cap // BLK,)),
        ],
        input_output_aliases={8 + HANDS: 0, 9 + HANDS: 1, 10 + HANDS: 2},
        compiler_params=params(),
        cost_estimate=pl.CostEstimate(flops=3 * 10**9, bytes_accessed=7 * 10**6, transcendentals=0),
        name="first_slots",
    )(start, turned, shifts, goals, again, alone, first, middle, *hands, held, one, two)


def local(vectors, child_labels):
    ways = lax.axis_size("cube")
    top = ways // 2
    nxt = ways // 4
    me = lax.axis_index("cube")
    here = jnp.stack([(me // top) & 1, (me // nxt) & 1]).astype(I32)
    after = lax.optimization_barrier
    pos, off, every, leavers = plan_call(here, child_labels)
    counts = [leavers] + [swap(leavers, bits) for bits in (nxt, top, top | nxt)]
    first, middle, rest = sort_call(here, child_labels, pos, off, every, vectors)
    first_in = swap(first, top)
    own, *hands = deal_call(rest, *counts)
    hands = [own] + [swap(hand, h + 1) for h, hand in enumerate(hands)]
    after_deal, _ = after((pos, own))
    second, meta = second_send_call(off, after_deal, first, vectors)
    second_in = swap(second, nxt)
    after_send, _ = after((after_deal, meta))
    held = own_call(after_send, vectors)
    limit = rest.shape[0]
    step = limit // 16
    packed, longest, begins = pack_call(step, hands)
    bit = HANDS
    while bit < nxt:
        longest = jnp.maximum(longest, swap(longest, bit))
        bit *= 2

    def cross(size):
        def branch(rows, first_in, meta):
            got = jnp.pad(swap(rows[:size], top), ((0, limit - size), (0, 0))) if size else jnp.zeros_like(rows)
            return got, swap(first_in, nxt), swap(meta, top)

        return branch

    sizes = range(0, limit + 1, step)
    packed, held, first_in = after((packed, held, first_in))
    packed_in, relay, meta_in = lax.switch(longest[0, 0], [cross(size) for size in sizes], packed, first_in, meta)
    middle, packed_in = after((middle, packed_in))
    middle_in = swap(middle, top)
    own, *hands = part_call(begins, packed_in)
    hands = [own] + [swap(hand, h + 1) for h, hand in enumerate(hands)]
    second_in, hands[1] = after((second_in, hands[1]))
    total = column_call(first, second_in, first_in, relay)
    bit = 1
    while bit < nxt:
        total = total + swap(total, bit)
        bit *= 2
    cents, centres, turned, shifts, one, two = centre_call(here, total, child_labels, vectors)
    held, two, again, alone, start, goals = second_call(
        centres, shifts, second_in, relay, first_in, meta_in, counts[2], held, two
    )
    held, one, two = first_call(
        start, turned, shifts, goals, again, alone, first_in, middle_in, hands, held, one, two
    )
    return held, one.reshape(-1), two.reshape(-1), cents


def solution(mesh):
    return jax.shard_map(
        local,
        mesh=mesh,
        in_specs=(P("cube", None), P(None, "cube")),
        out_specs=(P("cube", None), P("cube"), P("cube"), P()),
        check_vma=False,
    )
```

```python
import functools
import jax
import jax.numpy as jnp
from jax import lax
from jax.experimental import pallas as pl
from jax.experimental.pallas import tpu as pltpu
from jax.sharding import PartitionSpec as P

BF = jnp.bfloat16
F32 = jnp.float32
I32 = jnp.int32
BLK = 256
HANDS = 8
WIDE = BLK // 2 + 16
SLOTS = 128
VMEM_BYTES = 48 * 1024 * 1024


def swap(x, bits):
    return lax.ppermute(x, "cube", [(i, i ^ bits) for i in range(lax.axis_size("cube"))])


def dot(a, b):
    return lax.dot_general(a, b, (((1,), (0,)), ((), ())), preferred_element_type=F32)


def dot_t(a, b):
    return lax.dot_general(a, b, (((1,), (1,)), ((), ())), preferred_element_type=F32)


def iota(shape, dim):
    return lax.broadcasted_iota(I32, shape, dim)


def as_bf(mask):
    return jnp.where(mask, jnp.float32(1), jnp.float32(0)).astype(BF)


def pack(sums, counts, width):
    high = sums.astype(BF).astype(F32)
    middle = (sums - high).astype(BF).astype(F32)
    low = sums - high - middle
    spare = width - 128 * len(counts)
    counts = jnp.concatenate(counts + ([jnp.zeros((1, spare), I32)] if spare else []), axis=1)
    upper, lower = (counts >> 8).astype(F32), (counts & 255).astype(F32)
    return jnp.concatenate([high, middle, low, upper, lower, jnp.zeros((2, width), F32)], axis=0).astype(BF)


def unpack(extra):
    extra = extra.astype(F32)
    sums = extra[0:4] + extra[4:8] + extra[8:12]
    return sums, extra[12:13] * 256.0 + extra[13:14]


def count_at(extra, k):
    extra = extra[12:14, 128 * k : 128 * k + 1].astype(F32)
    return (extra[0:1] * 256.0 + extra[1:2]).astype(I32)


def spec(memory):
    return pl.BlockSpec(memory_space=memory)


def params():
    return pltpu.CompilerParams(vmem_limit_bytes=VMEM_BYTES)


def plan_kernel(here, labels, pos, off_ref, every, leavers):
    rows = labels.shape[1]
    blocks = rows // BLK
    leave = labels[0:1, :] != here[0]
    miss = labels[1:2, :] != here[1]
    code = jnp.where(leave, jnp.where(miss, 0, 1), jnp.where(miss, 2, 3))
    code = jnp.concatenate(
        [jnp.broadcast_to(code[:, b * BLK : (b + 1) * BLK], (8, BLK)) for b in range(blocks)], axis=0
    )
    tall = 8 * blocks
    kind = iota((tall, BLK), 0) & 7
    mask = (code == kind) | ((kind == 4) & (code <= 1))
    maskb = as_bf(mask)
    upper = as_bf(iota((BLK, BLK), 0) <= iota((BLK, BLK), 1))
    before = dot(maskb, upper)
    total = dot(maskb, jnp.ones((BLK, BLK), BF)).astype(BF)
    r, c = iota((tall, tall), 0), iota((tall, tall), 1)
    same = ((r ^ c) & 7) == 0
    earlier = as_bf((same & (c < r)) | (((r & 7) == 1) & ((c & 7) == 0)))
    off = dot(earlier, total)
    pos[...] = jnp.where(mask, (before + off).astype(I32) - 1, -1)
    off_ref[...] = (off + jnp.where(iota((tall, BLK), 1) < 64, 0.0, total.astype(F32)))[:, :128].astype(I32)
    r8, c8 = iota((8, tall), 0), iota((8, tall), 1)
    count = dot(as_bf(r8 == (c8 & 7)), total)[:, :128].astype(I32)
    every[...] = count
    leavers[...] = jnp.broadcast_to(count[4:5], leavers.shape)


def plan_call(here, labels):
    rows = labels.shape[1]
    tall = 8 * rows // BLK
    return pl.pallas_call(
        plan_kernel,
        out_shape=[
            jax.ShapeDtypeStruct((tall, BLK), I32),
            jax.ShapeDtypeStruct((tall, 128), I32),
            jax.ShapeDtypeStruct((8, 128), I32),
            jax.ShapeDtypeStruct((8, 128), I32),
        ],
        in_specs=[spec(pltpu.SMEM), spec(pltpu.VMEM)],
        out_specs=[spec(pltpu.VMEM)] * 4,
        compiler_params=params(),
        cost_estimate=pl.CostEstimate(flops=10**8, bytes_accessed=10**5, transcendentals=0),
        name="plan_places",
    )(here, labels)


def sort_kernel(here, labels, pos_ref, off_ref, every, x_hbm, first, middle, rest, x, buf, tail, sums, sem_in, sem_out):
    rows = labels.shape[1]
    blocks = rows // BLK
    cap = rows // 2
    step = rows // 4
    loads = [
        pltpu.make_async_copy(x_hbm.at[pl.ds(k * step, step)], x.at[pl.ds(k * step, step)], sem_in.at[k])
        for k in range(4)
    ]
    for load in loads:
        load.start()
    buf[...] = jnp.zeros_like(buf)
    group = 2 * labels[0:1, :] + labels[1:2, :]
    slot = iota((WIDE, BLK), 0)
    more_slot = iota((BLK + 16 - WIDE, BLK), 0) + WIDE
    sums[...] = jnp.zeros_like(sums)
    tails = []
    for b in range(blocks):
        if b % (step // BLK) == 0:
            loads[b // (step // BLK)].wait()
        vectors = x.at[pl.ds(b * BLK, BLK)]
        hot = [as_bf((iota((16, BLK), 0) & 3) == group[:, b * BLK : (b + 1) * BLK])]
        bases = []
        ends = []
        places = []
        for kind in (0, 1):
            line = slice(8 * b + kind, 8 * b + kind + 1)
            base = pl.multiple_of(jnp.minimum((off_ref[line, 0:1][0, 0] // 16) * 16, cap), 16)
            bases.append(base)
            ends.append(off_ref[line, 64:65][0, 0])
            places.append(pos_ref[line, :] - base)
            hot.append(as_bf(slot == places[kind]))
        got = dot(jnp.concatenate(hot, axis=0), vectors[...])
        sums[...] += got[0:8]
        got = got[16:].astype(BF)
        buf[pl.ds(bases[0], WIDE), :] += got[:WIDE]
        buf[pl.ds(bases[1], 16), :] += got[WIDE : WIDE + 16]
        buf[pl.ds(bases[1] + 16, WIDE - 16), :] = got[WIDE + 16 :]
        for kind in (0, 1):
            tails.append((b, places[kind], bases[kind], ends[kind] - bases[kind]))

    @pl.when(functools.reduce(jnp.maximum, [size for *_, size in tails]) > WIDE)
    def _():
        for b, place, base, size in tails:

            @pl.when(size > WIDE)
            def _():
                more = dot(as_bf(more_slot == place), x[b * BLK : (b + 1) * BLK, :]).astype(BF)
                buf[pl.ds(base + WIDE, BLK + 16 - WIDE), :] += more

    one, two = here[0], here[1]
    kinds = [every[k : k + 1] for k in range(4)]
    counts = []
    for g in range(4):
        away, miss = jnp.int32(g >> 1) != one, jnp.int32(g & 1) != two
        counts.append(jnp.where(away, jnp.where(miss, kinds[0], kinds[1]), jnp.where(miss, kinds[2], kinds[3])))
    tail[...] = pack(sums[0:4, :], counts + [kinds[0], kinds[2]], x.shape[1])
    part = cap // 4
    stores = [
        pltpu.make_async_copy(buf.at[pl.ds(0, part)], first.at[pl.ds(0, part)], sem_out.at[0]),
        pltpu.make_async_copy(buf.at[pl.ds(part, part)], middle, sem_out.at[1]),
        pltpu.make_async_copy(buf.at[pl.ds(2 * part, 2 * part)], rest, sem_out.at[2]),
        pltpu.make_async_copy(tail, first.at[pl.ds(part, 16)], sem_out.at[3]),
    ]
    for store in stores:
        store.start()
    for store in stores:
        store.wait()


def sort_call(here, labels, pos, off, every, vectors):
    rows, width = vectors.shape
    part = rows // 8
    return pl.pallas_call(
        sort_kernel,
        out_shape=[
            jax.ShapeDtypeStruct((part + 16, width), BF),
            jax.ShapeDtypeStruct((part, width), BF),
            jax.ShapeDtypeStruct((2 * part, width), BF),
        ],
        in_specs=[spec(pltpu.SMEM)] + [spec(pltpu.VMEM)] * 4 + [spec(pl.ANY)],
        out_specs=[spec(pl.ANY), spec(pltpu.HBM), spec(pl.ANY)],
        scratch_shapes=[
            pltpu.VMEM((rows, width), BF),
            pltpu.VMEM((rows // 2 + BLK + 16, width), BF),
            pltpu.VMEM((16, width), BF),
            pltpu.VMEM((8, width), F32),
            pltpu.SemaphoreType.DMA((4,)),
            pltpu.SemaphoreType.DMA((4,)),
        ],
        compiler_params=params(),
        cost_estimate=pl.CostEstimate(flops=8 * 10**9, bytes_accessed=10 * 10**6, transcendentals=0),
        name="sort_leavers",
    )(here, labels, pos, off, every, vectors)


def deal_kernel(rest, own, near, top, far, *refs):
    hands, (tail, sem) = refs[:HANDS], refs[HANDS:]
    rows, width = rest.shape
    turns = rows // 16 // HANDS
    counts = jnp.concatenate([ref[0:1, :] for ref in (own, near, top, far)], axis=1)
    counts = jnp.concatenate([counts, jnp.zeros((1, width - 512), I32)], axis=1)
    upper, lower = (counts >> 8).astype(F32), (counts & 255).astype(F32)
    tail[...] = jnp.concatenate([upper, lower, jnp.zeros((14, width), F32)], axis=0).astype(BF)
    copies = []
    for h, hand in enumerate(hands):
        for turn in range(turns):
            block = rest.at[pl.ds(16 * (h + HANDS * turn), 16)]
            copies.append(pltpu.make_async_copy(block, hand.at[pl.ds(16 * turn, 16)], sem.at[h, turn]))
        copies.append(pltpu.make_async_copy(tail, hand.at[pl.ds(16 * turns, 16)], sem.at[h, turns]))
    for copy in copies:
        copy.start()
    for copy in copies:
        copy.wait()


def deal_call(rest, *counts):
    rows, width = rest.shape
    turns = rows // 16 // HANDS
    return pl.pallas_call(
        deal_kernel,
        out_shape=[jax.ShapeDtypeStruct((16 * turns + 16, width), BF)] * HANDS,
        in_specs=[spec(pl.ANY)] + [spec(pltpu.VMEM)] * 4,
        out_specs=[spec(pl.ANY)] * HANDS,
        scratch_shapes=[pltpu.VMEM((16, width), BF), pltpu.SemaphoreType.DMA((HANDS, turns + 1))],
        compiler_params=params(),
        cost_estimate=pl.CostEstimate(flops=0, bytes_accessed=10**5, transcendentals=0),
        name="deal_rest",
    )(rest, *counts)


def pack_kernel(step, *refs):
    hands, (out, longest, begins) = refs[:HANDS], refs[HANDS:]
    rows = hands[0].shape[0] - 16
    out[...] = jnp.zeros_like(out)
    full = []
    for hand in hands:
        count = hand[rows : rows + 2, 0:512].astype(F32)
        count = (count[0:1] * 256.0 + count[1:2]).astype(I32)
        full.append((jnp.maximum(count - rows * HANDS, 0) + 15) >> 4)
    place = jnp.zeros((1, 512), I32)
    for h, hand in enumerate(hands):
        base = pl.multiple_of(place[0, 0] * 16, 16)
        out[pl.ds(base, rows), :] = hand[0:rows, :]
        begins[h : h + 1, :] = place[:, 256:384] * 16
        place = jnp.minimum(place + ((full[h] + (HANDS - 1 - h)) >> 3), (h + 1) * (rows // 16))
    most = jnp.zeros((1, 512), I32)
    for other in range(HANDS):
        size = jnp.zeros((1, 512), I32)
        for h in range(HANDS):
            size = size + ((full[other ^ h] + (HANDS - 1 - h)) >> 3)
        most = jnp.maximum(most, size)
    most = jnp.max(most.astype(F32), axis=1, keepdims=True).astype(I32)
    per = step // 16
    longest[...] = jnp.broadcast_to(jnp.minimum(most + per - 1, out.shape[0] // 16) // per, longest.shape)


def pack_call(step, hands):
    rows, width = hands[0].shape
    rows -= 16
    return pl.pallas_call(
        functools.partial(pack_kernel, step),
        out_shape=[
            jax.ShapeDtypeStruct((rows * HANDS, width), BF),
            jax.ShapeDtypeStruct((8, 128), I32),
            jax.ShapeDtypeStruct((8, 128), I32),
        ],
        in_specs=[spec(pltpu.VMEM)] * HANDS,
        out_specs=[spec(pltpu.VMEM)] * 3,
        compiler_params=params(),
        cost_estimate=pl.CostEstimate(flops=0, bytes_accessed=10**5, transcendentals=0),
        name="pack_hands",
    )(*hands)


def part_kernel(begins, pack_in, *refs):
    hands, sem = refs[:HANDS], refs[HANDS]
    rows = hands[0].shape[0]
    copies = []
    for h, hand in enumerate(hands):
        base = pl.multiple_of((begins[h, 0] // 16) * 16, 16)
        copies.append(pltpu.make_async_copy(pack_in.at[pl.ds(base, rows)], hand, sem.at[h]))
    for copy in copies:
        copy.start()
    for copy in copies:
        copy.wait()


def part_call(begins, pack_in):
    rows, width = pack_in.shape
    return pl.pallas_call(
        part_kernel,
        out_shape=[jax.ShapeDtypeStruct((rows // HANDS, width), BF)] * HANDS,
        in_specs=[spec(pltpu.SMEM), spec(pl.ANY)],
        out_specs=[spec(pl.ANY)] * HANDS,
        scratch_shapes=[pltpu.SemaphoreType.DMA((HANDS,))],
        compiler_params=params(),
        cost_estimate=pl.CostEstimate(flops=0, bytes_accessed=3 * 10**6, transcendentals=0),
        name="part_pack",
    )(begins, pack_in)


def second_send_kernel(off, pos, extra, x_ref, second, meta, buf, ranks):
    step = pl.program_id(0)

    @pl.when(step == 0)
    def _():
        buf[...] = jnp.zeros_like(buf)
        ranks[...] = jnp.zeros_like(ranks)

    half = second.shape[0] - 16
    cap = 4 * half
    wide = BLK + 16
    blocks = x_ref.shape[0] // BLK
    line = iota((16, BLK), 0)
    for sub in range(blocks):
        b = step * blocks + sub
        place = pos[8 * sub : 8 * sub + 8, :]
        base = jnp.minimum((off[8 * b + 2, 0] // 16) * 16, half)
        hot = as_bf(iota((wide, BLK), 0) == place[2:3, :] - base)
        got = dot(hot, x_ref[sub * BLK : (sub + 1) * BLK, :])
        buf[pl.ds(pl.multiple_of(base, 16), wide), :] += got.astype(BF)
        rank = place[4:5, :]
        value = jnp.where(line == 0, rank >> 8, jnp.where(line == 1, rank & 255, 1))
        value = jnp.where(rank >= 0, value, 0).astype(F32).astype(BF)
        for kind in (0, 1):
            base = pl.multiple_of(jnp.minimum((off[8 * b + kind, 0] // 128) * 128, cap), 128)
            hot = as_bf(iota((BLK + 128, BLK), 0) == place[kind : kind + 1, :] - base)
            ranks[:, pl.ds(base, BLK + 128)] += dot_t(value, hot)[:8]

    @pl.when(step == pl.num_programs(0) - 1)
    def _():
        second[0:half, :] = buf[0:half, :]
        second[half:, :] = extra[...]
        seen = ranks[2:3, :cap] > 0.5
        rank = (ranks[0:1, :cap] * 256.0 + ranks[1:2, :cap]).astype(I32)
        goal = jnp.where(seen, rank, 1 << 20)
        line = cap // 8
        for k in range(8):
            meta[k : k + 1, :] = goal[:, k * line : (k + 1) * line]


def second_send_call(off, pos, first, vectors):
    rows, width = vectors.shape
    cap = rows // 2
    half = rows // 8
    return pl.pallas_call(
        second_send_kernel,
        grid=(rows // 1024,),
        out_shape=[
            jax.ShapeDtypeStruct((half + 16, width), BF),
            jax.ShapeDtypeStruct((8, cap // 8), I32),
        ],
        in_specs=[
            spec(pltpu.SMEM),
            pl.BlockSpec((8 * 1024 // BLK, BLK), lambda b: (b, 0)),
            pl.BlockSpec((16, width), lambda b: (half // 16, 0)),
            pl.BlockSpec((1024, width), lambda b: (b, 0)),
        ],
        out_specs=[
            pl.BlockSpec((half + 16, width), lambda b: (0, 0)),
            pl.BlockSpec((8, cap // 8), lambda b: (0, 0)),
        ],
        scratch_shapes=[pltpu.VMEM((half + BLK + 16, width), BF), pltpu.VMEM((8, cap + BLK + 128), F32)],
        compiler_params=params(),
        cost_estimate=pl.CostEstimate(flops=10**8, bytes_accessed=10**6, transcendentals=0),
        name="second_send",
    )(off, pos, first, vectors)


def own_kernel(pos, x_ref, held):
    same = iota((BLK, BLK), 0) == iota((BLK, BLK), 1)
    for sub in range(x_ref.shape[0] // BLK):
        lines = slice(sub * BLK, (sub + 1) * BLK)
        held[lines, :] = dot(as_bf(same & (pos[8 * sub + 3 : 8 * sub + 4, :] >= 0)), x_ref[lines, :]).astype(BF)


def own_call(pos, vectors):
    rows, width = vectors.shape
    return pl.pallas_call(
        own_kernel,
        grid=(rows // 1024,),
        out_shape=jax.ShapeDtypeStruct((rows + rows // 2 + rows // 4, width), BF),
        in_specs=[
            pl.BlockSpec((8 * 1024 // BLK, BLK), lambda b: (b, 0)),
            pl.BlockSpec((1024, width), lambda b: (b, 0)),
        ],
        out_specs=pl.BlockSpec((1024, width), lambda b: (b, 0)),
        compiler_params=params(),
        cost_estimate=pl.CostEstimate(flops=10**8, bytes_accessed=10**6, transcendentals=0),
        name="own_slots",
    )(pos, vectors)


def scores(x, turned):
    score = dot(x, turned)
    lane = iota(score.shape, 1)
    high = score.astype(BF).astype(F32)
    middle = (score - high).astype(BF).astype(F32)
    terms = jnp.where(lane < 4, high, jnp.where(lane < 8, middle, score - high - middle)).astype(BF)
    lane = iota((16, 128), 1)
    return dot_t(as_bf(((lane & 3) == iota((16, 128), 0)) & (lane < 12)), terms)


def margins(score, shift, first, width):
    return (score[first + 1 : first + 2] - score[first : first + 1] - shift) / width


def put_lines(ref, start, values):
    for k in range(values.shape[1] // 128):
        ref[start + k : start + k + 1, :] = values[:, 128 * k : 128 * (k + 1)]


def centre_kernel(here, total, labels, x_ref, cents, turned, shifts, one, two):
    width = x_ref.shape[1]

    @pl.when(pl.program_id(0) == 0)
    def _():
        sums, counts = total[0:4, :], total[4:8, :]
        low = (sums[0:1] + sums[1:2]) / (counts[0:1] + counts[1:2])
        high = (sums[2:3] + sums[3:4]) / (counts[2:3] + counts[3:4])
        groups = sums / counts
        cents[0:1, :] = low
        cents[1:2, :] = high
        cents[2:6, :] = groups
        top = here[0] == 1
        left = jnp.where(top, groups[2:3], groups[0:1])
        right = jnp.where(top, groups[3:4], groups[1:2])
        rows = jnp.concatenate([low, high, left, right] * 3 + [jnp.zeros((116, width), F32)], axis=0)
        turned[...] = rows.T.astype(BF)
        for k, (a, b) in enumerate(((low, high), (left, right))):
            shift = 0.5 * (jnp.sum(b * b, axis=1, keepdims=True) - jnp.sum(a * a, axis=1, keepdims=True))
            shifts[k : k + 1, :] = jnp.broadcast_to(shift, (1, 128))

    score = scores(x_ref[...], turned[...])
    stay = labels[0:1, :] == here[0]
    keep = stay & (labels[1:2, :] == here[1])
    put_lines(one, 0, jnp.where(stay, margins(score, shifts[0:1, 0:1], 0, width), 0.0))
    put_lines(two, 0, jnp.where(keep, margins(score, shifts[1:2, 0:1], 2, width), 0.0))


def centre_call(here, total, labels, vectors):
    rows, width = vectors.shape
    cap = rows // 2
    return pl.pallas_call(
        centre_kernel,
        grid=(rows // 1024,),
        out_shape=[
            jax.ShapeDtypeStruct((6, width), F32),
            jax.ShapeDtypeStruct((width, 128), BF),
            jax.ShapeDtypeStruct((8, 128), F32),
            jax.ShapeDtypeStruct(((rows + cap) // 128, 128), F32),
            jax.ShapeDtypeStruct(((rows + cap + cap // 2) // 128, 128), F32),
        ],
        in_specs=[
            spec(pltpu.SMEM),
            pl.BlockSpec((8, width), lambda b: (0, 0)),
            pl.BlockSpec((2, 1024), lambda b: (0, b)),
            pl.BlockSpec((1024, width), lambda b: (b, 0)),
        ],
        out_specs=[
            pl.BlockSpec((6, width), lambda b: (0, 0)),
            pl.BlockSpec((width, 128), lambda b: (0, 0)),
            pl.BlockSpec((8, 128), lambda b: (0, 0)),
            pl.BlockSpec((8, 128), lambda b: (b, 0)),
            pl.BlockSpec((8, 128), lambda b: (b, 0)),
        ],
        compiler_params=params(),
        cost_estimate=pl.CostEstimate(flops=10**8, bytes_accessed=10**5, transcendentals=0),
        name="own_margins",
    )(here, total, labels, vectors)


def second_kernel(turned, shifts, second, relay, first, meta, leavers, held_in, two_in, held, two, again, alone, start, goals):
    del held_in, two_in
    half = second.shape[0] - 16
    slots = held.shape[0]
    cap = 2 * slots
    have = count_at(second[half:, :], 5)
    more = count_at(relay[half:, :], 4)
    both = count_at(first[half:, :], 4)
    lane = iota((1, half), 1)
    goal = jnp.where(lane < more, lane + have, -1)
    moved = dot(as_bf(iota((slots, half), 0) == goal), relay[0:half, :]).astype(BF)
    held[0:half, :] = moved[0:half] + second[0:half, :]
    held[half:, :] = moved[half:]
    score = scores(held[...], turned[...])
    width = held.shape[1]
    live = iota((1, slots), 1) < have + more
    put_lines(two, 0, jnp.where(live, margins(score, shifts[1:2, 0:1], 2, width), 0.0))

    score = scores(first[0:half, :], turned[...])
    value = jnp.where(lane < both, margins(score, shifts[0:1, 0:1], 0, width), 0.0)
    high = value.astype(BF).astype(F32)
    middle = (value - high).astype(BF).astype(F32)
    low = value - high - middle
    value = jnp.concatenate([high, middle, low, jnp.ones((1, half), F32), jnp.zeros((12, half), F32)], axis=0).astype(BF)
    place = jnp.concatenate([meta[k : k + 1, :] for k in range(8)], axis=1)
    goal = jnp.where(lane < both, place[:, :half], -1)
    for k in range(cap // BLK):
        hot = as_bf(iota((BLK, half), 0) + k * BLK == goal)
        got = dot_t(value, hot)
        put_lines(again, k * BLK // 128, got[0:1] + got[1:2] + got[2:3])
        free = (iota((1, BLK), 1) + k * BLK < leavers[0:1, 0:1]) & (got[3:4] < 0.5)
        put_lines(alone, k * BLK // 128, jnp.where(free, 1.0, 0.0))
    lines = cap // SLOTS
    lane = iota((lines, cap), 1)
    earlier = (lane < both) | (place < SLOTS * iota((lines, cap), 0))
    begin = jnp.sum(jnp.where(earlier, 1.0, 0.0), axis=1, keepdims=True).astype(I32)
    begin = jnp.minimum((begin >> 7) << 7, cap - SLOTS - 128)
    start[...] = jnp.broadcast_to(begin, start.shape)
    goals[...] = jnp.broadcast_to(jnp.where(iota((1, cap), 1) < both, -1, place), goals.shape)


def second_call(turned, shifts, second, relay, first, meta, leavers, held, two):
    half, width = second.shape
    half -= 16
    cap = 4 * half
    slots = cap // 2
    return pl.pallas_call(
        second_kernel,
        grid=(1,),
        out_shape=[
            jax.ShapeDtypeStruct(held.shape, BF),
            jax.ShapeDtypeStruct(two.shape, F32),
            jax.ShapeDtypeStruct((cap // 128, 128), F32),
            jax.ShapeDtypeStruct((cap // 128, 128), F32),
            jax.ShapeDtypeStruct((cap // SLOTS, 128), I32),
            jax.ShapeDtypeStruct((8, cap), I32),
        ],
        in_specs=[spec(pltpu.VMEM)] * 7 + [spec(pl.ANY)] * 2,
        out_specs=[
            pl.BlockSpec((slots, width), lambda b: (held.shape[0] // slots - 1, 0)),
            pl.BlockSpec((slots // 128, 128), lambda b: (held.shape[0] // slots - 1, 0)),
            pl.BlockSpec((cap // 128, 128), lambda b: (0, 0)),
            pl.BlockSpec((cap // 128, 128), lambda b: (0, 0)),
            pl.BlockSpec((cap // SLOTS, 128), lambda b: (0, 0)),
            pl.BlockSpec((8, cap), lambda b: (0, 0)),
        ],
        input_output_aliases={7: 0, 8: 1},
        compiler_params=params(),
        cost_estimate=pl.CostEstimate(flops=10**8, bytes_accessed=10**5, transcendentals=0),
        name="second_slots",
    )(turned, shifts, second, relay, first, meta, leavers, held, two)


def column_kernel(own, a, b, c, out):
    sums, counts = unpack(own[...])
    for other in (a, b, c):
        s, n = unpack(other[...])
        sums, counts = sums + s, counts + n
    out[0:4, :] = sums
    width = out.shape[1]
    for g in range(4):
        out[4 + g : 5 + g, :] = jnp.broadcast_to(counts[:, 128 * g : 128 * g + 1], (1, width))


def column_call(*pieces):
    width = pieces[0].shape[1]
    return pl.pallas_call(
        column_kernel,
        grid=(1,),
        out_shape=jax.ShapeDtypeStruct((8, width), F32),
        in_specs=[pl.BlockSpec((16, width), functools.partial(lambda last, b: (last, 0), p.shape[0] // 16 - 1)) for p in pieces],
        out_specs=pl.BlockSpec((8, width), lambda b: (0, 0)),
        compiler_params=params(),
        name="column_sums",
    )(*pieces)


def first_kernel(start, turned, shifts, goals, again, alone, first, middle, *refs):
    hands, (held_in, one_in, two_in, held, one, two, x, out, sem, sent) = refs[:HANDS], refs[HANDS:]
    del one_in, two_in, held_in
    part, width = middle.shape
    turns = hands[0].shape[0] // 16
    loads = [
        pltpu.make_async_copy(first.at[pl.ds(0, part)], x.at[pl.ds(0, part)], sem.at[HANDS, 0]),
        pltpu.make_async_copy(middle, x.at[pl.ds(part, part)], sem.at[HANDS, 1]),
    ]
    for h, hand in enumerate(hands):
        for turn in range(turns):
            block = x.at[pl.ds(2 * part + 16 * (h + HANDS * turn), 16)]
            loads.append(pltpu.make_async_copy(hand.at[pl.ds(16 * turn, 16)], block, sem.at[h, turn]))
    for load in loads:
        load.start()
    for load in loads:
        load.wait()
    span = SLOTS + 128
    base = 8 * part
    slot = iota((SLOTS, span), 0)
    group = 4
    stores = []
    for k in range(4 * part // SLOTS):
        begin = pl.multiple_of(start[k, 0], 128)
        hot = as_bf(slot == goals[0:1, pl.ds(begin, span)] - k * SLOTS)
        out[k * SLOTS : (k + 1) * SLOTS, :] = dot(hot, x[pl.ds(begin, span), :]).astype(BF)
        if k % group == group - 1:
            size = group * SLOTS
            lines = pl.ds((k + 1) * SLOTS - size, size)
            to = held.at[pl.ds(base + (k + 1) * SLOTS - size, size)]
            stores.append(pltpu.make_async_copy(out.at[lines], to, sent.at[k // group]))
            stores[-1].start()
            score = scores(out[lines, :], turned[...])
            m_one = margins(score, shifts[0:1, 0:1], 0, width)
            m_two = margins(score, shifts[1:2, 0:1], 2, width)
            for i in range(size // 128):
                line = (k + 1) * SLOTS // 128 - size // 128 + i
                line = slice(line, line + 1)
                lanes = slice(128 * i, 128 * (i + 1))
                one[line, :] = jnp.where(alone[line, :] > 0.5, m_one[:, lanes], again[line, :])
                two[line, :] = jnp.where(alone[line, :] > 0.5, m_two[:, lanes], 0.0)
    for store in stores:
        store.wait()


def first_call(start, turned, shifts, goals, again, alone, first, middle, hands, held, one, two):
    width = held.shape[1]
    cap = goals.shape[1]
    lines = cap // 128
    return pl.pallas_call(
        first_kernel,
        grid=(1,),
        out_shape=[
            jax.ShapeDtypeStruct(held.shape, BF),
            jax.ShapeDtypeStruct(one.shape, F32),
            jax.ShapeDtypeStruct(two.shape, F32),
        ],
        in_specs=[spec(pltpu.SMEM)] + [spec(pltpu.VMEM)] * 5 + [spec(pl.ANY)] * (HANDS + 5),
        out_specs=[
            spec(pl.ANY),
            pl.BlockSpec((lines, 128), lambda k: (2, 0)),
            pl.BlockSpec((lines, 128), lambda k: (2, 0)),
        ],
        scratch_shapes=[
            pltpu.VMEM((cap, width), BF),
            pltpu.VMEM((cap, width), BF),
            pltpu.SemaphoreType.DMA((HANDS + 1, cap // 32 // HANDS)),
            pltpu.SemaphoreType.DMA((cap // BLK,)),
        ],
        input_output_aliases={8 + HANDS: 0, 9 + HANDS: 1, 10 + HANDS: 2},
        compiler_params=params(),
        cost_estimate=pl.CostEstimate(flops=3 * 10**9, bytes_accessed=7 * 10**6, transcendentals=0),
        name="first_slots",
    )(start, turned, shifts, goals, again, alone, first, middle, *hands, held, one, two)


def local(vectors, child_labels):
    ways = lax.axis_size("cube")
    top = ways // 2
    nxt = ways // 4
    me = lax.axis_index("cube")
    here = jnp.stack([(me // top) & 1, (me // nxt) & 1]).astype(I32)
    after = lax.optimization_barrier
    pos, off, every, leavers = plan_call(here, child_labels)
    counts = [leavers] + [swap(leavers, bits) for bits in (nxt, top, top | nxt)]
    first, middle, rest = sort_call(here, child_labels, pos, off, every, vectors)
    first, *counts = after((first, *counts))
    first_in = swap(first, top)
    own, *hands = deal_call(rest, *counts)
    hands = [own] + [swap(hand, h + 1) for h, hand in enumerate(hands)]
    after_deal, hands[1], hands[2] = after((pos, hands[1], hands[2]))
    second, meta = second_send_call(off, after_deal, first, vectors)
    second_in = swap(second, nxt)
    after_send, _ = after((after_deal, meta))
    held = own_call(after_send, vectors)
    limit = rest.shape[0]
    step = limit // 32
    held, hands[7] = after((held, hands[7]))
    packed, longest, begins = pack_call(step, hands)
    bit = HANDS
    while bit < nxt:
        longest = jnp.maximum(longest, swap(longest, bit))
        bit *= 2

    def cross(size):
        def branch(rows, first_in, meta):
            got = jnp.pad(swap(rows[:size], top), ((0, limit - size), (0, 0))) if size else jnp.zeros_like(rows)
            return got, swap(first_in, nxt), swap(meta, top)

        return branch

    sizes = range(0, limit + 1, step)
    packed, first_in = after((packed, first_in))
    packed_in, relay, meta_in = lax.switch(longest[0, 0], [cross(size) for size in sizes], packed, first_in, meta)
    middle, packed_in = after((middle, packed_in))
    middle_in = swap(middle, top)
    own, *hands = part_call(begins, packed_in)
    hands = [own] + [swap(hand, h + 1) for h, hand in enumerate(hands)]
    second_in, hands[1] = after((second_in, hands[1]))
    total = column_call(first, second_in, first_in, relay)
    bit = 1
    while bit < nxt:
        total = total + swap(total, bit)
        bit *= 2
    cents, turned, shifts, one, two = centre_call(here, total, child_labels, vectors)
    held, two, again, alone, start, goals = second_call(
        turned, shifts, second_in, relay, first_in, meta_in, counts[2], held, two
    )
    held, one, two = first_call(
        start, turned, shifts, goals, again, alone, first_in, middle_in, hands, held, one, two
    )
    return held, one.reshape(-1), two.reshape(-1), cents


def solution(mesh):
    return jax.shard_map(
        local,
        mesh=mesh,
        in_specs=(P("cube", None), P(None, "cube")),
        out_specs=(P("cube", None), P("cube"), P("cube"), P()),
        check_vma=False,
    )
```

```python
import functools
import jax
import jax.numpy as jnp
from jax import lax
from jax.experimental import pallas as pl
from jax.experimental.pallas import tpu as pltpu
from jax.sharding import PartitionSpec as P

BF = jnp.bfloat16
F32 = jnp.float32
I32 = jnp.int32
BLK = 256
HANDS = 8
WIDE = BLK // 2 + 16
SLOTS = 128
VMEM_BYTES = 28 * 1024 * 1024


def swap(x, bits):
    return lax.ppermute(x, "cube", [(i, i ^ bits) for i in range(lax.axis_size("cube"))])


def dot(a, b):
    return lax.dot_general(a, b, (((1,), (0,)), ((), ())), preferred_element_type=F32)


def dot_t(a, b):
    return lax.dot_general(a, b, (((1,), (1,)), ((), ())), preferred_element_type=F32)


def iota(shape, dim):
    return lax.broadcasted_iota(I32, shape, dim)


def as_bf(mask):
    return jnp.where(mask, jnp.float32(1), jnp.float32(0)).astype(BF)


def pack(sums, counts, width):
    high = sums.astype(BF).astype(F32)
    middle = (sums - high).astype(BF).astype(F32)
    low = sums - high - middle
    spare = width - 128 * len(counts)
    counts = jnp.concatenate(counts + ([jnp.zeros((1, spare), I32)] if spare else []), axis=1)
    upper, lower = (counts >> 8).astype(F32), (counts & 255).astype(F32)
    return jnp.concatenate([high, middle, low, upper, lower, jnp.zeros((2, width), F32)], axis=0).astype(BF)


def unpack(extra):
    extra = extra.astype(F32)
    sums = extra[0:4] + extra[4:8] + extra[8:12]
    return sums, extra[12:13] * 256.0 + extra[13:14]


def count_at(extra, k):
    extra = extra[12:14, 128 * k : 128 * k + 1].astype(F32)
    return (extra[0:1] * 256.0 + extra[1:2]).astype(I32)


def spec(memory):
    return pl.BlockSpec(memory_space=memory)


def params():
    return pltpu.CompilerParams(vmem_limit_bytes=VMEM_BYTES)


def plan_kernel(here, labels, pos, off_ref, every, leavers):
    rows = labels.shape[1]
    blocks = rows // BLK
    leave = labels[0:1, :] != here[0]
    miss = labels[1:2, :] != here[1]
    code = jnp.where(leave, jnp.where(miss, 0, 1), jnp.where(miss, 2, 3))
    code = jnp.concatenate(
        [jnp.broadcast_to(code[:, b * BLK : (b + 1) * BLK], (8, BLK)) for b in range(blocks)], axis=0
    )
    tall = 8 * blocks
    kind = iota((tall, BLK), 0) & 7
    mask = (code == kind) | ((kind == 4) & (code <= 1))
    maskb = as_bf(mask)
    upper = as_bf(iota((BLK, BLK), 0) <= iota((BLK, BLK), 1))
    before = dot(maskb, upper)
    total = dot(maskb, jnp.ones((BLK, BLK), BF)).astype(BF)
    r, c = iota((tall, tall), 0), iota((tall, tall), 1)
    same = ((r ^ c) & 7) == 0
    earlier = as_bf((same & (c < r)) | (((r & 7) == 1) & ((c & 7) == 0)))
    off = dot(earlier, total)
    pos[...] = jnp.where(mask, (before + off).astype(I32) - 1, -1)
    off_ref[...] = (off + jnp.where(iota((tall, BLK), 1) < 64, 0.0, total.astype(F32)))[:, :128].astype(I32)
    r8, c8 = iota((8, tall), 0), iota((8, tall), 1)
    count = dot(as_bf(r8 == (c8 & 7)), total)[:, :128].astype(I32)
    every[...] = count
    leavers[...] = jnp.broadcast_to(count[4:5], leavers.shape)


def plan_call(here, labels):
    rows = labels.shape[1]
    tall = 8 * rows // BLK
    return pl.pallas_call(
        plan_kernel,
        out_shape=[
            jax.ShapeDtypeStruct((tall, BLK), I32),
            jax.ShapeDtypeStruct((tall, 128), I32),
            jax.ShapeDtypeStruct((8, 128), I32),
            jax.ShapeDtypeStruct((8, 128), I32),
        ],
        in_specs=[spec(pltpu.SMEM), spec(pltpu.VMEM)],
        out_specs=[spec(pltpu.VMEM)] * 4,
        compiler_params=params(),
        cost_estimate=pl.CostEstimate(flops=2 * 10**10, bytes_accessed=10**7, transcendentals=0),
        name="plan_places",
    )(here, labels)


def sort_kernel(here, labels, pos_ref, off_ref, every, x, first, middle, rest, buf, sums):
    rows = labels.shape[1]
    blocks = rows // BLK
    cap = rows // 2
    buf[...] = jnp.zeros_like(buf)
    group = 2 * labels[0:1, :] + labels[1:2, :]
    slot = iota((WIDE, BLK), 0)
    more_slot = iota((BLK + 16 - WIDE, BLK), 0) + WIDE
    sums[...] = jnp.zeros_like(sums)
    tails = []
    for b in range(blocks):
        vectors = x.at[pl.ds(b * BLK, BLK)]
        hot = [as_bf((iota((16, BLK), 0) & 3) == group[:, b * BLK : (b + 1) * BLK])]
        bases = []
        ends = []
        places = []
        for kind in (0, 1):
            line = slice(8 * b + kind, 8 * b + kind + 1)
            base = pl.multiple_of(jnp.minimum((off_ref[line, 0:1][0, 0] // 16) * 16, cap), 16)
            bases.append(base)
            ends.append(off_ref[line, 64:65][0, 0])
            places.append(pos_ref[line, :] - base)
            hot.append(as_bf(slot == places[kind]))
        got = dot(jnp.concatenate(hot, axis=0), vectors[...])
        sums[...] += got[0:8]
        got = got[16:].astype(BF)
        buf[pl.ds(bases[0], WIDE), :] += got[:WIDE]
        buf[pl.ds(bases[1], 16), :] += got[WIDE : WIDE + 16]
        buf[pl.ds(bases[1] + 16, WIDE - 16), :] = got[WIDE + 16 :]
        for kind in (0, 1):
            tails.append((b, places[kind], bases[kind], ends[kind] - bases[kind]))

    @pl.when(functools.reduce(jnp.maximum, [size for *_, size in tails]) > WIDE)
    def _():
        for b, place, base, size in tails:

            @pl.when(size > WIDE)
            def _():
                more = dot(as_bf(more_slot == place), x[b * BLK : (b + 1) * BLK, :]).astype(BF)
                buf[pl.ds(base + WIDE, BLK + 16 - WIDE), :] += more

    one, two = here[0], here[1]
    kinds = [every[k : k + 1] for k in range(4)]
    counts = []
    for g in range(4):
        away, miss = jnp.int32(g >> 1) != one, jnp.int32(g & 1) != two
        counts.append(jnp.where(away, jnp.where(miss, kinds[0], kinds[1]), jnp.where(miss, kinds[2], kinds[3])))
    part = cap // 4
    first[0:part, :] = buf[0:part, :]
    first[part:, :] = pack(sums[0:4, :], counts + [kinds[0], kinds[2]], x.shape[1])
    middle[...] = buf[part : 2 * part, :]
    rest[...] = buf[2 * part : cap, :]


def sort_call(here, labels, pos, off, every, vectors):
    rows, width = vectors.shape
    part = rows // 8
    return pl.pallas_call(
        sort_kernel,
        out_shape=[
            jax.ShapeDtypeStruct((part + 16, width), BF),
            jax.ShapeDtypeStruct((part, width), BF),
            jax.ShapeDtypeStruct((2 * part, width), BF),
        ],
        in_specs=[spec(pltpu.SMEM)] + [spec(pltpu.VMEM)] * 5,
        out_specs=[spec(pltpu.VMEM)] * 3,
        scratch_shapes=[pltpu.VMEM((rows // 2 + BLK + 16, width), BF), pltpu.VMEM((8, width), F32)],
        compiler_params=params(),
        cost_estimate=pl.CostEstimate(flops=8 * 10**9, bytes_accessed=10 * 10**6, transcendentals=0),
        name="sort_leavers",
    )(here, labels, pos, off, every, vectors)


def deal_kernel(rest, own, near, top, far, *hands):
    rows, width = rest.shape
    turns = rows // 16 // HANDS
    counts = jnp.concatenate([ref[0:1, :] for ref in (own, near, top, far)], axis=1)
    counts = jnp.concatenate([counts, jnp.zeros((1, width - 512), I32)], axis=1)
    upper, lower = (counts >> 8).astype(F32), (counts & 255).astype(F32)
    tail = jnp.concatenate([upper, lower, jnp.zeros((14, width), F32)], axis=0).astype(BF)
    for h, hand in enumerate(hands):
        for turn in range(turns):
            block = 16 * (h + HANDS * turn)
            hand[16 * turn : 16 * turn + 16, :] = rest[block : block + 16, :]
        hand[16 * turns :, :] = tail


def deal_call(rest, *counts):
    rows, width = rest.shape
    turns = rows // 16 // HANDS
    return pl.pallas_call(
        deal_kernel,
        out_shape=[jax.ShapeDtypeStruct((16 * turns + 16, width), BF)] * HANDS,
        in_specs=[spec(pltpu.VMEM)] * 5,
        out_specs=[spec(pltpu.VMEM)] * HANDS,
        compiler_params=params(),
        cost_estimate=pl.CostEstimate(flops=0, bytes_accessed=10**5, transcendentals=0),
        name="deal_rest",
    )(rest, *counts)


def pack_kernel(step, *refs):
    hands, (out, longest, begins) = refs[:HANDS], refs[HANDS:]
    rows = hands[0].shape[0] - 16
    out[...] = jnp.zeros_like(out)
    full = []
    for hand in hands:
        count = hand[rows : rows + 2, 0:512].astype(F32)
        count = (count[0:1] * 256.0 + count[1:2]).astype(I32)
        full.append((jnp.maximum(count - rows * HANDS, 0) + 15) >> 4)
    place = jnp.zeros((1, 512), I32)
    for h, hand in enumerate(hands):
        base = pl.multiple_of(place[0, 0] * 16, 16)
        out[pl.ds(base, rows), :] = hand[0:rows, :]
        begins[h : h + 1, :] = place[:, 256:384] * 16
        place = jnp.minimum(place + ((full[h] + (HANDS - 1 - h)) >> 3), (h + 1) * (rows // 16))
    most = jnp.zeros((1, 512), I32)
    for other in range(HANDS):
        size = jnp.zeros((1, 512), I32)
        for h in range(HANDS):
            size = size + ((full[other ^ h] + (HANDS - 1 - h)) >> 3)
        most = jnp.maximum(most, size)
    most = jnp.max(most.astype(F32), axis=1, keepdims=True).astype(I32)
    per = step // 16
    longest[...] = jnp.broadcast_to(jnp.minimum(most + per - 1, out.shape[0] // 16) // per, longest.shape)


def pack_call(step, hands):
    rows, width = hands[0].shape
    rows -= 16
    return pl.pallas_call(
        functools.partial(pack_kernel, step),
        out_shape=[
            jax.ShapeDtypeStruct((rows * HANDS, width), BF),
            jax.ShapeDtypeStruct((8, 128), I32),
            jax.ShapeDtypeStruct((8, 128), I32),
        ],
        in_specs=[spec(pltpu.VMEM)] * HANDS,
        out_specs=[spec(pltpu.VMEM)] * 3,
        compiler_params=params(),
        cost_estimate=pl.CostEstimate(flops=0, bytes_accessed=10**5, transcendentals=0),
        name="pack_hands",
    )(*hands)


def part_kernel(begins, pack_in, *refs):
    hands, sem = refs[:HANDS], refs[HANDS]
    rows = hands[0].shape[0]
    copies = []
    for h, hand in enumerate(hands):
        base = pl.multiple_of((begins[h, 0] // 16) * 16, 16)
        copies.append(pltpu.make_async_copy(pack_in.at[pl.ds(base, rows)], hand, sem.at[h]))
    for copy in copies:
        copy.start()
    for copy in copies:
        copy.wait()


def part_call(begins, pack_in):
    rows, width = pack_in.shape
    return pl.pallas_call(
        part_kernel,
        out_shape=[jax.ShapeDtypeStruct((rows // HANDS, width), BF)] * HANDS,
        in_specs=[spec(pltpu.SMEM), spec(pl.ANY)],
        out_specs=[spec(pl.ANY)] * HANDS,
        scratch_shapes=[pltpu.SemaphoreType.DMA((HANDS,))],
        compiler_params=params(),
        cost_estimate=pl.CostEstimate(flops=0, bytes_accessed=3 * 10**6, transcendentals=0),
        name="part_pack",
    )(begins, pack_in)


def second_send_kernel(off, pos, first, x, second, buf):
    half = second.shape[0] - 16
    buf[...] = jnp.zeros_like(buf)
    slot = iota((WIDE, BLK), 0)
    more_slot = iota((BLK + 16 - WIDE, BLK), 0) + WIDE
    tails = []
    for b in range(x.shape[0] // BLK):
        line = slice(8 * b + 2, 8 * b + 3)
        base = pl.multiple_of(jnp.minimum((off[line, 0:1][0, 0] // 16) * 16, half), 16)
        place = pos[line, :] - base
        got = dot(as_bf(slot == place), x[b * BLK : (b + 1) * BLK, :]).astype(BF)
        buf[pl.ds(base, 16), :] += got[:16]
        buf[pl.ds(base + 16, WIDE - 16), :] = got[16:]
        tails.append((b, place, base, off[line, 64:65][0, 0] - base))

    @pl.when(functools.reduce(jnp.maximum, [size for *_, size in tails]) > WIDE)
    def _():
        for b, place, base, size in tails:

            @pl.when(size > WIDE)
            def _():
                more = dot(as_bf(more_slot == place), x[b * BLK : (b + 1) * BLK, :]).astype(BF)
                buf[pl.ds(base + WIDE, BLK + 16 - WIDE), :] += more

    second[0:half, :] = buf[0:half, :]
    second[half:, :] = first[half:, :]


def second_send_call(off, pos, first, x):
    rows, width = x.shape
    half = rows // 8
    return pl.pallas_call(
        second_send_kernel,
        out_shape=jax.ShapeDtypeStruct((half + 16, width), BF),
        in_specs=[spec(pltpu.VMEM)] * 4,
        out_specs=spec(pltpu.VMEM),
        scratch_shapes=[pltpu.VMEM((half + BLK + 16, width), BF)],
        compiler_params=params(),
        cost_estimate=pl.CostEstimate(flops=10**8, bytes_accessed=10**6, transcendentals=0),
        name="second_send",
    )(off, pos, first, x)


def rank_kernel(off, pos, meta, ranks):
    ranks[...] = jnp.zeros_like(ranks)
    cap = 8 * meta.shape[1]
    line = iota((16, BLK), 0)
    slot = iota((BLK + 128, BLK), 0)
    for b in range(pos.shape[0] // 8):
        rank = pos[8 * b + 4 : 8 * b + 5, :]
        value = jnp.where(line == 0, rank >> 8, jnp.where(line == 1, rank & 255, 1))
        value = jnp.where(rank >= 0, value, 0).astype(F32).astype(BF)
        for kind in (0, 1):
            row = slice(8 * b + kind, 8 * b + kind + 1)
            base = pl.multiple_of(jnp.minimum((off[row, 0:1][0, 0] // 128) * 128, cap), 128)
            ranks[:, pl.ds(base, BLK + 128)] += dot_t(value, as_bf(slot == pos[row, :] - base))[:8]
    seen = ranks[2:3, :cap] > 0.5
    rank = (ranks[0:1, :cap] * 256.0 + ranks[1:2, :cap]).astype(I32)
    goal = jnp.where(seen, rank, 1 << 20)
    line = cap // 8
    for k in range(8):
        meta[k : k + 1, :] = goal[:, k * line : (k + 1) * line]


def rank_call(off, pos):
    cap = pos.shape[0] // 8 * BLK // 2
    return pl.pallas_call(
        rank_kernel,
        out_shape=jax.ShapeDtypeStruct((8, cap // 8), I32),
        in_specs=[spec(pltpu.VMEM)] * 2,
        out_specs=spec(pltpu.VMEM),
        scratch_shapes=[pltpu.VMEM((8, cap + BLK + 128), F32)],
        compiler_params=params(),
        cost_estimate=pl.CostEstimate(flops=10**8, bytes_accessed=10**6, transcendentals=0),
        name="list_ranks",
    )(off, pos)


def own_kernel(pos, x, held):
    same = iota((BLK, BLK), 0) == iota((BLK, BLK), 1)
    start = pl.program_id(0) * held.shape[0]
    for sub in range(held.shape[0] // BLK):
        keep = as_bf(same & (pos[8 * sub + 3 : 8 * sub + 4, :] >= 0))
        held[sub * BLK : (sub + 1) * BLK, :] = dot(keep, x[pl.ds(start + sub * BLK, BLK), :]).astype(BF)


def own_call(pos, x):
    rows, width = x.shape
    return pl.pallas_call(
        own_kernel,
        grid=(rows // 1024,),
        out_shape=jax.ShapeDtypeStruct((rows + rows // 2 + rows // 4, width), BF),
        in_specs=[pl.BlockSpec((8 * 1024 // BLK, BLK), lambda b: (b, 0)), spec(pltpu.VMEM)],
        out_specs=pl.BlockSpec((1024, width), lambda b: (b, 0)),
        compiler_params=params(),
        cost_estimate=pl.CostEstimate(flops=10**8, bytes_accessed=10**6, transcendentals=0),
        name="own_slots",
    )(pos, x)


def scores(x, turned):
    score = dot(x, turned)
    lane = iota(score.shape, 1)
    high = score.astype(BF).astype(F32)
    middle = (score - high).astype(BF).astype(F32)
    terms = jnp.where(lane < 4, high, jnp.where(lane < 8, middle, score - high - middle)).astype(BF)
    lane = iota((16, 128), 1)
    return dot_t(as_bf(((lane & 3) == iota((16, 128), 0)) & (lane < 12)), terms)


def margins(score, shift, first, width):
    return (score[first + 1 : first + 2] - score[first : first + 1] - shift) / width


def put_lines(ref, start, values):
    for k in range(values.shape[1] // 128):
        ref[start + k : start + k + 1, :] = values[:, 128 * k : 128 * (k + 1)]


def centre_kernel(here, total, labels, x_ref, cents, turned, shifts, one, two):
    width = x_ref.shape[1]
    lines = labels.shape[1]

    @pl.when(pl.program_id(0) == 0)
    def _():
        sums, counts = total[0:4, :], total[4:8, :]
        low = (sums[0:1] + sums[1:2]) / (counts[0:1] + counts[1:2])
        high = (sums[2:3] + sums[3:4]) / (counts[2:3] + counts[3:4])
        groups = sums / counts
        cents[0:1, :] = low
        cents[1:2, :] = high
        cents[2:6, :] = groups
        top = here[0] == 1
        left = jnp.where(top, groups[2:3], groups[0:1])
        right = jnp.where(top, groups[3:4], groups[1:2])
        rows = jnp.concatenate([low, high, left, right] * 3 + [jnp.zeros((116, width), F32)], axis=0)
        turned[...] = rows.T.astype(BF)
        for k, (a, b) in enumerate(((low, high), (left, right))):
            shift = 0.5 * (jnp.sum(b * b, axis=1, keepdims=True) - jnp.sum(a * a, axis=1, keepdims=True))
            shifts[k : k + 1, :] = jnp.broadcast_to(shift, (1, 128))

    score = scores(x_ref[pl.ds(pl.program_id(0) * lines, lines), :], turned[...])
    stay = labels[0:1, :] == here[0]
    keep = stay & (labels[1:2, :] == here[1])
    put_lines(one, 0, jnp.where(stay, margins(score, shifts[0:1, 0:1], 0, width), 0.0))
    put_lines(two, 0, jnp.where(keep, margins(score, shifts[1:2, 0:1], 2, width), 0.0))


def centre_call(here, total, labels, vectors):
    rows, width = vectors.shape
    cap = rows // 2
    return pl.pallas_call(
        centre_kernel,
        grid=(rows // 1024,),
        out_shape=[
            jax.ShapeDtypeStruct((6, width), F32),
            jax.ShapeDtypeStruct((width, 128), BF),
            jax.ShapeDtypeStruct((8, 128), F32),
            jax.ShapeDtypeStruct(((rows + cap) // 128, 128), F32),
            jax.ShapeDtypeStruct(((rows + cap + cap // 2) // 128, 128), F32),
        ],
        in_specs=[
            spec(pltpu.SMEM),
            pl.BlockSpec((8, width), lambda b: (0, 0)),
            pl.BlockSpec((2, 1024), lambda b: (0, b)),
            spec(pltpu.VMEM),
        ],
        out_specs=[
            pl.BlockSpec((6, width), lambda b: (0, 0)),
            pl.BlockSpec((width, 128), lambda b: (0, 0)),
            pl.BlockSpec((8, 128), lambda b: (0, 0)),
            pl.BlockSpec((8, 128), lambda b: (b, 0)),
            pl.BlockSpec((8, 128), lambda b: (b, 0)),
        ],
        compiler_params=params(),
        cost_estimate=pl.CostEstimate(flops=10**8, bytes_accessed=10**5, transcendentals=0),
        name="own_margins",
    )(here, total, labels, vectors)


def second_kernel(turned, shifts, second, relay, first, meta, leavers, held_in, two_in, held, two, again, alone, start, goals):
    del held_in, two_in
    half = second.shape[0] - 16
    slots = held.shape[0]
    cap = 2 * slots
    have = count_at(second[half:, :], 5)
    more = count_at(relay[half:, :], 4)
    both = count_at(first[half:, :], 4)
    lane = iota((1, half), 1)
    goal = jnp.where(lane < more, lane + have, -1)
    moved = dot(as_bf(iota((slots, half), 0) == goal), relay[0:half, :]).astype(BF)
    held[0:half, :] = moved[0:half] + second[0:half, :]
    held[half:, :] = moved[half:]
    score = scores(held[...], turned[...])
    width = held.shape[1]
    live = iota((1, slots), 1) < have + more
    put_lines(two, 0, jnp.where(live, margins(score, shifts[1:2, 0:1], 2, width), 0.0))

    score = scores(first[0:half, :], turned[...])
    value = jnp.where(lane < both, margins(score, shifts[0:1, 0:1], 0, width), 0.0)
    high = value.astype(BF).astype(F32)
    middle = (value - high).astype(BF).astype(F32)
    low = value - high - middle
    value = jnp.concatenate([high, middle, low, jnp.ones((1, half), F32), jnp.zeros((12, half), F32)], axis=0).astype(BF)
    place = jnp.concatenate([meta[k : k + 1, :] for k in range(8)], axis=1)
    goal = jnp.where(lane < both, place[:, :half], -1)
    for k in range(cap // BLK):
        hot = as_bf(iota((BLK, half), 0) + k * BLK == goal)
        got = dot_t(value, hot)
        put_lines(again, k * BLK // 128, got[0:1] + got[1:2] + got[2:3])
        free = (iota((1, BLK), 1) + k * BLK < leavers[0:1, 0:1]) & (got[3:4] < 0.5)
        put_lines(alone, k * BLK // 128, jnp.where(free, 1.0, 0.0))
    lines = cap // SLOTS
    lane = iota((lines, cap), 1)
    earlier = (lane < both) | (place < SLOTS * iota((lines, cap), 0))
    begin = jnp.sum(jnp.where(earlier, 1.0, 0.0), axis=1, keepdims=True).astype(I32)
    begin = jnp.minimum((begin >> 7) << 7, cap - SLOTS - 128)
    start[...] = jnp.broadcast_to(begin, start.shape)
    goals[...] = jnp.broadcast_to(jnp.where(iota((1, cap), 1) < both, -1, place), goals.shape)


def second_call(turned, shifts, second, relay, first, meta, leavers, held, two):
    half, width = second.shape
    half -= 16
    cap = 4 * half
    slots = cap // 2
    return pl.pallas_call(
        second_kernel,
        grid=(1,),
        out_shape=[
            jax.ShapeDtypeStruct(held.shape, BF),
            jax.ShapeDtypeStruct(two.shape, F32),
            jax.ShapeDtypeStruct((cap // 128, 128), F32),
            jax.ShapeDtypeStruct((cap // 128, 128), F32),
            jax.ShapeDtypeStruct((cap // SLOTS, 128), I32),
            jax.ShapeDtypeStruct((8, cap), I32),
        ],
        in_specs=[spec(pltpu.VMEM)] * 7 + [spec(pl.ANY)] * 2,
        out_specs=[
            pl.BlockSpec((slots, width), lambda b: (held.shape[0] // slots - 1, 0)),
            pl.BlockSpec((slots // 128, 128), lambda b: (held.shape[0] // slots - 1, 0)),
            pl.BlockSpec((cap // 128, 128), lambda b: (0, 0)),
            pl.BlockSpec((cap // 128, 128), lambda b: (0, 0)),
            pl.BlockSpec((cap // SLOTS, 128), lambda b: (0, 0)),
            pl.BlockSpec((8, cap), lambda b: (0, 0)),
        ],
        input_output_aliases={7: 0, 8: 1},
        compiler_params=params(),
        cost_estimate=pl.CostEstimate(flops=10**8, bytes_accessed=10**5, transcendentals=0),
        name="second_slots",
    )(turned, shifts, second, relay, first, meta, leavers, held, two)


def column_kernel(own, a, b, c, out):
    sums, counts = unpack(own[...])
    for other in (a, b, c):
        s, n = unpack(other[...])
        sums, counts = sums + s, counts + n
    out[0:4, :] = sums
    width = out.shape[1]
    for g in range(4):
        out[4 + g : 5 + g, :] = jnp.broadcast_to(counts[:, 128 * g : 128 * g + 1], (1, width))


def column_call(*pieces):
    width = pieces[0].shape[1]
    return pl.pallas_call(
        column_kernel,
        grid=(1,),
        out_shape=jax.ShapeDtypeStruct((8, width), F32),
        in_specs=[pl.BlockSpec((16, width), functools.partial(lambda last, b: (last, 0), p.shape[0] // 16 - 1)) for p in pieces],
        out_specs=pl.BlockSpec((8, width), lambda b: (0, 0)),
        compiler_params=params(),
        name="column_sums",
    )(*pieces)


def first_kernel(start, turned, shifts, goals, again, alone, first, middle, *refs):
    hands, (held_in, one_in, two_in, held, one, two, x, out, sent) = refs[:HANDS], refs[HANDS:]
    del one_in, two_in, held_in
    part, width = middle.shape
    x[0:part, :] = first[0:part, :]
    x[part : 2 * part, :] = middle[...]
    for h, hand in enumerate(hands):
        for turn in range(hand.shape[0] // 16):
            block = 2 * part + 16 * (h + HANDS * turn)
            x[block : block + 16, :] = hand[16 * turn : 16 * turn + 16, :]
    span = SLOTS + 128
    base = 8 * part
    slot = iota((SLOTS, span), 0)
    group = 4
    stores = []
    for k in range(4 * part // SLOTS):
        begin = pl.multiple_of(start[k, 0], 128)
        hot = as_bf(slot == goals[0:1, pl.ds(begin, span)] - k * SLOTS)
        out[k * SLOTS : (k + 1) * SLOTS, :] = dot(hot, x[pl.ds(begin, span), :]).astype(BF)
        if k % group == group - 1:
            size = group * SLOTS
            lines = pl.ds((k + 1) * SLOTS - size, size)
            to = held.at[pl.ds(base + (k + 1) * SLOTS - size, size)]
            stores.append(pltpu.make_async_copy(out.at[lines], to, sent.at[k // group]))
            stores[-1].start()
            score = scores(out[lines, :], turned[...])
            m_one = margins(score, shifts[0:1, 0:1], 0, width)
            m_two = margins(score, shifts[1:2, 0:1], 2, width)
            for i in range(size // 128):
                line = (k + 1) * SLOTS // 128 - size // 128 + i
                line = slice(line, line + 1)
                lanes = slice(128 * i, 128 * (i + 1))
                one[line, :] = jnp.where(alone[line, :] > 0.5, m_one[:, lanes], again[line, :])
                two[line, :] = jnp.where(alone[line, :] > 0.5, m_two[:, lanes], 0.0)
    for store in stores:
        store.wait()


def first_call(start, turned, shifts, goals, again, alone, first, middle, hands, held, one, two):
    width = held.shape[1]
    cap = goals.shape[1]
    lines = cap // 128
    return pl.pallas_call(
        first_kernel,
        grid=(1,),
        out_shape=[
            jax.ShapeDtypeStruct(held.shape, BF),
            jax.ShapeDtypeStruct(one.shape, F32),
            jax.ShapeDtypeStruct(two.shape, F32),
        ],
        in_specs=[spec(pltpu.SMEM)] + [spec(pltpu.VMEM)] * (HANDS + 7) + [spec(pl.ANY)] * 3,
        out_specs=[
            spec(pl.ANY),
            pl.BlockSpec((lines, 128), lambda k: (2, 0)),
            pl.BlockSpec((lines, 128), lambda k: (2, 0)),
        ],
        scratch_shapes=[
            pltpu.VMEM((cap, width), BF),
            pltpu.VMEM((cap, width), BF),
            pltpu.SemaphoreType.DMA((cap // BLK,)),
        ],
        input_output_aliases={8 + HANDS: 0, 9 + HANDS: 1, 10 + HANDS: 2},
        compiler_params=params(),
        cost_estimate=pl.CostEstimate(flops=3 * 10**9, bytes_accessed=7 * 10**6, transcendentals=0),
        name="first_slots",
    )(start, turned, shifts, goals, again, alone, first, middle, *hands, held, one, two)


def local(vectors, child_labels):
    ways = lax.axis_size("cube")
    top = ways // 2
    nxt = ways // 4
    me = lax.axis_index("cube")
    here = jnp.stack([(me // top) & 1, (me // nxt) & 1]).astype(I32)
    after = lax.optimization_barrier
    pos, off, every, leavers = plan_call(here, child_labels)
    counts = [leavers] + [swap(leavers, bits) for bits in (nxt, top, top | nxt)]
    first, middle, rest = sort_call(here, child_labels, pos, off, every, vectors)
    first, *counts = after((first, *counts))
    first_in = swap(first, top)
    second = second_send_call(off, pos, first, vectors)
    second_in = swap(second, nxt)
    rest, second = after((rest, second))
    own, *hands = deal_call(rest, *counts)
    hands = [own] + [swap(hand, h + 1) for h, hand in enumerate(hands)]
    after_deal, hands[1] = after((pos, hands[1]))
    meta = rank_call(off, after_deal)
    held = own_call(after_deal, vectors)
    limit = rest.shape[0]
    step = limit // 32
    held, meta, hands[7] = after((held, meta, hands[7]))
    packed, longest, begins = pack_call(step, hands)
    bit = HANDS
    while bit < nxt:
        longest = jnp.maximum(longest, swap(longest, bit))
        bit *= 2

    def cross(size):
        def branch(rows, first_in, meta):
            got = jnp.pad(swap(rows[:size], top), ((0, limit - size), (0, 0))) if size else jnp.zeros_like(rows)
            return got, swap(first_in, nxt), swap(meta, top)

        return branch

    sizes = range(0, limit + 1, step)
    packed, first_in = after((packed, first_in))
    packed_in, relay, meta_in = lax.switch(longest[0, 0], [cross(size) for size in sizes], packed, first_in, meta)
    middle, packed_in = after((middle, packed_in))
    middle_in = swap(middle, top)
    own, *hands = part_call(begins, packed_in)
    hands = [own] + [swap(hand, h + 1) for h, hand in enumerate(hands)]
    second_in, hands[1] = after((second_in, hands[1]))
    total = column_call(first, second_in, first_in, relay)
    bit = 1
    while bit < nxt:
        total = total + swap(total, bit)
        bit *= 2
    cents, turned, shifts, one, two = centre_call(here, total, child_labels, vectors)
    held, two, again, alone, start, goals = second_call(
        turned, shifts, second_in, relay, first_in, meta_in, counts[2], held, two
    )
    held, one, two = first_call(
        start, turned, shifts, goals, again, alone, first_in, middle_in, hands, held, one, two
    )
    return held, one.reshape(-1), two.reshape(-1), cents


def solution(mesh):
    return jax.shard_map(
        local,
        mesh=mesh,
        in_specs=(P("cube", None), P(None, "cube")),
        out_specs=(P("cube", None), P("cube"), P("cube"), P()),
        check_vma=False,
    )
```

```python
import functools
import jax
import jax.numpy as jnp
from jax import lax
from jax.experimental import pallas as pl
from jax.experimental.pallas import tpu as pltpu
from jax.sharding import PartitionSpec as P

BF = jnp.bfloat16
F32 = jnp.float32
I32 = jnp.int32
BLK = 256
HANDS = 8
WIDE = BLK // 2 + 16
SLOTS = 128
VMEM_BYTES = 28 * 1024 * 1024


def swap(x, bits):
    return lax.ppermute(x, "cube", [(i, i ^ bits) for i in range(lax.axis_size("cube"))])


def dot(a, b):
    return lax.dot_general(a, b, (((1,), (0,)), ((), ())), preferred_element_type=F32)


def dot_t(a, b):
    return lax.dot_general(a, b, (((1,), (1,)), ((), ())), preferred_element_type=F32)


def iota(shape, dim):
    return lax.broadcasted_iota(I32, shape, dim)


def as_bf(mask):
    return jnp.where(mask, jnp.float32(1), jnp.float32(0)).astype(BF)


def pack(sums, counts, width):
    high = sums.astype(BF).astype(F32)
    middle = (sums - high).astype(BF).astype(F32)
    low = sums - high - middle
    spare = width - 128 * len(counts)
    counts = jnp.concatenate(counts + ([jnp.zeros((1, spare), I32)] if spare else []), axis=1)
    upper, lower = (counts >> 8).astype(F32), (counts & 255).astype(F32)
    return jnp.concatenate([high, middle, low, upper, lower, jnp.zeros((2, width), F32)], axis=0).astype(BF)


def unpack(extra):
    extra = extra.astype(F32)
    sums = extra[0:4] + extra[4:8] + extra[8:12]
    return sums, extra[12:13] * 256.0 + extra[13:14]


def count_at(extra, k):
    extra = extra[12:14, 128 * k : 128 * k + 1].astype(F32)
    return (extra[0:1] * 256.0 + extra[1:2]).astype(I32)


def spec(memory):
    return pl.BlockSpec(memory_space=memory)


def params():
    return pltpu.CompilerParams(vmem_limit_bytes=VMEM_BYTES)


def plan_kernel(here, labels, pos, off_ref, every, leavers):
    rows = labels.shape[1]
    blocks = rows // BLK
    leave = labels[0:1, :] != here[0]
    miss = labels[1:2, :] != here[1]
    code = jnp.where(leave, jnp.where(miss, 0, 1), jnp.where(miss, 2, 3))
    code = jnp.concatenate(
        [jnp.broadcast_to(code[:, b * BLK : (b + 1) * BLK], (8, BLK)) for b in range(blocks)], axis=0
    )
    tall = 8 * blocks
    kind = iota((tall, BLK), 0) & 7
    mask = (code == kind) | ((kind == 4) & (code <= 1))
    maskb = as_bf(mask)
    upper = as_bf(iota((BLK, BLK), 0) <= iota((BLK, BLK), 1))
    before = dot(maskb, upper)
    total = dot(maskb, jnp.ones((BLK, BLK), BF)).astype(BF)
    r, c = iota((tall, tall), 0), iota((tall, tall), 1)
    same = ((r ^ c) & 7) == 0
    earlier = as_bf((same & (c < r)) | (((r & 7) == 1) & ((c & 7) == 0)))
    off = dot(earlier, total)
    pos[...] = jnp.where(mask, (before + off).astype(I32) - 1, -1)
    off_ref[...] = (off + jnp.where(iota((tall, BLK), 1) < 64, 0.0, total.astype(F32)))[:, :128].astype(I32)
    r8, c8 = iota((8, tall), 0), iota((8, tall), 1)
    count = dot(as_bf(r8 == (c8 & 7)), total)[:, :128].astype(I32)
    every[...] = count
    leavers[...] = jnp.broadcast_to(count[4:5], leavers.shape)


def plan_call(here, labels):
    rows = labels.shape[1]
    tall = 8 * rows // BLK
    return pl.pallas_call(
        plan_kernel,
        out_shape=[
            jax.ShapeDtypeStruct((tall, BLK), I32),
            jax.ShapeDtypeStruct((tall, 128), I32),
            jax.ShapeDtypeStruct((8, 128), I32),
            jax.ShapeDtypeStruct((8, 128), I32),
        ],
        in_specs=[spec(pltpu.SMEM), spec(pltpu.VMEM)],
        out_specs=[spec(pltpu.VMEM)] * 4,
        compiler_params=params(),
        cost_estimate=pl.CostEstimate(flops=2 * 10**10, bytes_accessed=10**7, transcendentals=0),
        name="plan_places",
    )(here, labels)


def sort_kernel(here, labels, pos_ref, off_ref, every, x, first, middle, rest, buf, sums):
    rows = labels.shape[1]
    blocks = rows // BLK
    cap = rows // 2
    buf[...] = jnp.zeros_like(buf)
    group = 2 * labels[0:1, :] + labels[1:2, :]
    slot = iota((WIDE, BLK), 0)
    more_slot = iota((BLK + 16 - WIDE, BLK), 0) + WIDE
    sums[...] = jnp.zeros_like(sums)
    tails = []
    for b in range(blocks):
        vectors = x.at[pl.ds(b * BLK, BLK)]
        hot = [as_bf((iota((16, BLK), 0) & 3) == group[:, b * BLK : (b + 1) * BLK])]
        bases = []
        ends = []
        places = []
        for kind in (0, 1):
            line = slice(8 * b + kind, 8 * b + kind + 1)
            base = pl.multiple_of(jnp.minimum((off_ref[line, 0:1][0, 0] // 16) * 16, cap), 16)
            bases.append(base)
            ends.append(off_ref[line, 64:65][0, 0])
            places.append(pos_ref[line, :] - base)
            hot.append(as_bf(slot == places[kind]))
        got = dot(jnp.concatenate(hot, axis=0), vectors[...])
        sums[...] += got[0:8]
        got = got[16:].astype(BF)
        buf[pl.ds(bases[0], WIDE), :] += got[:WIDE]
        buf[pl.ds(bases[1], 16), :] += got[WIDE : WIDE + 16]
        buf[pl.ds(bases[1] + 16, WIDE - 16), :] = got[WIDE + 16 :]
        for kind in (0, 1):
            tails.append((b, places[kind], bases[kind], ends[kind] - bases[kind]))

    @pl.when(functools.reduce(jnp.maximum, [size for *_, size in tails]) > WIDE)
    def _():
        for b, place, base, size in tails:

            @pl.when(size > WIDE)
            def _():
                more = dot(as_bf(more_slot == place), x[b * BLK : (b + 1) * BLK, :]).astype(BF)
                buf[pl.ds(base + WIDE, BLK + 16 - WIDE), :] += more

    one, two = here[0], here[1]
    kinds = [every[k : k + 1] for k in range(4)]
    counts = []
    for g in range(4):
        away, miss = jnp.int32(g >> 1) != one, jnp.int32(g & 1) != two
        counts.append(jnp.where(away, jnp.where(miss, kinds[0], kinds[1]), jnp.where(miss, kinds[2], kinds[3])))
    part = cap // 4
    first[0:part, :] = buf[0:part, :]
    first[part:, :] = pack(sums[0:4, :], counts + [kinds[0], kinds[2]], x.shape[1])
    middle[...] = buf[part : 2 * part, :]
    rest[...] = buf[2 * part : cap, :]


def sort_call(here, labels, pos, off, every, vectors):
    rows, width = vectors.shape
    part = rows // 8
    return pl.pallas_call(
        sort_kernel,
        out_shape=[
            jax.ShapeDtypeStruct((part + 16, width), BF),
            jax.ShapeDtypeStruct((part, width), BF),
            jax.ShapeDtypeStruct((2 * part, width), BF),
        ],
        in_specs=[spec(pltpu.SMEM)] + [spec(pltpu.VMEM)] * 5,
        out_specs=[spec(pltpu.VMEM)] * 3,
        scratch_shapes=[pltpu.VMEM((rows // 2 + BLK + 16, width), BF), pltpu.VMEM((8, width), F32)],
        compiler_params=params(),
        cost_estimate=pl.CostEstimate(flops=8 * 10**9, bytes_accessed=10 * 10**6, transcendentals=0),
        name="sort_leavers",
    )(here, labels, pos, off, every, vectors)


def deal_kernel(rest, own, near, top, far, *hands):
    rows, width = rest.shape
    turns = rows // 16 // HANDS
    counts = jnp.concatenate([ref[0:1, :] for ref in (own, near, top, far)], axis=1)
    counts = jnp.concatenate([counts, jnp.zeros((1, width - 512), I32)], axis=1)
    upper, lower = (counts >> 8).astype(F32), (counts & 255).astype(F32)
    tail = jnp.concatenate([upper, lower, jnp.zeros((14, width), F32)], axis=0).astype(BF)
    for h, hand in enumerate(hands):
        for turn in range(turns):
            block = 16 * (h + HANDS * turn)
            hand[16 * turn : 16 * turn + 16, :] = rest[block : block + 16, :]
        hand[16 * turns :, :] = tail


def deal_call(rest, *counts):
    rows, width = rest.shape
    turns = rows // 16 // HANDS
    return pl.pallas_call(
        deal_kernel,
        out_shape=[jax.ShapeDtypeStruct((16 * turns + 16, width), BF)] * HANDS,
        in_specs=[spec(pltpu.VMEM)] * 5,
        out_specs=[spec(pltpu.VMEM)] * HANDS,
        compiler_params=params(),
        cost_estimate=pl.CostEstimate(flops=0, bytes_accessed=10**5, transcendentals=0),
        name="deal_rest",
    )(rest, *counts)


def pack_kernel(step, *refs):
    hands, (out, longest, begins) = refs[:HANDS], refs[HANDS:]
    rows = hands[0].shape[0] - 16
    out[...] = jnp.zeros_like(out)
    full = []
    for hand in hands:
        count = hand[rows : rows + 2, 0:512].astype(F32)
        count = (count[0:1] * 256.0 + count[1:2]).astype(I32)
        full.append((jnp.maximum(count - rows * HANDS, 0) + 15) >> 4)
    place = jnp.zeros((1, 512), I32)
    for h, hand in enumerate(hands):
        base = pl.multiple_of(place[0, 0] * 16, 16)
        out[pl.ds(base, rows), :] = hand[0:rows, :]
        begins[h : h + 1, :] = place[:, 256:384] * 16
        place = jnp.minimum(place + ((full[h] + (HANDS - 1 - h)) >> 3), (h + 1) * (rows // 16))
    most = jnp.zeros((1, 512), I32)
    for other in range(HANDS):
        size = jnp.zeros((1, 512), I32)
        for h in range(HANDS):
            size = size + ((full[other ^ h] + (HANDS - 1 - h)) >> 3)
        most = jnp.maximum(most, size)
    most = jnp.max(most.astype(F32), axis=1, keepdims=True).astype(I32)
    per = step // 16
    longest[...] = jnp.broadcast_to(jnp.minimum(most + per - 1, out.shape[0] // 16) // per, longest.shape)


def pack_call(step, hands):
    rows, width = hands[0].shape
    rows -= 16
    return pl.pallas_call(
        functools.partial(pack_kernel, step),
        out_shape=[
            jax.ShapeDtypeStruct((rows * HANDS, width), BF),
            jax.ShapeDtypeStruct((8, 128), I32),
            jax.ShapeDtypeStruct((8, 128), I32),
        ],
        in_specs=[spec(pltpu.VMEM)] * HANDS,
        out_specs=[spec(pltpu.VMEM)] * 3,
        compiler_params=params(),
        cost_estimate=pl.CostEstimate(flops=0, bytes_accessed=10**5, transcendentals=0),
        name="pack_hands",
    )(*hands)


def part_kernel(begins, pack_in, *refs):
    hands, sem = refs[:HANDS], refs[HANDS]
    rows = hands[0].shape[0]
    copies = []
    for h, hand in enumerate(hands):
        base = pl.multiple_of((begins[h, 0] // 16) * 16, 16)
        copies.append(pltpu.make_async_copy(pack_in.at[pl.ds(base, rows)], hand, sem.at[h]))
    for copy in copies:
        copy.start()
    for copy in copies:
        copy.wait()


def part_call(begins, pack_in):
    rows, width = pack_in.shape
    return pl.pallas_call(
        part_kernel,
        out_shape=[jax.ShapeDtypeStruct((rows // HANDS, width), BF)] * HANDS,
        in_specs=[spec(pltpu.SMEM), spec(pl.ANY)],
        out_specs=[spec(pl.ANY)] * HANDS,
        scratch_shapes=[pltpu.SemaphoreType.DMA((HANDS,))],
        compiler_params=params(),
        cost_estimate=pl.CostEstimate(flops=0, bytes_accessed=3 * 10**6, transcendentals=0),
        name="part_pack",
    )(begins, pack_in)


def second_send_kernel(off, pos, first, x, second, buf):
    half = second.shape[0] - 16
    buf[...] = jnp.zeros_like(buf)
    slot = iota((WIDE, BLK), 0)
    more_slot = iota((BLK + 16 - WIDE, BLK), 0) + WIDE
    tails = []
    for b in range(x.shape[0] // BLK):
        line = slice(8 * b + 2, 8 * b + 3)
        base = pl.multiple_of(jnp.minimum((off[line, 0:1][0, 0] // 16) * 16, half), 16)
        place = pos[line, :] - base
        got = dot(as_bf(slot == place), x[b * BLK : (b + 1) * BLK, :]).astype(BF)
        buf[pl.ds(base, 16), :] += got[:16]
        buf[pl.ds(base + 16, WIDE - 16), :] = got[16:]
        tails.append((b, place, base, off[line, 64:65][0, 0] - base))

    @pl.when(functools.reduce(jnp.maximum, [size for *_, size in tails]) > WIDE)
    def _():
        for b, place, base, size in tails:

            @pl.when(size > WIDE)
            def _():
                more = dot(as_bf(more_slot == place), x[b * BLK : (b + 1) * BLK, :]).astype(BF)
                buf[pl.ds(base + WIDE, BLK + 16 - WIDE), :] += more

    second[0:half, :] = buf[0:half, :]
    second[half:, :] = first[half:, :]


def second_send_call(off, pos, first, x):
    rows, width = x.shape
    half = rows // 8
    return pl.pallas_call(
        second_send_kernel,
        out_shape=jax.ShapeDtypeStruct((half + 16, width), BF),
        in_specs=[spec(pltpu.VMEM)] * 4,
        out_specs=spec(pltpu.VMEM),
        scratch_shapes=[pltpu.VMEM((half + BLK + 16, width), BF)],
        compiler_params=params(),
        cost_estimate=pl.CostEstimate(flops=10**8, bytes_accessed=10**6, transcendentals=0),
        name="second_send",
    )(off, pos, first, x)


def rank_kernel(off, pos, meta, ranks):
    ranks[...] = jnp.zeros_like(ranks)
    cap = 8 * meta.shape[1]
    line = iota((16, BLK), 0)
    slot = iota((BLK + 128, BLK), 0)
    for b in range(pos.shape[0] // 8):
        rank = pos[8 * b + 4 : 8 * b + 5, :]
        value = jnp.where(line == 0, rank >> 8, jnp.where(line == 1, rank & 255, 1))
        value = jnp.where(rank >= 0, value, 0).astype(F32).astype(BF)
        for kind in (0, 1):
            row = slice(8 * b + kind, 8 * b + kind + 1)
            base = pl.multiple_of(jnp.minimum((off[row, 0:1][0, 0] // 128) * 128, cap), 128)
            ranks[:, pl.ds(base, BLK + 128)] += dot_t(value, as_bf(slot == pos[row, :] - base))[:8]
    seen = ranks[2:3, :cap] > 0.5
    rank = (ranks[0:1, :cap] * 256.0 + ranks[1:2, :cap]).astype(I32)
    goal = jnp.where(seen, rank, 1 << 20)
    line = cap // 8
    for k in range(8):
        meta[k : k + 1, :] = goal[:, k * line : (k + 1) * line]


def rank_call(off, pos):
    cap = pos.shape[0] // 8 * BLK // 2
    return pl.pallas_call(
        rank_kernel,
        out_shape=jax.ShapeDtypeStruct((8, cap // 8), I32),
        in_specs=[spec(pltpu.VMEM)] * 2,
        out_specs=spec(pltpu.VMEM),
        scratch_shapes=[pltpu.VMEM((8, cap + BLK + 128), F32)],
        compiler_params=params(),
        cost_estimate=pl.CostEstimate(flops=10**8, bytes_accessed=10**6, transcendentals=0),
        name="list_ranks",
    )(off, pos)


def own_kernel(pos, x, held):
    same = iota((BLK, BLK), 0) == iota((BLK, BLK), 1)
    start = pl.program_id(0) * held.shape[0]
    for sub in range(held.shape[0] // BLK):
        keep = as_bf(same & (pos[8 * sub + 3 : 8 * sub + 4, :] >= 0))
        held[sub * BLK : (sub + 1) * BLK, :] = dot(keep, x[pl.ds(start + sub * BLK, BLK), :]).astype(BF)


def own_call(pos, x):
    rows, width = x.shape
    return pl.pallas_call(
        own_kernel,
        grid=(rows // 1024,),
        out_shape=jax.ShapeDtypeStruct((rows + rows // 2 + rows // 4, width), BF),
        in_specs=[pl.BlockSpec((8 * 1024 // BLK, BLK), lambda b: (b, 0)), spec(pltpu.VMEM)],
        out_specs=pl.BlockSpec((1024, width), lambda b: (b, 0)),
        compiler_params=params(),
        cost_estimate=pl.CostEstimate(flops=10**8, bytes_accessed=10**6, transcendentals=0),
        name="own_slots",
    )(pos, x)


def scores(x, turned):
    score = dot(x, turned)
    lane = iota(score.shape, 1)
    high = score.astype(BF).astype(F32)
    middle = (score - high).astype(BF).astype(F32)
    terms = jnp.where(lane < 4, high, jnp.where(lane < 8, middle, score - high - middle)).astype(BF)
    lane = iota((16, 128), 1)
    return dot_t(as_bf(((lane & 3) == iota((16, 128), 0)) & (lane < 12)), terms)


def margins(score, shift, first, width):
    return (score[first + 1 : first + 2] - score[first : first + 1] - shift) / width


def put_lines(ref, start, values):
    for k in range(values.shape[1] // 128):
        ref[start + k : start + k + 1, :] = values[:, 128 * k : 128 * (k + 1)]


def centre_kernel(here, total, labels, x_hbm, cents, turned, shifts, one, two, x, sem):
    rows, width = x.shape
    part = 1024
    loads = [
        pltpu.make_async_copy(x_hbm.at[pl.ds(k * part, part)], x.at[pl.ds(k * part, part)], sem.at[k])
        for k in range(rows // part)
    ]
    for load in loads:
        load.start()
    sums, counts = total[0:4, :], total[4:8, :]
    low = (sums[0:1] + sums[1:2]) / (counts[0:1] + counts[1:2])
    high = (sums[2:3] + sums[3:4]) / (counts[2:3] + counts[3:4])
    groups = sums / counts
    cents[0:1, :] = low
    cents[1:2, :] = high
    cents[2:6, :] = groups
    top = here[0] == 1
    left = jnp.where(top, groups[2:3], groups[0:1])
    right = jnp.where(top, groups[3:4], groups[1:2])
    columns = jnp.concatenate([low, high, left, right] * 3 + [jnp.zeros((116, width), F32)], axis=0).T.astype(BF)
    turned[...] = columns
    gaps = []
    for k, (a, b) in enumerate(((low, high), (left, right))):
        gaps.append(0.5 * (jnp.sum(b * b, axis=1, keepdims=True) - jnp.sum(a * a, axis=1, keepdims=True)))
        shifts[k : k + 1, :] = jnp.broadcast_to(gaps[k], (1, 128))
    shifts[2:, :] = jnp.zeros((6, 128), F32)
    stay = labels[0:1, :] == here[0]
    keep = stay & (labels[1:2, :] == here[1])
    for k, load in enumerate(loads):
        load.wait()
        lanes = slice(k * part, (k + 1) * part)
        score = scores(x[lanes, :], columns)
        put_lines(one, k * part // 128, jnp.where(stay[:, lanes], margins(score, gaps[0], 0, width), 0.0))
        put_lines(two, k * part // 128, jnp.where(keep[:, lanes], margins(score, gaps[1], 2, width), 0.0))


def centre_call(here, total, labels, vectors):
    rows, width = vectors.shape
    cap = rows // 2
    return pl.pallas_call(
        centre_kernel,
        grid=(1,),
        out_shape=[
            jax.ShapeDtypeStruct((6, width), F32),
            jax.ShapeDtypeStruct((width, 128), BF),
            jax.ShapeDtypeStruct((8, 128), F32),
            jax.ShapeDtypeStruct(((rows + cap) // 128, 128), F32),
            jax.ShapeDtypeStruct(((rows + cap + cap // 2) // 128, 128), F32),
        ],
        in_specs=[spec(pltpu.SMEM), spec(pltpu.VMEM), spec(pltpu.VMEM), spec(pltpu.HBM)],
        out_specs=[
            pl.BlockSpec((6, width), lambda b: (0, 0)),
            pl.BlockSpec((width, 128), lambda b: (0, 0)),
            pl.BlockSpec((8, 128), lambda b: (0, 0)),
            pl.BlockSpec((rows // 128, 128), lambda b: (0, 0)),
            pl.BlockSpec((rows // 128, 128), lambda b: (0, 0)),
        ],
        scratch_shapes=[pltpu.VMEM((rows, width), BF), pltpu.SemaphoreType.DMA((rows // 1024,))],
        compiler_params=params(),
        cost_estimate=pl.CostEstimate(flops=10**8, bytes_accessed=10**5, transcendentals=0),
        name="own_margins",
    )(here, total, labels, vectors)


def second_kernel(turned, shifts, second, relay, first, meta, leavers, held_in, two_in, held, two, again, alone, start, bounds, goals):
    del held_in, two_in
    half = second.shape[0] - 16
    slots = held.shape[0]
    cap = 2 * slots
    have = count_at(second[half:, :], 5)
    more = count_at(relay[half:, :], 4)
    both = count_at(first[half:, :], 4)
    lane = iota((1, half), 1)
    goal = jnp.where(lane < more, lane + have, -1)
    moved = dot(as_bf(iota((slots, half), 0) == goal), relay[0:half, :]).astype(BF)
    held[0:half, :] = moved[0:half] + second[0:half, :]
    held[half:, :] = moved[half:]
    score = scores(held[...], turned[...])
    width = held.shape[1]
    live = iota((1, slots), 1) < have + more
    put_lines(two, 0, jnp.where(live, margins(score, shifts[1:2, 0:1], 2, width), 0.0))

    score = scores(first[0:half, :], turned[...])
    value = jnp.where(lane < both, margins(score, shifts[0:1, 0:1], 0, width), 0.0)
    high = value.astype(BF).astype(F32)
    middle = (value - high).astype(BF).astype(F32)
    low = value - high - middle
    value = jnp.concatenate([high, middle, low, jnp.ones((1, half), F32), jnp.zeros((12, half), F32)], axis=0).astype(BF)
    place = jnp.concatenate([meta[k : k + 1, :] for k in range(8)], axis=1)
    goal = jnp.where(lane < both, place[:, :half], -1)
    for k in range(cap // BLK):
        hot = as_bf(iota((BLK, half), 0) + k * BLK == goal)
        got = dot_t(value, hot)
        put_lines(again, k * BLK // 128, got[0:1] + got[1:2] + got[2:3])
        free = (iota((1, BLK), 1) + k * BLK < leavers[0:1, 0:1]) & (got[3:4] < 0.5)
        put_lines(alone, k * BLK // 128, jnp.where(free, 1.0, 0.0))
    lines = cap // SLOTS
    lane = iota((lines, cap), 1)
    earlier = (lane < both) | (place < SLOTS * iota((lines, cap), 0))
    begin = jnp.sum(jnp.where(earlier, 1.0, 0.0), axis=1, keepdims=True).astype(I32)
    begin = jnp.minimum((begin >> 7) << 7, cap - SLOTS - 128)
    start[...] = jnp.broadcast_to(begin, start.shape)
    lane = iota((8, cap), 1)
    edge = 2 * SLOTS * iota((8, cap), 0)
    before = jnp.sum(jnp.where((lane < both) | (place < edge), 1.0, 0.0), axis=1, keepdims=True)
    until = jnp.sum(jnp.where((lane < both) | (place < edge + 2 * SLOTS), 1.0, 0.0), axis=1, keepdims=True)
    low = jnp.sum(jnp.where(until <= half, 1.0, 0.0), axis=0, keepdims=True).astype(I32)
    high = jnp.sum(jnp.where(before < 2 * half, 1.0, 0.0), axis=0, keepdims=True).astype(I32)
    bounds[...] = jnp.broadcast_to(jnp.where(iota((8, 1), 0) == 0, low, high), bounds.shape)
    goals[...] = jnp.broadcast_to(jnp.where(iota((1, cap), 1) < both, -1, place), goals.shape)


def second_call(turned, shifts, second, relay, first, meta, leavers, held, two):
    half, width = second.shape
    half -= 16
    cap = 4 * half
    slots = cap // 2
    return pl.pallas_call(
        second_kernel,
        grid=(1,),
        out_shape=[
            jax.ShapeDtypeStruct(held.shape, BF),
            jax.ShapeDtypeStruct(two.shape, F32),
            jax.ShapeDtypeStruct((cap // 128, 128), F32),
            jax.ShapeDtypeStruct((cap // 128, 128), F32),
            jax.ShapeDtypeStruct((cap // SLOTS, 128), I32),
            jax.ShapeDtypeStruct((8, 128), I32),
            jax.ShapeDtypeStruct((8, cap), I32),
        ],
        in_specs=[spec(pltpu.VMEM)] * 7 + [spec(pl.ANY)] * 2,
        out_specs=[
            pl.BlockSpec((slots, width), lambda b: (held.shape[0] // slots - 1, 0)),
            pl.BlockSpec((slots // 128, 128), lambda b: (held.shape[0] // slots - 1, 0)),
            pl.BlockSpec((cap // 128, 128), lambda b: (0, 0)),
            pl.BlockSpec((cap // 128, 128), lambda b: (0, 0)),
            pl.BlockSpec((cap // SLOTS, 128), lambda b: (0, 0)),
            pl.BlockSpec((8, 128), lambda b: (0, 0)),
            pl.BlockSpec((8, cap), lambda b: (0, 0)),
        ],
        input_output_aliases={7: 0, 8: 1},
        compiler_params=params(),
        cost_estimate=pl.CostEstimate(flops=10**8, bytes_accessed=10**5, transcendentals=0),
        name="second_slots",
    )(turned, shifts, second, relay, first, meta, leavers, held, two)


def column_kernel(own, a, b, c, out):
    sums, counts = unpack(own[...])
    for other in (a, b, c):
        s, n = unpack(other[...])
        sums, counts = sums + s, counts + n
    out[0:4, :] = sums
    width = out.shape[1]
    for g in range(4):
        out[4 + g : 5 + g, :] = jnp.broadcast_to(counts[:, 128 * g : 128 * g + 1], (1, width))


def column_call(*pieces):
    width = pieces[0].shape[1]
    return pl.pallas_call(
        column_kernel,
        grid=(1,),
        out_shape=jax.ShapeDtypeStruct((8, width), F32),
        in_specs=[pl.BlockSpec((16, width), functools.partial(lambda last, b: (last, 0), p.shape[0] // 16 - 1)) for p in pieces],
        out_specs=pl.BlockSpec((8, width), lambda b: (0, 0)),
        compiler_params=params(),
        name="column_sums",
    )(*pieces)


def first_kernel(late, start, bounds, turned, shifts, goals, again, alone, first, *refs):
    middle, refs = (refs[0], refs[1:]) if late else (None, refs)
    hands, (held_in, one_in, two_in, held, one, two, x, out, sent) = refs[:HANDS], refs[HANDS:]
    del held_in
    width = first.shape[1]
    part = first.shape[0] - 16
    pairs = 4 * part // (2 * SLOTS)
    x[0:part, :] = first[0:part, :]
    x[part : 2 * part, :] = middle[...] if late else jnp.zeros((part, width), BF)
    for h, hand in enumerate(hands):
        for turn in range(hand.shape[0] // 16):
            block = 2 * part + 16 * (h + HANDS * turn)
            x[block : block + 16, :] = hand[16 * turn : 16 * turn + 16, :]
    if late:
        one[...] = one_in[...]
        two[...] = two_in[...]
    else:
        one[...] = jnp.zeros_like(one)
        two[...] = jnp.zeros_like(two)
    span = SLOTS + 128
    base = 8 * part
    slot = iota((SLOTS, span), 0)

    def store(pair):
        lines = pl.multiple_of(pair * 2 * SLOTS, 2 * SLOTS)
        to = held.at[pl.ds(base + lines, 2 * SLOTS)]
        return pltpu.make_async_copy(out.at[pl.ds(lines, 2 * SLOTS)], to, sent.at[pair])

    def place(pair, _):
        lines = pl.multiple_of(pair * 2 * SLOTS, 2 * SLOTS)
        rows = []
        for i in range(2):
            begin = pl.multiple_of((start[2 * pair + i, 0] // 128) * 128, 128)
            hot = as_bf(slot == goals[0:1, pl.ds(begin, span)] - (lines + i * SLOTS))
            rows.append(dot(hot, x[pl.ds(begin, span), :]).astype(BF))
        rows = jnp.concatenate(rows, axis=0)
        out[pl.ds(lines, 2 * SLOTS), :] = rows
        store(pair).start()
        score = scores(rows, turned[...])
        m_one = margins(score, shifts[0:1, 0:1], 0, width)
        m_two = margins(score, shifts[1:2, 0:1], 2, width)
        for i in range(2):
            line = pl.ds(2 * pair + i, 1)
            lanes = slice(SLOTS * i, SLOTS * (i + 1))
            one[line, :] = jnp.where(alone[line, :] > 0.5, m_one[:, lanes], again[line, :])
            two[line, :] = jnp.where(alone[line, :] > 0.5, m_two[:, lanes], 0.0)
        return 0

    def finish(pair, _):
        store(pair).wait()
        return 0

    low = jnp.minimum(bounds[0, 0], pairs)
    high = jnp.clip(bounds[1, 0], low, pairs)
    ranges = [(low, high)] if late else [(0, low), (high, pairs)]
    for work in (place, finish):
        for begin, end in ranges:
            lax.fori_loop(begin, end, work, 0)


def first_call(start, bounds, turned, shifts, goals, again, alone, first, middle, hands, held, one, two):
    width = held.shape[1]
    cap = goals.shape[1]
    lines = cap // 128
    late = middle is not None
    pieces = [first, *([middle] if late else []), *hands]
    block = pl.BlockSpec((lines, 128), lambda k: (2, 0))
    given = 7 + len(pieces)
    return pl.pallas_call(
        functools.partial(first_kernel, late),
        grid=(1,),
        out_shape=[
            jax.ShapeDtypeStruct(held.shape, BF),
            jax.ShapeDtypeStruct(one.shape, F32),
            jax.ShapeDtypeStruct(two.shape, F32),
        ],
        in_specs=[spec(pltpu.SMEM)] * 2
        + [spec(pltpu.VMEM)] * (given - 2)
        + [spec(pl.ANY)]
        + ([block] * 2 if late else [spec(pl.ANY)] * 2),
        out_specs=[spec(pl.ANY), block, block],
        scratch_shapes=[
            pltpu.VMEM((cap, width), BF),
            pltpu.VMEM((cap, width), BF),
            pltpu.SemaphoreType.DMA((cap // (2 * SLOTS),)),
        ],
        input_output_aliases={given: 0, given + 1: 1, given + 2: 2},
        compiler_params=params(),
        cost_estimate=pl.CostEstimate(flops=10**9, bytes_accessed=10**6, transcendentals=0),
        name="last_slots" if late else "first_slots",
    )(start, bounds, turned, shifts, goals, again, alone, *pieces, held, one, two)


def local(vectors, child_labels):
    ways = lax.axis_size("cube")
    top = ways // 2
    nxt = ways // 4
    me = lax.axis_index("cube")
    here = jnp.stack([(me // top) & 1, (me // nxt) & 1]).astype(I32)
    after = lax.optimization_barrier
    pos, off, every, leavers = plan_call(here, child_labels)
    counts = [leavers] + [swap(leavers, bits) for bits in (nxt, top, top | nxt)]
    first, middle, rest = sort_call(here, child_labels, pos, off, every, vectors)
    first, *counts = after((first, *counts))
    first_in = swap(first, top)
    second = second_send_call(off, pos, first, vectors)
    second_in = swap(second, nxt)
    rest, second = after((rest, second))
    own, *hands = deal_call(rest, *counts)
    hands = [own] + [swap(hand, h + 1) for h, hand in enumerate(hands)]
    after_deal, hands[1] = after((pos, hands[1]))
    meta = rank_call(off, after_deal)
    held = own_call(after_deal, vectors)
    limit = rest.shape[0]
    step = limit // 32
    held, meta, hands[7] = after((held, meta, hands[7]))
    packed, longest, begins = pack_call(step, hands)
    bit = HANDS
    while bit < nxt:
        longest = jnp.maximum(longest, swap(longest, bit))
        bit *= 2

    def cross(size):
        def branch(rows, first_in, meta):
            got = jnp.pad(swap(rows[:size], top), ((0, limit - size), (0, 0))) if size else jnp.zeros_like(rows)
            return got, swap(first_in, nxt), swap(meta, top)

        return branch

    sizes = range(0, limit + 1, step)
    packed, first_in = after((packed, first_in))
    packed_in, relay, meta_in = lax.switch(longest[0, 0], [cross(size) for size in sizes], packed, first_in, meta)
    middle, packed_in = after((middle, packed_in))
    middle_in = swap(middle, top)
    own, *hands = part_call(begins, packed_in)
    hands = [own] + [swap(hand, h + 1) for h, hand in enumerate(hands)]
    second_in, hands[1] = after((second_in, hands[1]))
    total = column_call(first, second_in, first_in, relay)
    bit = 1
    while bit < nxt:
        total = total + swap(total, bit)
        bit *= 2
    cents, turned, shifts, one, two = centre_call(here, total, child_labels, vectors)
    held, two, again, alone, start, bounds, goals = second_call(
        turned, shifts, second_in, relay, first_in, meta_in, counts[2], held, two
    )
    known = start, bounds, turned, shifts, goals, again, alone, first_in
    held, one, two = first_call(*known, None, hands, held, one, two)
    held, one, two = first_call(*known, middle_in, hands, held, one, two)
    return held, one.reshape(-1), two.reshape(-1), cents


def solution(mesh):
    return jax.shard_map(
        local,
        mesh=mesh,
        in_specs=(P("cube", None), P(None, "cube")),
        out_specs=(P("cube", None), P("cube"), P("cube"), P()),
        check_vma=False,
    )
```

```python
import functools
import jax
import jax.numpy as jnp
from jax import lax
from jax.experimental import pallas as pl
from jax.experimental.pallas import tpu as pltpu
from jax.sharding import PartitionSpec as P

BF = jnp.bfloat16
F32 = jnp.float32
I32 = jnp.int32
BLK = 256
HANDS = 8
WIDE = BLK // 2 + 16
SLOTS = 128
VMEM_BYTES = 28 * 1024 * 1024


def swap(x, bits):
    return lax.ppermute(x, "cube", [(i, i ^ bits) for i in range(lax.axis_size("cube"))])


def dot(a, b):
    return lax.dot_general(a, b, (((1,), (0,)), ((), ())), preferred_element_type=F32)


def dot_t(a, b):
    return lax.dot_general(a, b, (((1,), (1,)), ((), ())), preferred_element_type=F32)


def iota(shape, dim):
    return lax.broadcasted_iota(I32, shape, dim)


def as_bf(mask):
    return jnp.where(mask, jnp.float32(1), jnp.float32(0)).astype(BF)


def pack(sums, counts, width):
    high = sums.astype(BF).astype(F32)
    middle = (sums - high).astype(BF).astype(F32)
    low = sums - high - middle
    spare = width - 128 * len(counts)
    counts = jnp.concatenate(counts + ([jnp.zeros((1, spare), I32)] if spare else []), axis=1)
    upper, lower = (counts >> 8).astype(F32), (counts & 255).astype(F32)
    return jnp.concatenate([high, middle, low, upper, lower, jnp.zeros((2, width), F32)], axis=0).astype(BF)


def unpack(extra):
    extra = extra.astype(F32)
    sums = extra[0:4] + extra[4:8] + extra[8:12]
    return sums, extra[12:13] * 256.0 + extra[13:14]


def count_at(extra, k):
    extra = extra[12:14, 128 * k : 128 * k + 1].astype(F32)
    return (extra[0:1] * 256.0 + extra[1:2]).astype(I32)


def spec(memory):
    return pl.BlockSpec(memory_space=memory)


def params():
    return pltpu.CompilerParams(vmem_limit_bytes=VMEM_BYTES)


def plan_kernel(here, labels, pos, off_ref, every, leavers):
    rows = labels.shape[1]
    blocks = rows // BLK
    leave = labels[0:1, :] != here[0]
    miss = labels[1:2, :] != here[1]
    code = jnp.where(leave, jnp.where(miss, 0, 1), jnp.where(miss, 2, 3))
    code = jnp.concatenate(
        [jnp.broadcast_to(code[:, b * BLK : (b + 1) * BLK], (8, BLK)) for b in range(blocks)], axis=0
    )
    tall = 8 * blocks
    kind = iota((tall, BLK), 0) & 7
    mask = (code == kind) | ((kind == 4) & (code <= 1))
    maskb = as_bf(mask)
    upper = as_bf(iota((BLK, BLK), 0) <= iota((BLK, BLK), 1))
    before = dot(maskb, upper)
    total = dot(maskb, jnp.ones((BLK, BLK), BF)).astype(BF)
    r, c = iota((tall, tall), 0), iota((tall, tall), 1)
    same = ((r ^ c) & 7) == 0
    earlier = as_bf((same & (c < r)) | (((r & 7) == 1) & ((c & 7) == 0)))
    off = dot(earlier, total)
    pos[...] = jnp.where(mask, (before + off).astype(I32) - 1, -1)
    off_ref[...] = (off + jnp.where(iota((tall, BLK), 1) < 64, 0.0, total.astype(F32)))[:, :128].astype(I32)
    r8, c8 = iota((8, tall), 0), iota((8, tall), 1)
    count = dot(as_bf(r8 == (c8 & 7)), total)[:, :128].astype(I32)
    every[...] = count
    leavers[...] = jnp.broadcast_to(count[4:5], leavers.shape)


def plan_call(here, labels):
    rows = labels.shape[1]
    tall = 8 * rows // BLK
    return pl.pallas_call(
        plan_kernel,
        out_shape=[
            jax.ShapeDtypeStruct((tall, BLK), I32),
            jax.ShapeDtypeStruct((tall, 128), I32),
            jax.ShapeDtypeStruct((8, 128), I32),
            jax.ShapeDtypeStruct((8, 128), I32),
        ],
        in_specs=[spec(pltpu.SMEM), spec(pltpu.VMEM)],
        out_specs=[spec(pltpu.VMEM)] * 4,
        compiler_params=params(),
        cost_estimate=pl.CostEstimate(flops=2 * 10**10, bytes_accessed=10**7, transcendentals=0),
        name="plan_places",
    )(here, labels)


def sort_kernel(here, labels, pos_ref, off_ref, every, x, first, middle, rest, buf, sums):
    rows = labels.shape[1]
    blocks = rows // BLK
    cap = rows // 2
    buf[...] = jnp.zeros_like(buf)
    group = 2 * labels[0:1, :] + labels[1:2, :]
    slot = iota((WIDE, BLK), 0)
    more_slot = iota((BLK + 16 - WIDE, BLK), 0) + WIDE
    sums[...] = jnp.zeros_like(sums)
    tails = []
    for b in range(blocks):
        vectors = x.at[pl.ds(b * BLK, BLK)]
        hot = [as_bf((iota((16, BLK), 0) & 3) == group[:, b * BLK : (b + 1) * BLK])]
        bases = []
        ends = []
        places = []
        for kind in (0, 1):
            line = slice(8 * b + kind, 8 * b + kind + 1)
            base = pl.multiple_of(jnp.minimum((off_ref[line, 0:1][0, 0] // 16) * 16, cap), 16)
            bases.append(base)
            ends.append(off_ref[line, 64:65][0, 0])
            places.append(pos_ref[line, :] - base)
            hot.append(as_bf(slot == places[kind]))
        got = dot(jnp.concatenate(hot, axis=0), vectors[...])
        sums[...] += got[0:8]
        got = got[16:].astype(BF)
        buf[pl.ds(bases[0], WIDE), :] += got[:WIDE]
        buf[pl.ds(bases[1], 16), :] += got[WIDE : WIDE + 16]
        buf[pl.ds(bases[1] + 16, WIDE - 16), :] = got[WIDE + 16 :]
        for kind in (0, 1):
            tails.append((b, places[kind], bases[kind], ends[kind] - bases[kind]))

    @pl.when(functools.reduce(jnp.maximum, [size for *_, size in tails]) > WIDE)
    def _():
        for b, place, base, size in tails:

            @pl.when(size > WIDE)
            def _():
                more = dot(as_bf(more_slot == place), x[b * BLK : (b + 1) * BLK, :]).astype(BF)
                buf[pl.ds(base + WIDE, BLK + 16 - WIDE), :] += more

    one, two = here[0], here[1]
    kinds = [every[k : k + 1] for k in range(4)]
    counts = []
    for g in range(4):
        away, miss = jnp.int32(g >> 1) != one, jnp.int32(g & 1) != two
        counts.append(jnp.where(away, jnp.where(miss, kinds[0], kinds[1]), jnp.where(miss, kinds[2], kinds[3])))
    part = cap // 4
    first[0:part, :] = buf[0:part, :]
    first[part:, :] = pack(sums[0:4, :], counts + [kinds[0], kinds[2]], x.shape[1])
    middle[...] = buf[part : 2 * part, :]
    rest[...] = buf[2 * part : cap, :]


def sort_call(here, labels, pos, off, every, vectors):
    rows, width = vectors.shape
    part = rows // 8
    return pl.pallas_call(
        sort_kernel,
        out_shape=[
            jax.ShapeDtypeStruct((part + 16, width), BF),
            jax.ShapeDtypeStruct((part, width), BF),
            jax.ShapeDtypeStruct((2 * part, width), BF),
        ],
        in_specs=[spec(pltpu.SMEM)] + [spec(pltpu.VMEM)] * 5,
        out_specs=[spec(pltpu.VMEM)] * 3,
        scratch_shapes=[pltpu.VMEM((rows // 2 + BLK + 16, width), BF), pltpu.VMEM((8, width), F32)],
        compiler_params=params(),
        cost_estimate=pl.CostEstimate(flops=8 * 10**9, bytes_accessed=10 * 10**6, transcendentals=0),
        name="sort_leavers",
    )(here, labels, pos, off, every, vectors)


def deal_kernel(rest, own, near, top, far, *hands):
    rows, width = rest.shape
    turns = rows // 16 // HANDS
    counts = jnp.concatenate([ref[0:1, :] for ref in (own, near, top, far)], axis=1)
    counts = jnp.concatenate([counts, jnp.zeros((1, width - 512), I32)], axis=1)
    upper, lower = (counts >> 8).astype(F32), (counts & 255).astype(F32)
    tail = jnp.concatenate([upper, lower, jnp.zeros((14, width), F32)], axis=0).astype(BF)
    for h, hand in enumerate(hands):
        for turn in range(turns):
            block = 16 * (h + HANDS * turn)
            hand[16 * turn : 16 * turn + 16, :] = rest[block : block + 16, :]
        hand[16 * turns :, :] = tail


def deal_call(rest, *counts):
    rows, width = rest.shape
    turns = rows // 16 // HANDS
    return pl.pallas_call(
        deal_kernel,
        out_shape=[jax.ShapeDtypeStruct((16 * turns + 16, width), BF)] * HANDS,
        in_specs=[spec(pltpu.VMEM)] * 5,
        out_specs=[spec(pltpu.VMEM)] * HANDS,
        compiler_params=params(),
        cost_estimate=pl.CostEstimate(flops=0, bytes_accessed=10**5, transcendentals=0),
        name="deal_rest",
    )(rest, *counts)


def pack_kernel(step, *refs):
    hands, (out, longest, begins) = refs[:HANDS], refs[HANDS:]
    rows = hands[0].shape[0] - 16
    out[...] = jnp.zeros_like(out)
    full = []
    for hand in hands:
        count = hand[rows : rows + 2, 0:512].astype(F32)
        count = (count[0:1] * 256.0 + count[1:2]).astype(I32)
        full.append((jnp.maximum(count - rows * HANDS, 0) + 15) >> 4)
    place = jnp.zeros((1, 512), I32)
    for h, hand in enumerate(hands):
        base = pl.multiple_of(place[0, 0] * 16, 16)
        out[pl.ds(base, rows), :] = hand[0:rows, :]
        begins[h : h + 1, :] = place[:, 256:384] * 16
        place = jnp.minimum(place + ((full[h] + (HANDS - 1 - h)) >> 3), (h + 1) * (rows // 16))
    most = jnp.zeros((1, 512), I32)
    for other in range(HANDS):
        size = jnp.zeros((1, 512), I32)
        for h in range(HANDS):
            size = size + ((full[other ^ h] + (HANDS - 1 - h)) >> 3)
        most = jnp.maximum(most, size)
    most = jnp.max(most.astype(F32), axis=1, keepdims=True).astype(I32)
    per = step // 16
    longest[...] = jnp.broadcast_to(jnp.minimum(most + per - 1, out.shape[0] // 16) // per, longest.shape)


def pack_call(step, hands):
    rows, width = hands[0].shape
    rows -= 16
    return pl.pallas_call(
        functools.partial(pack_kernel, step),
        out_shape=[
            jax.ShapeDtypeStruct((rows * HANDS, width), BF),
            jax.ShapeDtypeStruct((8, 128), I32),
            jax.ShapeDtypeStruct((8, 128), I32),
        ],
        in_specs=[spec(pltpu.VMEM)] * HANDS,
        out_specs=[spec(pltpu.VMEM)] * 3,
        compiler_params=params(),
        cost_estimate=pl.CostEstimate(flops=0, bytes_accessed=10**5, transcendentals=0),
        name="pack_hands",
    )(*hands)


def part_kernel(begins, pack_in, *refs):
    hands, sem = refs[:HANDS], refs[HANDS]
    rows = hands[0].shape[0]
    copies = []
    for h, hand in enumerate(hands):
        base = pl.multiple_of((begins[h, 0] // 16) * 16, 16)
        copies.append(pltpu.make_async_copy(pack_in.at[pl.ds(base, rows)], hand, sem.at[h]))
    for copy in copies:
        copy.start()
    for copy in copies:
        copy.wait()


def part_call(begins, pack_in):
    rows, width = pack_in.shape
    return pl.pallas_call(
        part_kernel,
        out_shape=[jax.ShapeDtypeStruct((rows // HANDS, width), BF)] * HANDS,
        in_specs=[spec(pltpu.SMEM), spec(pl.ANY)],
        out_specs=[spec(pl.ANY)] * HANDS,
        scratch_shapes=[pltpu.SemaphoreType.DMA((HANDS,))],
        compiler_params=params(),
        cost_estimate=pl.CostEstimate(flops=2 * 10**10, bytes_accessed=3 * 10**6, transcendentals=0),
        name="part_pack",
    )(begins, pack_in)


def second_send_kernel(off, pos, first, x, second, buf):
    half = second.shape[0] - 16
    buf[...] = jnp.zeros_like(buf)
    slot = iota((WIDE, BLK), 0)
    more_slot = iota((BLK + 16 - WIDE, BLK), 0) + WIDE
    tails = []
    for b in range(x.shape[0] // BLK):
        line = slice(8 * b + 2, 8 * b + 3)
        base = pl.multiple_of(jnp.minimum((off[line, 0:1][0, 0] // 16) * 16, half), 16)
        place = pos[line, :] - base
        got = dot(as_bf(slot == place), x[b * BLK : (b + 1) * BLK, :]).astype(BF)
        buf[pl.ds(base, 16), :] += got[:16]
        buf[pl.ds(base + 16, WIDE - 16), :] = got[16:]
        tails.append((b, place, base, off[line, 64:65][0, 0] - base))

    @pl.when(functools.reduce(jnp.maximum, [size for *_, size in tails]) > WIDE)
    def _():
        for b, place, base, size in tails:

            @pl.when(size > WIDE)
            def _():
                more = dot(as_bf(more_slot == place), x[b * BLK : (b + 1) * BLK, :]).astype(BF)
                buf[pl.ds(base + WIDE, BLK + 16 - WIDE), :] += more

    second[0:half, :] = buf[0:half, :]
    second[half:, :] = first[half:, :]


def second_send_call(off, pos, first, x):
    rows, width = x.shape
    half = rows // 8
    return pl.pallas_call(
        second_send_kernel,
        out_shape=jax.ShapeDtypeStruct((half + 16, width), BF),
        in_specs=[spec(pltpu.VMEM)] * 4,
        out_specs=spec(pltpu.VMEM),
        scratch_shapes=[pltpu.VMEM((half + BLK + 16, width), BF)],
        compiler_params=params(),
        cost_estimate=pl.CostEstimate(flops=10**8, bytes_accessed=10**6, transcendentals=0),
        name="second_send",
    )(off, pos, first, x)


def rank_kernel(off, pos, meta, ranks):
    ranks[...] = jnp.zeros_like(ranks)
    cap = 8 * meta.shape[1]
    line = iota((16, BLK), 0)
    slot = iota((BLK + 128, BLK), 0)
    for b in range(pos.shape[0] // 8):
        rank = pos[8 * b + 4 : 8 * b + 5, :]
        value = jnp.where(line == 0, rank >> 8, jnp.where(line == 1, rank & 255, 1))
        value = jnp.where(rank >= 0, value, 0).astype(F32).astype(BF)
        for kind in (0, 1):
            row = slice(8 * b + kind, 8 * b + kind + 1)
            base = pl.multiple_of(jnp.minimum((off[row, 0:1][0, 0] // 128) * 128, cap), 128)
            ranks[:, pl.ds(base, BLK + 128)] += dot_t(value, as_bf(slot == pos[row, :] - base))[:8]
    seen = ranks[2:3, :cap] > 0.5
    rank = (ranks[0:1, :cap] * 256.0 + ranks[1:2, :cap]).astype(I32)
    goal = jnp.where(seen, rank, 1 << 20)
    line = cap // 8
    for k in range(8):
        meta[k : k + 1, :] = goal[:, k * line : (k + 1) * line]


def rank_call(off, pos):
    cap = pos.shape[0] // 8 * BLK // 2
    return pl.pallas_call(
        rank_kernel,
        out_shape=jax.ShapeDtypeStruct((8, cap // 8), I32),
        in_specs=[spec(pltpu.VMEM)] * 2,
        out_specs=spec(pltpu.VMEM),
        scratch_shapes=[pltpu.VMEM((8, cap + BLK + 128), F32)],
        compiler_params=params(),
        cost_estimate=pl.CostEstimate(flops=10**8, bytes_accessed=10**6, transcendentals=0),
        name="list_ranks",
    )(off, pos)


def own_kernel(pos, x, held):
    same = iota((BLK, BLK), 0) == iota((BLK, BLK), 1)
    start = pl.program_id(0) * held.shape[0]
    for sub in range(held.shape[0] // BLK):
        keep = as_bf(same & (pos[8 * sub + 3 : 8 * sub + 4, :] >= 0))
        held[sub * BLK : (sub + 1) * BLK, :] = dot(keep, x[pl.ds(start + sub * BLK, BLK), :]).astype(BF)


def own_call(pos, x):
    rows, width = x.shape
    return pl.pallas_call(
        own_kernel,
        grid=(rows // 1024,),
        out_shape=jax.ShapeDtypeStruct((rows + rows // 2 + rows // 4, width), BF),
        in_specs=[pl.BlockSpec((8 * 1024 // BLK, BLK), lambda b: (b, 0)), spec(pltpu.VMEM)],
        out_specs=pl.BlockSpec((1024, width), lambda b: (b, 0)),
        compiler_params=params(),
        cost_estimate=pl.CostEstimate(flops=10**8, bytes_accessed=10**6, transcendentals=0),
        name="own_slots",
    )(pos, x)


def scores(x, turned):
    score = dot(x, turned)
    lane = iota(score.shape, 1)
    high = score.astype(BF).astype(F32)
    middle = (score - high).astype(BF).astype(F32)
    terms = jnp.where(lane < 4, high, jnp.where(lane < 8, middle, score - high - middle)).astype(BF)
    lane = iota((16, 128), 1)
    return dot_t(as_bf(((lane & 3) == iota((16, 128), 0)) & (lane < 12)), terms)


def margins(score, shift, first, width):
    return (score[first + 1 : first + 2] - score[first : first + 1] - shift) / width


def put_lines(ref, start, values):
    for k in range(values.shape[1] // 128):
        ref[start + k : start + k + 1, :] = values[:, 128 * k : 128 * (k + 1)]


def split(values):
    terms = []
    for value in values:
        high = value.astype(BF).astype(F32)
        middle = (value - high).astype(BF).astype(F32)
        terms += [high, middle, value - high - middle]
    return jnp.concatenate(terms + [jnp.zeros((16 - len(terms), values[0].shape[1]), F32)], axis=0).astype(BF)


def second_kernel(second, relay, first, meta, held_in, held, copy, known, start, bounds, goals):
    del held_in
    half = second.shape[0] - 16
    slots = held.shape[0]
    cap = 2 * slots
    have = count_at(second[half:, :], 5)
    more = count_at(relay[half:, :], 4)
    both = count_at(first[half:, :], 4)
    lane = iota((1, half), 1)
    goal = jnp.where(lane < more, lane + have, -1)
    moved = dot(as_bf(iota((slots, half), 0) == goal), relay[0:half, :]).astype(BF)
    held[0:half, :] = moved[0:half] + second[0:half, :]
    held[half:, :] = moved[half:]
    copy[...] = held[...]
    known[...] = jnp.broadcast_to(jnp.where(iota((8, 1), 0) == 0, have + more, both), known.shape)
    place = jnp.concatenate([meta[k : k + 1, :] for k in range(8)], axis=1)
    lines = cap // SLOTS
    own = iota((1, cap), 1) < both
    edge = SLOTS * iota((lines, cap), 0)
    before = jnp.sum(jnp.where(own | (place < edge), 1.0, 0.0), axis=1, keepdims=True)
    begin = jnp.minimum((before.astype(I32) >> 7) << 7, cap - SLOTS - 128)
    start[...] = jnp.broadcast_to(begin, start.shape)
    edge = 2 * SLOTS * iota((lines // 2, cap), 0)
    before = jnp.sum(jnp.where(own | (place < edge), 1.0, 0.0), axis=1, keepdims=True)
    until = jnp.sum(jnp.where(own | (place < edge + 2 * SLOTS), 1.0, 0.0), axis=1, keepdims=True)
    low = jnp.sum(jnp.where(until <= half, 1.0, 0.0), axis=0, keepdims=True).astype(I32)
    high = jnp.sum(jnp.where(before < 2 * half, 1.0, 0.0), axis=0, keepdims=True).astype(I32)
    bounds[...] = jnp.broadcast_to(jnp.where(iota((8, 1), 0) == 0, low, high), bounds.shape)
    goals[...] = jnp.broadcast_to(jnp.where(own, -1, place), goals.shape)


def second_call(second, relay, first, meta, held):
    half, width = second.shape
    half -= 16
    cap = 4 * half
    slots = cap // 2
    return pl.pallas_call(
        second_kernel,
        grid=(1,),
        out_shape=[
            jax.ShapeDtypeStruct(held.shape, BF),
            jax.ShapeDtypeStruct((slots, width), BF),
            jax.ShapeDtypeStruct((8, 128), I32),
            jax.ShapeDtypeStruct((cap // SLOTS, 128), I32),
            jax.ShapeDtypeStruct((8, 128), I32),
            jax.ShapeDtypeStruct((8, cap), I32),
        ],
        in_specs=[spec(pltpu.VMEM)] * 4 + [spec(pl.ANY)],
        out_specs=[pl.BlockSpec((slots, width), lambda b: (held.shape[0] // slots - 1, 0))] + [spec(pltpu.VMEM)] * 5,
        input_output_aliases={4: 0},
        compiler_params=params(),
        cost_estimate=pl.CostEstimate(flops=10**8, bytes_accessed=10**5, transcendentals=0),
        name="second_slots",
    )(second, relay, first, meta, held)


def centre_kernel(here, total, labels, x, second, first, meta, known, cents, turned, shifts, one, two, again):
    rows, width = x.shape
    part = 1024
    sums, counts = total[0:4, :], total[4:8, :]
    low = (sums[0:1] + sums[1:2]) / (counts[0:1] + counts[1:2])
    high = (sums[2:3] + sums[3:4]) / (counts[2:3] + counts[3:4])
    groups = sums / counts
    cents[0:1, :] = low
    cents[1:2, :] = high
    cents[2:6, :] = groups
    top = here[0] == 1
    left = jnp.where(top, groups[2:3], groups[0:1])
    right = jnp.where(top, groups[3:4], groups[1:2])
    columns = jnp.concatenate([low, high, left, right] * 3 + [jnp.zeros((116, width), F32)], axis=0).T.astype(BF)
    turned[...] = columns
    gaps = []
    for k, (a, b) in enumerate(((low, high), (left, right))):
        gaps.append(0.5 * (jnp.sum(b * b, axis=1, keepdims=True) - jnp.sum(a * a, axis=1, keepdims=True)))
        shifts[k : k + 1, :] = jnp.broadcast_to(gaps[k], (1, 128))
    shifts[2:, :] = jnp.zeros((6, 128), F32)
    one[rows // 128 :, :] = jnp.zeros((rows // 256, 128), F32)
    two[rows // 128 : 3 * rows // 256, :] = jnp.zeros((rows // 256, 128), F32)
    stay = labels[0:1, :] == here[0]
    keep = stay & (labels[1:2, :] == here[1])
    for k in range(rows // part):
        lanes = slice(k * part, (k + 1) * part)
        score = scores(x[lanes, :], columns)
        put_lines(one, k * part // 128, jnp.where(stay[:, lanes], margins(score, gaps[0], 0, width), 0.0))
        put_lines(two, k * part // 128, jnp.where(keep[:, lanes], margins(score, gaps[1], 2, width), 0.0))
    score = scores(second[...], columns)
    live = iota((1, second.shape[0]), 1) < known[0:1, 0:1]
    put_lines(two, 3 * rows // 256, jnp.where(live, margins(score, gaps[1], 2, width), 0.0))
    half = first.shape[0] - 16
    both = iota((1, half), 1) < known[1:2, 0:1]
    score = scores(first[0:half, :], columns)
    value = split([jnp.where(both, margins(score, gaps[0], 0, width), 0.0)])
    goal = jnp.concatenate([meta[k : k + 1, :] for k in range(half // meta.shape[1])], axis=1)
    goal = jnp.where(both, goal, -1)
    for k in range(4 * half // BLK):
        got = dot_t(value, as_bf(iota((BLK, half), 0) + k * BLK == goal))
        put_lines(again, k * BLK // 128, got[0:1] + got[1:2] + got[2:3])


def centre_call(here, total, labels, vectors, second, first, meta, known):
    rows, width = vectors.shape
    cap = rows // 2
    return pl.pallas_call(
        centre_kernel,
        out_shape=[
            jax.ShapeDtypeStruct((6, width), F32),
            jax.ShapeDtypeStruct((width, 128), BF),
            jax.ShapeDtypeStruct((8, 128), F32),
            jax.ShapeDtypeStruct(((rows + cap) // 128, 128), F32),
            jax.ShapeDtypeStruct(((rows + cap + cap // 2) // 128, 128), F32),
            jax.ShapeDtypeStruct((cap // 128, 128), F32),
        ],
        in_specs=[spec(pltpu.SMEM)] + [spec(pltpu.VMEM)] * 7,
        out_specs=[spec(pltpu.VMEM)] * 6,
        compiler_params=params(),
        cost_estimate=pl.CostEstimate(flops=10**8, bytes_accessed=10**5, transcendentals=0),
        name="all_margins",
    )(here, total, labels, vectors, second, first, meta, known)


def column_kernel(own, a, b, c, out):
    sums, counts = unpack(own[...])
    for other in (a, b, c):
        s, n = unpack(other[...])
        sums, counts = sums + s, counts + n
    out[0:4, :] = sums
    width = out.shape[1]
    for g in range(4):
        out[4 + g : 5 + g, :] = jnp.broadcast_to(counts[:, 128 * g : 128 * g + 1], (1, width))


def column_call(*pieces):
    width = pieces[0].shape[1]
    return pl.pallas_call(
        column_kernel,
        grid=(1,),
        out_shape=jax.ShapeDtypeStruct((8, width), F32),
        in_specs=[pl.BlockSpec((16, width), functools.partial(lambda last, b: (last, 0), p.shape[0] // 16 - 1)) for p in pieces],
        out_specs=pl.BlockSpec((8, width), lambda b: (0, 0)),
        compiler_params=params(),
        name="column_sums",
    )(*pieces)


def first_kernel(late, start, bounds, turned, shifts, goals, again, first, *refs):
    (middle, past, *refs) = refs if late else (None, None, *refs)
    hands, refs = refs[:HANDS], refs[HANDS:]
    held_in, one_in, two_in, held, one, two, values, x, out, sent = refs
    del held_in
    width = first.shape[1]
    part = first.shape[0] - 16
    pairs = 4 * part // (2 * SLOTS)

    def weigh(begin):
        lanes = slice(begin, begin + part)
        score = scores(x[lanes, :], turned[...])
        m_one = margins(score, shifts[0:1, 0:1], 0, width)
        values[:, lanes] = split([m_one, margins(score, shifts[1:2, 0:1], 2, width)])

    reach = 2 * SLOTS
    low = part - reach if late else 0
    x[low:part, :] = first[low:part, :]
    x[part : 2 * part, :] = middle[...] if late else jnp.zeros((part, width), BF)
    for h, hand in enumerate(hands):
        for turn in range(reach // 16 // HANDS if late else hand.shape[0] // 16):
            block = 2 * part + 16 * (h + HANDS * turn)
            x[block : block + 16, :] = hand[16 * turn : 16 * turn + 16, :]
    if late:
        one[...] = one_in[...]
        two[...] = two_in[...]
        values[...] = past[...]
        weigh(part)
    else:
        one[...] = jnp.zeros_like(one)
        two[...] = jnp.zeros_like(two)
        values[:, part : 2 * part] = jnp.zeros((16, part), BF)
        for k in (0, 2, 3):
            weigh(k * part)
    span = SLOTS + 128
    base = 8 * part
    slot = iota((SLOTS, span), 0)

    def store(pair):
        lines = pl.multiple_of(pair * 2 * SLOTS, 2 * SLOTS)
        to = held.at[pl.ds(base + lines, 2 * SLOTS)]
        return pltpu.make_async_copy(out.at[pl.ds(lines, 2 * SLOTS)], to, sent.at[pair])

    def place(pair, _):
        for i in range(2):
            lines = pl.multiple_of(pair * 2 * SLOTS + i * SLOTS, SLOTS)
            begin = pl.multiple_of((start[2 * pair + i, 0] // 128) * 128, 128)
            hot = as_bf(slot == goals[0:1, pl.ds(begin, span)] - lines)
            out[pl.ds(lines, SLOTS), :] = dot(hot, x[pl.ds(begin, span), :]).astype(BF)
            got = dot_t(values[:, pl.ds(begin, span)], hot)
            line = pl.ds(2 * pair + i, 1)
            one[line, :] = got[0:1] + got[1:2] + got[2:3] + again[line, :]
            two[line, :] = got[3:4] + got[4:5] + got[5:6]
        store(pair).start()
        return 0

    def finish(pair, _):
        store(pair).wait()
        return 0

    low = jnp.minimum(bounds[0, 0], pairs)
    high = jnp.clip(bounds[1, 0], low, pairs)
    ranges = [(low, high)] if late else [(0, low), (high, pairs)]
    for work in (place, finish):
        for begin, end in ranges:
            lax.fori_loop(begin, end, work, 0)


def first_call(start, bounds, turned, shifts, goals, again, first, added, hands, held, one, two):
    width = held.shape[1]
    cap = goals.shape[1]
    lines = cap // 128
    late = bool(added)
    pieces = [first, *added, *hands]
    block = pl.BlockSpec((lines, 128), lambda k: (2, 0))
    given = 6 + len(pieces)
    kept = jax.ShapeDtypeStruct((16, cap), BF)
    return pl.pallas_call(
        functools.partial(first_kernel, late),
        grid=(1,),
        out_shape=[
            jax.ShapeDtypeStruct(held.shape, BF),
            jax.ShapeDtypeStruct(one.shape, F32),
            jax.ShapeDtypeStruct(two.shape, F32),
        ]
        + ([] if late else [kept]),
        in_specs=[spec(pltpu.SMEM)] * 2
        + [spec(pltpu.VMEM)] * (given - 2)
        + [spec(pl.ANY)]
        + ([block] * 2 if late else [spec(pl.ANY)] * 2),
        out_specs=[spec(pl.ANY), block, block] + ([] if late else [spec(pltpu.VMEM)]),
        scratch_shapes=([pltpu.VMEM((16, cap), BF)] if late else [])
        + [
            pltpu.VMEM((cap, width), BF),
            pltpu.VMEM((cap, width), BF),
            pltpu.SemaphoreType.DMA((cap // (2 * SLOTS),)),
        ],
        input_output_aliases={given: 0, given + 1: 1, given + 2: 2},
        compiler_params=params(),
        cost_estimate=pl.CostEstimate(flops=10**8, bytes_accessed=10**5, transcendentals=0),
        name="last_slots" if late else "first_slots",
    )(start, bounds, turned, shifts, goals, again, *pieces, held, one, two)


def local(vectors, child_labels):
    ways = lax.axis_size("cube")
    top = ways // 2
    nxt = ways // 4
    me = lax.axis_index("cube")
    here = jnp.stack([(me // top) & 1, (me // nxt) & 1]).astype(I32)
    after = lax.optimization_barrier
    pos, off, every, leavers = plan_call(here, child_labels)
    counts = [leavers] + [swap(leavers, bits) for bits in (nxt, top, top | nxt)]
    first, middle, rest = sort_call(here, child_labels, pos, off, every, vectors)
    first, *counts = after((first, *counts))
    first_in = swap(first, top)
    second = second_send_call(off, pos, first, vectors)
    second_in = swap(second, nxt)
    rest, second = after((rest, second))
    own, *hands = deal_call(rest, *counts)
    hands = [own] + [swap(hand, h + 1) for h, hand in enumerate(hands)]
    after_deal, hands[1] = after((pos, hands[1]))
    meta = rank_call(off, after_deal)
    held = own_call(after_deal, vectors)
    limit = rest.shape[0]
    step = limit // 32
    held, meta, hands[7] = after((held, meta, hands[7]))
    packed, longest, begins = pack_call(step, hands)
    bit = HANDS
    while bit < nxt:
        longest = jnp.maximum(longest, swap(longest, bit))
        bit *= 2

    def cross(size):
        def branch(rows, first_in, meta):
            got = jnp.pad(swap(rows[:size], top), ((0, limit - size), (0, 0))) if size else jnp.zeros_like(rows)
            return got, swap(first_in, nxt), swap(meta, top)

        return branch

    sizes = range(0, limit + 1, step)
    packed, first_in = after((packed, first_in))
    packed_in, relay, meta_in = lax.switch(longest[0, 0], [cross(size) for size in sizes], packed, first_in, meta)
    middle, packed_in = after((middle, packed_in))
    middle_in = swap(middle, top)
    own, *hands = part_call(begins, packed_in)
    held, copy, known, start, bounds, goals = second_call(second_in, relay, first_in, meta_in, held)
    own, second_in, relay = after((own, second_in, relay))
    total = column_call(first, second_in, first_in, relay)
    sent = [None] * (HANDS - 1)
    bit = 1
    while bit < nxt:
        if bit < HANDS:
            ready = range(bit - 1, 2 * bit - 1)
            total, *late = after((total + swap(total, bit), *[hands[h] for h in ready]))
            for h, hand in zip(ready, late):
                sent[h] = swap(hand, h + 1)
        else:
            total = total + swap(total, bit)
        bit *= 2
    hands = [own, *sent]
    cents, turned, shifts, one, two, again = centre_call(
        here, total, child_labels, vectors, copy, first_in, meta_in, known
    )
    told = start, bounds, turned, shifts, goals, again, first_in
    held, one, two, values = first_call(*told, (), hands, held, one, two)
    held, one, two = first_call(*told, (middle_in, values), hands, held, one, two)
    return held, one.reshape(-1), two.reshape(-1), cents


def solution(mesh):
    return jax.shard_map(
        local,
        mesh=mesh,
        in_specs=(P("cube", None), P(None, "cube")),
        out_specs=(P("cube", None), P("cube"), P("cube"), P()),
        check_vma=False,
    )
```

```python
import functools
import jax
import jax.numpy as jnp
from jax import lax
from jax.experimental import pallas as pl
from jax.experimental.pallas import tpu as pltpu
from jax.sharding import PartitionSpec as P

BF = jnp.bfloat16
F32 = jnp.float32
I32 = jnp.int32
BLK = 256
HANDS = 8
WIDE = BLK // 2 + 16
SLOTS = 128
VMEM_BYTES = 28 * 1024 * 1024


def swap(x, bits):
    return lax.ppermute(x, "cube", [(i, i ^ bits) for i in range(lax.axis_size("cube"))])


def dot(a, b):
    return lax.dot_general(a, b, (((1,), (0,)), ((), ())), preferred_element_type=F32)


def dot_t(a, b):
    return lax.dot_general(a, b, (((1,), (1,)), ((), ())), preferred_element_type=F32)


def iota(shape, dim):
    return lax.broadcasted_iota(I32, shape, dim)


def as_bf(mask):
    return jnp.where(mask, jnp.float32(1), jnp.float32(0)).astype(BF)


def pack(sums, counts, width):
    high = sums.astype(BF).astype(F32)
    middle = (sums - high).astype(BF).astype(F32)
    low = sums - high - middle
    spare = width - 128 * len(counts)
    counts = jnp.concatenate(counts + ([jnp.zeros((1, spare), I32)] if spare else []), axis=1)
    upper, lower = (counts >> 8).astype(F32), (counts & 255).astype(F32)
    return jnp.concatenate([high, middle, low, upper, lower, jnp.zeros((2, width), F32)], axis=0).astype(BF)


def unpack(extra):
    extra = extra.astype(F32)
    sums = extra[0:4] + extra[4:8] + extra[8:12]
    return sums, extra[12:13] * 256.0 + extra[13:14]


def count_at(extra, k):
    extra = extra[12:14, 128 * k : 128 * k + 1].astype(F32)
    return (extra[0:1] * 256.0 + extra[1:2]).astype(I32)


def spec(memory):
    return pl.BlockSpec(memory_space=memory)


def params():
    return pltpu.CompilerParams(vmem_limit_bytes=VMEM_BYTES)


def plan_kernel(here, labels, pos, off_ref, every, leavers):
    rows = labels.shape[1]
    blocks = rows // BLK
    leave = labels[0:1, :] != here[0]
    miss = labels[1:2, :] != here[1]
    code = jnp.where(leave, jnp.where(miss, 0, 1), jnp.where(miss, 2, 3))
    code = jnp.concatenate(
        [jnp.broadcast_to(code[:, b * BLK : (b + 1) * BLK], (8, BLK)) for b in range(blocks)], axis=0
    )
    tall = 8 * blocks
    kind = iota((tall, BLK), 0) & 7
    mask = (code == kind) | ((kind == 4) & (code <= 1))
    maskb = as_bf(mask)
    upper = as_bf(iota((BLK, BLK), 0) <= iota((BLK, BLK), 1))
    before = dot(maskb, upper)
    total = dot(maskb, jnp.ones((BLK, BLK), BF)).astype(BF)
    r, c = iota((tall, tall), 0), iota((tall, tall), 1)
    same = ((r ^ c) & 7) == 0
    earlier = as_bf((same & (c < r)) | (((r & 7) == 1) & ((c & 7) == 0)))
    off = dot(earlier, total)
    pos[...] = jnp.where(mask, (before + off).astype(I32) - 1, -1)
    off_ref[...] = (off + jnp.where(iota((tall, BLK), 1) < 64, 0.0, total.astype(F32)))[:, :128].astype(I32)
    r8, c8 = iota((8, tall), 0), iota((8, tall), 1)
    count = dot(as_bf(r8 == (c8 & 7)), total)[:, :128].astype(I32)
    every[...] = count
    leavers[...] = jnp.broadcast_to(count[4:5], leavers.shape)


def plan_call(here, labels):
    rows = labels.shape[1]
    tall = 8 * rows // BLK
    return pl.pallas_call(
        plan_kernel,
        out_shape=[
            jax.ShapeDtypeStruct((tall, BLK), I32),
            jax.ShapeDtypeStruct((tall, 128), I32),
            jax.ShapeDtypeStruct((8, 128), I32),
            jax.ShapeDtypeStruct((8, 128), I32),
        ],
        in_specs=[spec(pltpu.SMEM), spec(pltpu.VMEM)],
        out_specs=[spec(pltpu.VMEM)] * 4,
        compiler_params=params(),
        cost_estimate=pl.CostEstimate(flops=2 * 10**10, bytes_accessed=10**7, transcendentals=0),
        name="plan_places",
    )(here, labels)


def sort_kernel(here, labels, pos_ref, off_ref, every, x, first, middle, rest, buf, sums):
    rows = labels.shape[1]
    blocks = rows // BLK
    cap = rows // 2
    buf[...] = jnp.zeros_like(buf)
    group = 2 * labels[0:1, :] + labels[1:2, :]
    slot = iota((WIDE, BLK), 0)
    more_slot = iota((BLK + 16 - WIDE, BLK), 0) + WIDE
    sums[...] = jnp.zeros_like(sums)
    tails = []
    for b in range(blocks):
        vectors = x.at[pl.ds(b * BLK, BLK)]
        hot = [as_bf((iota((16, BLK), 0) & 3) == group[:, b * BLK : (b + 1) * BLK])]
        bases = []
        ends = []
        places = []
        for kind in (0, 1):
            line = slice(8 * b + kind, 8 * b + kind + 1)
            base = pl.multiple_of(jnp.minimum((off_ref[line, 0:1][0, 0] // 16) * 16, cap), 16)
            bases.append(base)
            ends.append(off_ref[line, 64:65][0, 0])
            places.append(pos_ref[line, :] - base)
            hot.append(as_bf(slot == places[kind]))
        got = dot(jnp.concatenate(hot, axis=0), vectors[...])
        sums[...] += got[0:8]
        got = got[16:].astype(BF)
        buf[pl.ds(bases[0], WIDE), :] += got[:WIDE]
        buf[pl.ds(bases[1], 16), :] += got[WIDE : WIDE + 16]
        buf[pl.ds(bases[1] + 16, WIDE - 16), :] = got[WIDE + 16 :]
        for kind in (0, 1):
            tails.append((b, places[kind], bases[kind], ends[kind] - bases[kind]))

    @pl.when(functools.reduce(jnp.maximum, [size for *_, size in tails]) > WIDE)
    def _():
        for b, place, base, size in tails:

            @pl.when(size > WIDE)
            def _():
                more = dot(as_bf(more_slot == place), x[b * BLK : (b + 1) * BLK, :]).astype(BF)
                buf[pl.ds(base + WIDE, BLK + 16 - WIDE), :] += more

    one, two = here[0], here[1]
    kinds = [every[k : k + 1] for k in range(4)]
    counts = []
    for g in range(4):
        away, miss = jnp.int32(g >> 1) != one, jnp.int32(g & 1) != two
        counts.append(jnp.where(away, jnp.where(miss, kinds[0], kinds[1]), jnp.where(miss, kinds[2], kinds[3])))
    part = cap // 4
    first[0:part, :] = buf[0:part, :]
    first[part:, :] = pack(sums[0:4, :], counts + [kinds[0], kinds[2]], x.shape[1])
    middle[...] = buf[part : 2 * part, :]
    rest[...] = buf[2 * part : cap, :]


def sort_call(here, labels, pos, off, every, vectors):
    rows, width = vectors.shape
    part = rows // 8
    return pl.pallas_call(
        sort_kernel,
        out_shape=[
            jax.ShapeDtypeStruct((part + 16, width), BF),
            jax.ShapeDtypeStruct((part, width), BF),
            jax.ShapeDtypeStruct((2 * part, width), BF),
        ],
        in_specs=[spec(pltpu.SMEM)] + [spec(pltpu.VMEM)] * 5,
        out_specs=[spec(pltpu.VMEM)] * 3,
        scratch_shapes=[pltpu.VMEM((rows // 2 + BLK + 16, width), BF), pltpu.VMEM((8, width), F32)],
        compiler_params=params(),
        cost_estimate=pl.CostEstimate(flops=8 * 10**9, bytes_accessed=10 * 10**6, transcendentals=0),
        name="sort_leavers",
    )(here, labels, pos, off, every, vectors)


def deal_kernel(rest, own, near, top, far, *hands):
    rows, width = rest.shape
    turns = rows // 16 // HANDS
    counts = jnp.concatenate([ref[0:1, :] for ref in (own, near, top, far)], axis=1)
    counts = jnp.concatenate([counts, jnp.zeros((1, width - 512), I32)], axis=1)
    upper, lower = (counts >> 8).astype(F32), (counts & 255).astype(F32)
    tail = jnp.concatenate([upper, lower, jnp.zeros((14, width), F32)], axis=0).astype(BF)
    for h, hand in enumerate(hands):
        for turn in range(turns):
            block = 16 * (h + HANDS * turn)
            hand[16 * turn : 16 * turn + 16, :] = rest[block : block + 16, :]
        hand[16 * turns :, :] = tail


def deal_call(rest, *counts):
    rows, width = rest.shape
    turns = rows // 16 // HANDS
    return pl.pallas_call(
        deal_kernel,
        out_shape=[jax.ShapeDtypeStruct((16 * turns + 16, width), BF)] * HANDS,
        in_specs=[spec(pltpu.VMEM)] * 5,
        out_specs=[spec(pltpu.VMEM)] * HANDS,
        compiler_params=params(),
        cost_estimate=pl.CostEstimate(flops=0, bytes_accessed=10**5, transcendentals=0),
        name="deal_rest",
    )(rest, *counts)


def pack_kernel(step, *refs):
    hands, (out, longest, begins) = refs[:HANDS], refs[HANDS:]
    rows = hands[0].shape[0] - 16
    out[...] = jnp.zeros_like(out)
    full = []
    for hand in hands:
        count = hand[rows : rows + 2, 0:512].astype(F32)
        count = (count[0:1] * 256.0 + count[1:2]).astype(I32)
        full.append((jnp.maximum(count - rows * HANDS, 0) + 15) >> 4)
    place = jnp.zeros((1, 512), I32)
    for h, hand in enumerate(hands):
        base = pl.multiple_of(place[0, 0] * 16, 16)
        out[pl.ds(base, rows), :] = hand[0:rows, :]
        begins[h : h + 1, :] = place[:, 256:384] * 16
        place = jnp.minimum(place + ((full[h] + (HANDS - 1 - h)) >> 3), (h + 1) * (rows // 16))
    most = jnp.zeros((1, 512), I32)
    for other in range(HANDS):
        size = jnp.zeros((1, 512), I32)
        for h in range(HANDS):
            size = size + ((full[other ^ h] + (HANDS - 1 - h)) >> 3)
        most = jnp.maximum(most, size)
    most = jnp.max(most.astype(F32), axis=1, keepdims=True).astype(I32)
    per = step // 16
    longest[...] = jnp.broadcast_to(jnp.minimum(most + per - 1, out.shape[0] // 16) // per, longest.shape)


def pack_call(step, hands):
    rows, width = hands[0].shape
    rows -= 16
    return pl.pallas_call(
        functools.partial(pack_kernel, step),
        out_shape=[
            jax.ShapeDtypeStruct((rows * HANDS, width), BF),
            jax.ShapeDtypeStruct((8, 128), I32),
            jax.ShapeDtypeStruct((8, 128), I32),
        ],
        in_specs=[spec(pltpu.VMEM)] * HANDS,
        out_specs=[spec(pltpu.VMEM)] * 3,
        compiler_params=params(),
        cost_estimate=pl.CostEstimate(flops=0, bytes_accessed=10**5, transcendentals=0),
        name="pack_hands",
    )(*hands)


def part_kernel(begins, pack_in, *refs):
    hands, sem = refs[:HANDS], refs[HANDS]
    rows = hands[0].shape[0]
    copies = []
    for h, hand in enumerate(hands):
        base = pl.multiple_of((begins[h, 0] // 16) * 16, 16)
        copies.append(pltpu.make_async_copy(pack_in.at[pl.ds(base, rows)], hand, sem.at[h]))
    for copy in copies:
        copy.start()
    for copy in copies:
        copy.wait()


def part_call(begins, pack_in):
    rows, width = pack_in.shape
    return pl.pallas_call(
        part_kernel,
        out_shape=[jax.ShapeDtypeStruct((rows // HANDS, width), BF)] * HANDS,
        in_specs=[spec(pltpu.SMEM), spec(pl.ANY)],
        out_specs=[spec(pl.ANY)] * HANDS,
        scratch_shapes=[pltpu.SemaphoreType.DMA((HANDS,))],
        compiler_params=params(),
        cost_estimate=pl.CostEstimate(flops=2 * 10**10, bytes_accessed=3 * 10**6, transcendentals=0),
        name="part_pack",
    )(begins, pack_in)


def second_send_kernel(off, pos, first, x, second, buf):
    half = second.shape[0] - 16
    buf[...] = jnp.zeros_like(buf)
    slot = iota((WIDE, BLK), 0)
    more_slot = iota((BLK + 16 - WIDE, BLK), 0) + WIDE
    tails = []
    for b in range(x.shape[0] // BLK):
        line = slice(8 * b + 2, 8 * b + 3)
        base = pl.multiple_of(jnp.minimum((off[line, 0:1][0, 0] // 16) * 16, half), 16)
        place = pos[line, :] - base
        got = dot(as_bf(slot == place), x[b * BLK : (b + 1) * BLK, :]).astype(BF)
        buf[pl.ds(base, 16), :] += got[:16]
        buf[pl.ds(base + 16, WIDE - 16), :] = got[16:]
        tails.append((b, place, base, off[line, 64:65][0, 0] - base))

    @pl.when(functools.reduce(jnp.maximum, [size for *_, size in tails]) > WIDE)
    def _():
        for b, place, base, size in tails:

            @pl.when(size > WIDE)
            def _():
                more = dot(as_bf(more_slot == place), x[b * BLK : (b + 1) * BLK, :]).astype(BF)
                buf[pl.ds(base + WIDE, BLK + 16 - WIDE), :] += more

    second[0:half, :] = buf[0:half, :]
    second[half:, :] = first[half:, :]


def second_send_call(off, pos, first, x):
    rows, width = x.shape
    half = rows // 8
    return pl.pallas_call(
        second_send_kernel,
        out_shape=jax.ShapeDtypeStruct((half + 16, width), BF),
        in_specs=[spec(pltpu.VMEM)] * 4,
        out_specs=spec(pltpu.VMEM),
        scratch_shapes=[pltpu.VMEM((half + BLK + 16, width), BF)],
        compiler_params=params(),
        cost_estimate=pl.CostEstimate(flops=10**8, bytes_accessed=10**6, transcendentals=0),
        name="second_send",
    )(off, pos, first, x)


def rank_kernel(off, pos, meta, ranks):
    ranks[...] = jnp.zeros_like(ranks)
    cap = 8 * meta.shape[1]
    line = iota((16, BLK), 0)
    slot = iota((BLK + 128, BLK), 0)
    for b in range(pos.shape[0] // 8):
        rank = pos[8 * b + 4 : 8 * b + 5, :]
        value = jnp.where(line == 0, rank >> 8, jnp.where(line == 1, rank & 255, 1))
        value = jnp.where(rank >= 0, value, 0).astype(F32).astype(BF)
        for kind in (0, 1):
            row = slice(8 * b + kind, 8 * b + kind + 1)
            base = pl.multiple_of(jnp.minimum((off[row, 0:1][0, 0] // 128) * 128, cap), 128)
            ranks[:, pl.ds(base, BLK + 128)] += dot_t(value, as_bf(slot == pos[row, :] - base))[:8]
    seen = ranks[2:3, :cap] > 0.5
    rank = (ranks[0:1, :cap] * 256.0 + ranks[1:2, :cap]).astype(I32)
    goal = jnp.where(seen, rank, 1 << 20)
    line = cap // 8
    for k in range(8):
        meta[k : k + 1, :] = goal[:, k * line : (k + 1) * line]


def rank_call(off, pos):
    cap = pos.shape[0] // 8 * BLK // 2
    return pl.pallas_call(
        rank_kernel,
        out_shape=jax.ShapeDtypeStruct((8, cap // 8), I32),
        in_specs=[spec(pltpu.VMEM)] * 2,
        out_specs=spec(pltpu.VMEM),
        scratch_shapes=[pltpu.VMEM((8, cap + BLK + 128), F32)],
        compiler_params=params(),
        cost_estimate=pl.CostEstimate(flops=10**8, bytes_accessed=10**6, transcendentals=0),
        name="list_ranks",
    )(off, pos)


def own_kernel(pos, x, held):
    same = iota((BLK, BLK), 0) == iota((BLK, BLK), 1)
    start = pl.program_id(0) * held.shape[0]
    for sub in range(held.shape[0] // BLK):
        keep = as_bf(same & (pos[8 * sub + 3 : 8 * sub + 4, :] >= 0))
        held[sub * BLK : (sub + 1) * BLK, :] = dot(keep, x[pl.ds(start + sub * BLK, BLK), :]).astype(BF)


def own_call(pos, x):
    rows, width = x.shape
    return pl.pallas_call(
        own_kernel,
        grid=(rows // 1024,),
        out_shape=jax.ShapeDtypeStruct((rows + rows // 2 + rows // 4, width), BF),
        in_specs=[pl.BlockSpec((8 * 1024 // BLK, BLK), lambda b: (b, 0)), spec(pltpu.VMEM)],
        out_specs=pl.BlockSpec((1024, width), lambda b: (b, 0)),
        compiler_params=params(),
        cost_estimate=pl.CostEstimate(flops=10**8, bytes_accessed=10**6, transcendentals=0),
        name="own_slots",
    )(pos, x)


def scores(x, turned):
    score = dot(x, turned)
    lane = iota(score.shape, 1)
    high = score.astype(BF).astype(F32)
    middle = (score - high).astype(BF).astype(F32)
    terms = jnp.where(lane < 4, high, jnp.where(lane < 8, middle, score - high - middle)).astype(BF)
    lane = iota((16, 128), 1)
    return dot_t(as_bf(((lane & 3) == iota((16, 128), 0)) & (lane < 12)), terms)


def margins(score, shift, first, width):
    return (score[first + 1 : first + 2] - score[first : first + 1] - shift) / width


def put_lines(ref, start, values):
    for k in range(values.shape[1] // 128):
        ref[start + k : start + k + 1, :] = values[:, 128 * k : 128 * (k + 1)]


def split(values):
    terms = []
    for value in values:
        high = value.astype(BF).astype(F32)
        middle = (value - high).astype(BF).astype(F32)
        terms += [high, middle, value - high - middle]
    return jnp.concatenate(terms + [jnp.zeros((16 - len(terms), values[0].shape[1]), F32)], axis=0).astype(BF)


def second_kernel(second, relay, first, meta, held_in, held, copy, known, start, twice, bounds, goals):
    del held_in
    half = second.shape[0] - 16
    slots = held.shape[0]
    cap = 2 * slots
    have = count_at(second[half:, :], 5)
    more = count_at(relay[half:, :], 4)
    both = count_at(first[half:, :], 4)
    lane = iota((1, half), 1)
    goal = jnp.where(lane < more, lane + have, -1)
    moved = dot(as_bf(iota((slots, half), 0) == goal), relay[0:half, :]).astype(BF)
    held[0:half, :] = moved[0:half] + second[0:half, :]
    held[half:, :] = moved[half:]
    copy[...] = held[...]
    known[...] = jnp.broadcast_to(jnp.where(iota((8, 1), 0) == 0, have + more, both), known.shape)
    place = jnp.concatenate([meta[k : k + 1, :] for k in range(8)], axis=1)
    lines = cap // SLOTS
    own = iota((1, cap), 1) < both
    edge = SLOTS * iota((lines, cap), 0)
    before = jnp.sum(jnp.where(own | (place < edge), 1.0, 0.0), axis=1, keepdims=True)
    begin = jnp.minimum((before.astype(I32) >> 7) << 7, cap - SLOTS - 128)
    start[...] = jnp.broadcast_to(begin, start.shape)
    before = jnp.sum(jnp.where(own & (place < edge), 1.0, 0.0), axis=1, keepdims=True)
    begin = jnp.minimum((before.astype(I32) >> 7) << 7, half - SLOTS - 128)
    twice[...] = jnp.broadcast_to(begin, twice.shape)
    edge = 2 * SLOTS * iota((lines // 2, cap), 0)
    before = jnp.sum(jnp.where(own | (place < edge), 1.0, 0.0), axis=1, keepdims=True)
    until = jnp.sum(jnp.where(own | (place < edge + 2 * SLOTS), 1.0, 0.0), axis=1, keepdims=True)
    low = jnp.sum(jnp.where(until <= half, 1.0, 0.0), axis=0, keepdims=True).astype(I32)
    high = jnp.sum(jnp.where(before < 2 * half, 1.0, 0.0), axis=0, keepdims=True).astype(I32)
    bounds[...] = jnp.broadcast_to(jnp.where(iota((8, 1), 0) == 0, low, high), bounds.shape)
    goals[...] = jnp.broadcast_to(jnp.where(own, -1, place), goals.shape)


def second_call(second, relay, first, meta, held):
    half, width = second.shape
    half -= 16
    cap = 4 * half
    slots = cap // 2
    return pl.pallas_call(
        second_kernel,
        grid=(1,),
        out_shape=[
            jax.ShapeDtypeStruct(held.shape, BF),
            jax.ShapeDtypeStruct((slots, width), BF),
            jax.ShapeDtypeStruct((8, 128), I32),
            jax.ShapeDtypeStruct((cap // SLOTS, 128), I32),
            jax.ShapeDtypeStruct((cap // SLOTS, 128), I32),
            jax.ShapeDtypeStruct((8, 128), I32),
            jax.ShapeDtypeStruct((8, cap), I32),
        ],
        in_specs=[spec(pltpu.VMEM)] * 4 + [spec(pl.ANY)],
        out_specs=[pl.BlockSpec((slots, width), lambda b: (held.shape[0] // slots - 1, 0))] + [spec(pltpu.VMEM)] * 6,
        input_output_aliases={4: 0},
        compiler_params=params(),
        cost_estimate=pl.CostEstimate(flops=10**8, bytes_accessed=10**5, transcendentals=0),
        name="second_slots",
    )(second, relay, first, meta, held)


def centre_kernel(here, twice, total, labels, x, second, first, meta, known, cents, turned, shifts, one, two, again, value, goal):
    rows, width = x.shape
    part = 1024
    sums, counts = total[0:4, :], total[4:8, :]
    low = (sums[0:1] + sums[1:2]) / (counts[0:1] + counts[1:2])
    high = (sums[2:3] + sums[3:4]) / (counts[2:3] + counts[3:4])
    groups = sums / counts
    cents[0:1, :] = low
    cents[1:2, :] = high
    cents[2:6, :] = groups
    top = here[0] == 1
    left = jnp.where(top, groups[2:3], groups[0:1])
    right = jnp.where(top, groups[3:4], groups[1:2])
    columns = jnp.concatenate([low, high, left, right] * 3 + [jnp.zeros((116, width), F32)], axis=0).T.astype(BF)
    turned[...] = columns
    gaps = []
    for k, (a, b) in enumerate(((low, high), (left, right))):
        gaps.append(0.5 * (jnp.sum(b * b, axis=1, keepdims=True) - jnp.sum(a * a, axis=1, keepdims=True)))
        shifts[k : k + 1, :] = jnp.broadcast_to(gaps[k], (1, 128))
    shifts[2:, :] = jnp.zeros((6, 128), F32)
    one[rows // 128 :, :] = jnp.zeros((rows // 256, 128), F32)
    two[rows // 128 : 3 * rows // 256, :] = jnp.zeros((rows // 256, 128), F32)
    stay = labels[0:1, :] == here[0]
    keep = stay & (labels[1:2, :] == here[1])
    for k in range(rows // part):
        lanes = slice(k * part, (k + 1) * part)
        score = scores(x[lanes, :], columns)
        put_lines(one, k * part // 128, jnp.where(stay[:, lanes], margins(score, gaps[0], 0, width), 0.0))
        put_lines(two, k * part // 128, jnp.where(keep[:, lanes], margins(score, gaps[1], 2, width), 0.0))
    score = scores(second[...], columns)
    live = iota((1, second.shape[0]), 1) < known[0:1, 0:1]
    put_lines(two, 3 * rows // 256, jnp.where(live, margins(score, gaps[1], 2, width), 0.0))
    half = first.shape[0] - 16
    both = iota((1, half), 1) < known[1:2, 0:1]
    score = scores(first[0:half, :], columns)
    value[...] = split([jnp.where(both, margins(score, gaps[0], 0, width), 0.0)])
    place = jnp.concatenate([meta[k : k + 1, :] for k in range(half // meta.shape[1])], axis=1)
    goal[...] = jnp.broadcast_to(jnp.where(both, place, -1), goal.shape)
    span = SLOTS + 128
    for k in range(4 * half // SLOTS):
        lanes = pl.ds(pl.multiple_of((twice[k, 0] // 128) * 128, 128), span)
        got = dot_t(value[:, lanes], as_bf(iota((SLOTS, span), 0) + k * SLOTS == goal[0:1, lanes]))
        put_lines(again, k * SLOTS // 128, got[0:1] + got[1:2] + got[2:3])


def centre_call(here, twice, total, labels, vectors, second, first, meta, known):
    rows, width = vectors.shape
    cap = rows // 2
    return pl.pallas_call(
        centre_kernel,
        out_shape=[
            jax.ShapeDtypeStruct((6, width), F32),
            jax.ShapeDtypeStruct((width, 128), BF),
            jax.ShapeDtypeStruct((8, 128), F32),
            jax.ShapeDtypeStruct(((rows + cap) // 128, 128), F32),
            jax.ShapeDtypeStruct(((rows + cap + cap // 2) // 128, 128), F32),
            jax.ShapeDtypeStruct((cap // 128, 128), F32),
        ],
        in_specs=[spec(pltpu.SMEM)] * 2 + [spec(pltpu.VMEM)] * 7,
        out_specs=[spec(pltpu.VMEM)] * 6,
        scratch_shapes=[pltpu.VMEM((16, cap // 4), BF), pltpu.VMEM((8, cap // 4), I32)],
        compiler_params=params(),
        cost_estimate=pl.CostEstimate(flops=10**8, bytes_accessed=10**5, transcendentals=0),
        name="all_margins",
    )(here, twice, total, labels, vectors, second, first, meta, known)


def column_kernel(own, a, b, c, out):
    sums, counts = unpack(own[...])
    for other in (a, b, c):
        s, n = unpack(other[...])
        sums, counts = sums + s, counts + n
    out[0:4, :] = sums
    width = out.shape[1]
    for g in range(4):
        out[4 + g : 5 + g, :] = jnp.broadcast_to(counts[:, 128 * g : 128 * g + 1], (1, width))


def column_call(*pieces):
    width = pieces[0].shape[1]
    return pl.pallas_call(
        column_kernel,
        grid=(1,),
        out_shape=jax.ShapeDtypeStruct((8, width), F32),
        in_specs=[pl.BlockSpec((16, width), functools.partial(lambda last, b: (last, 0), p.shape[0] // 16 - 1)) for p in pieces],
        out_specs=pl.BlockSpec((8, width), lambda b: (0, 0)),
        compiler_params=params(),
        name="column_sums",
    )(*pieces)


def first_kernel(late, start, bounds, turned, shifts, goals, again, first, *refs):
    (middle, past, *refs) = refs if late else (None, None, *refs)
    hands, refs = refs[:HANDS], refs[HANDS:]
    held_in, one_in, two_in, held, one, two, values, x, out, sent = refs
    del held_in
    width = first.shape[1]
    part = first.shape[0] - 16
    pairs = 4 * part // (2 * SLOTS)

    def weigh(begin):
        lanes = slice(begin, begin + part)
        score = scores(x[lanes, :], turned[...])
        m_one = margins(score, shifts[0:1, 0:1], 0, width)
        values[:, lanes] = split([m_one, margins(score, shifts[1:2, 0:1], 2, width)])

    reach = 2 * SLOTS
    low = part - reach if late else 0
    x[low:part, :] = first[low:part, :]
    x[part : 2 * part, :] = middle[...] if late else jnp.zeros((part, width), BF)
    for h, hand in enumerate(hands):
        for turn in range(reach // 16 // HANDS if late else hand.shape[0] // 16):
            block = 2 * part + 16 * (h + HANDS * turn)
            x[block : block + 16, :] = hand[16 * turn : 16 * turn + 16, :]
    if late:
        one[...] = one_in[...]
        two[...] = two_in[...]
        values[...] = past[...]
        weigh(part)
    else:
        one[...] = jnp.zeros_like(one)
        two[...] = jnp.zeros_like(two)
        values[:, part : 2 * part] = jnp.zeros((16, part), BF)
        for k in (0, 2, 3):
            weigh(k * part)
    span = SLOTS + 128
    base = 8 * part
    slot = iota((SLOTS, span), 0)

    def store(pair):
        lines = pl.multiple_of(pair * 2 * SLOTS, 2 * SLOTS)
        to = held.at[pl.ds(base + lines, 2 * SLOTS)]
        return pltpu.make_async_copy(out.at[pl.ds(lines, 2 * SLOTS)], to, sent.at[pair])

    def place_block(k):
        lines = pl.multiple_of(k * SLOTS, SLOTS)
        begin = pl.multiple_of((start[k, 0] // 128) * 128, 128)
        hot = as_bf(slot == goals[0:1, pl.ds(begin, span)] - lines)
        out[pl.ds(lines, SLOTS), :] = dot(hot, x[pl.ds(begin, span), :]).astype(BF)
        got = dot_t(values[:, pl.ds(begin, span)], hot)
        line = pl.ds(k, 1)
        one[line, :] = got[0:1] + got[1:2] + got[2:3] + again[line, :]
        two[line, :] = got[3:4] + got[4:5] + got[5:6]

    def place(pair, _):
        for i in range(2):
            place_block(2 * pair + i)
        store(pair).start()
        return 0

    def place_two(step, first_pair):
        for i in range(4):
            place_block(2 * (first_pair + 2 * step) + i)
        for i in range(2):
            store(first_pair + 2 * step + i).start()
        return first_pair

    def finish(pair, _):
        store(pair).wait()
        return 0

    low = jnp.minimum(bounds[0, 0], pairs)
    high = jnp.clip(bounds[1, 0], low, pairs)
    ranges = [(low, high)] if late else [(0, low), (high, pairs)]
    for begin, end in ranges:
        twos = (end - begin) // 2
        lax.fori_loop(0, twos, place_two, begin)
        lax.fori_loop(begin + 2 * twos, end, place, 0)
    for begin, end in ranges:
        lax.fori_loop(begin, end, finish, 0)


def first_call(start, bounds, turned, shifts, goals, again, first, added, hands, held, one, two):
    width = held.shape[1]
    cap = goals.shape[1]
    lines = cap // 128
    late = bool(added)
    pieces = [first, *added, *hands]
    block = pl.BlockSpec((lines, 128), lambda k: (2, 0))
    given = 6 + len(pieces)
    kept = jax.ShapeDtypeStruct((16, cap), BF)
    return pl.pallas_call(
        functools.partial(first_kernel, late),
        grid=(1,),
        out_shape=[
            jax.ShapeDtypeStruct(held.shape, BF),
            jax.ShapeDtypeStruct(one.shape, F32),
            jax.ShapeDtypeStruct(two.shape, F32),
        ]
        + ([] if late else [kept]),
        in_specs=[spec(pltpu.SMEM)] * 2
        + [spec(pltpu.VMEM)] * (given - 2)
        + [spec(pl.ANY)]
        + ([block] * 2 if late else [spec(pl.ANY)] * 2),
        out_specs=[spec(pl.ANY), block, block] + ([] if late else [spec(pltpu.VMEM)]),
        scratch_shapes=([pltpu.VMEM((16, cap), BF)] if late else [])
        + [
            pltpu.VMEM((cap, width), BF),
            pltpu.VMEM((cap, width), BF),
            pltpu.SemaphoreType.DMA((cap // (2 * SLOTS),)),
        ],
        input_output_aliases={given: 0, given + 1: 1, given + 2: 2},
        compiler_params=params(),
        cost_estimate=pl.CostEstimate(flops=10**8, bytes_accessed=10**5, transcendentals=0),
        name="last_slots" if late else "first_slots",
    )(start, bounds, turned, shifts, goals, again, *pieces, held, one, two)


def local(vectors, child_labels):
    ways = lax.axis_size("cube")
    top = ways // 2
    nxt = ways // 4
    me = lax.axis_index("cube")
    here = jnp.stack([(me // top) & 1, (me // nxt) & 1]).astype(I32)
    after = lax.optimization_barrier
    pos, off, every, leavers = plan_call(here, child_labels)
    counts = [leavers] + [swap(leavers, bits) for bits in (nxt, top, top | nxt)]
    first, middle, rest = sort_call(here, child_labels, pos, off, every, vectors)
    first, *counts = after((first, *counts))
    first_in = swap(first, top)
    second = second_send_call(off, pos, first, vectors)
    second_in = swap(second, nxt)
    rest, second = after((rest, second))
    own, *hands = deal_call(rest, *counts)
    hands = [own] + [swap(hand, h + 1) for h, hand in enumerate(hands)]
    after_deal, hands[1] = after((pos, hands[1]))
    meta = rank_call(off, after_deal)
    held = own_call(after_deal, vectors)
    limit = rest.shape[0]
    step = limit // 32
    held, meta, hands[7] = after((held, meta, hands[7]))
    packed, longest, begins = pack_call(step, hands)
    bit = HANDS
    while bit < nxt:
        longest = jnp.maximum(longest, swap(longest, bit))
        bit *= 2

    def cross(size):
        def branch(rows, first_in, meta):
            got = jnp.pad(swap(rows[:size], top), ((0, limit - size), (0, 0))) if size else jnp.zeros_like(rows)
            return got, swap(first_in, nxt), swap(meta, top)

        return branch

    sizes = range(0, limit + 1, step)
    packed, first_in = after((packed, first_in))
    packed_in, relay, meta_in = lax.switch(longest[0, 0], [cross(size) for size in sizes], packed, first_in, meta)
    middle, packed_in = after((middle, packed_in))
    middle_in = swap(middle, top)
    own, *hands = part_call(begins, packed_in)
    held, copy, known, start, twice, bounds, goals = second_call(second_in, relay, first_in, meta_in, held)
    own, second_in, relay = after((own, second_in, relay))
    total = column_call(first, second_in, first_in, relay)
    sent = [None] * (HANDS - 1)
    bit = 1
    while bit < nxt:
        if bit < HANDS:
            ready = range(bit - 1, 2 * bit - 1)
            other = swap(total, bit)
            if bit == HANDS // 4:
                other, known = after((other, known))
            total, *late = after((total + other, *[hands[h] for h in ready]))
            for h, hand in zip(ready, late):
                sent[h] = swap(hand, h + 1)
        else:
            total = total + swap(total, bit)
        bit *= 2
    hands = [own, *sent]
    cents, turned, shifts, one, two, again = centre_call(
        here, twice, total, child_labels, vectors, copy, first_in, meta_in, known
    )
    told = start, bounds, turned, shifts, goals, again, first_in
    held, one, two, values = first_call(*told, (), hands, held, one, two)
    held, one, two = first_call(*told, (middle_in, values), hands, held, one, two)
    return held, one.reshape(-1), two.reshape(-1), cents


def solution(mesh):
    return jax.shard_map(
        local,
        mesh=mesh,
        in_specs=(P("cube", None), P(None, "cube")),
        out_specs=(P("cube", None), P("cube"), P("cube"), P()),
        check_vma=False,
    )
```

```python
import functools
import jax
import jax.numpy as jnp
from jax import lax
from jax.experimental import pallas as pl
from jax.experimental.pallas import tpu as pltpu
from jax.sharding import PartitionSpec as P

BF = jnp.bfloat16
F32 = jnp.float32
I32 = jnp.int32
BLK = 256
HANDS = 8
WIDE = BLK // 2 + 16
SLOTS = 128
VMEM_BYTES = 28 * 1024 * 1024


def swap(x, bits):
    return lax.ppermute(x, "cube", [(i, i ^ bits) for i in range(lax.axis_size("cube"))])


def dot(a, b):
    return lax.dot_general(a, b, (((1,), (0,)), ((), ())), preferred_element_type=F32)


def dot_t(a, b):
    return lax.dot_general(a, b, (((1,), (1,)), ((), ())), preferred_element_type=F32)


def iota(shape, dim):
    return lax.broadcasted_iota(I32, shape, dim)


def as_bf(mask):
    return jnp.where(mask, jnp.float32(1), jnp.float32(0)).astype(BF)


def pack(sums, counts, width):
    high = sums.astype(BF).astype(F32)
    middle = (sums - high).astype(BF).astype(F32)
    low = sums - high - middle
    spare = width - 128 * len(counts)
    counts = jnp.concatenate(counts + ([jnp.zeros((1, spare), I32)] if spare else []), axis=1)
    upper, lower = (counts >> 8).astype(F32), (counts & 255).astype(F32)
    return jnp.concatenate([high, middle, low, upper, lower, jnp.zeros((2, width), F32)], axis=0).astype(BF)


def unpack(extra):
    extra = extra.astype(F32)
    sums = extra[0:4] + extra[4:8] + extra[8:12]
    return sums, extra[12:13] * 256.0 + extra[13:14]


def count_at(extra, k):
    extra = extra[12:14, 128 * k : 128 * k + 1].astype(F32)
    return (extra[0:1] * 256.0 + extra[1:2]).astype(I32)


def spec(memory):
    return pl.BlockSpec(memory_space=memory)


def params():
    return pltpu.CompilerParams(vmem_limit_bytes=VMEM_BYTES)


def plan_kernel(here, labels, pos, off_ref, every, leavers):
    rows = labels.shape[1]
    blocks = rows // BLK
    leave = labels[0:1, :] != here[0]
    miss = labels[1:2, :] != here[1]
    code = jnp.where(leave, jnp.where(miss, 0, 1), jnp.where(miss, 2, 3))
    code = jnp.concatenate(
        [jnp.broadcast_to(code[:, b * BLK : (b + 1) * BLK], (8, BLK)) for b in range(blocks)], axis=0
    )
    tall = 8 * blocks
    kind = iota((tall, BLK), 0) & 7
    mask = (code == kind) | ((kind == 4) & (code <= 1))
    maskb = as_bf(mask)
    upper = as_bf(iota((BLK, BLK), 0) <= iota((BLK, BLK), 1))
    before = dot(maskb, upper)
    total = dot(maskb, jnp.ones((BLK, BLK), BF)).astype(BF)
    r, c = iota((tall, tall), 0), iota((tall, tall), 1)
    same = ((r ^ c) & 7) == 0
    earlier = as_bf((same & (c < r)) | (((r & 7) == 1) & ((c & 7) == 0)))
    off = dot(earlier, total)
    pos[...] = jnp.where(mask, (before + off).astype(I32) - 1, -1)
    off_ref[...] = (off + jnp.where(iota((tall, BLK), 1) < 64, 0.0, total.astype(F32)))[:, :128].astype(I32)
    r8, c8 = iota((8, tall), 0), iota((8, tall), 1)
    count = dot(as_bf(r8 == (c8 & 7)), total)[:, :128].astype(I32)
    every[...] = count
    leavers[...] = jnp.broadcast_to(count[4:5], leavers.shape)


def plan_call(here, labels):
    rows = labels.shape[1]
    tall = 8 * rows // BLK
    return pl.pallas_call(
        plan_kernel,
        out_shape=[
            jax.ShapeDtypeStruct((tall, BLK), I32),
            jax.ShapeDtypeStruct((tall, 128), I32),
            jax.ShapeDtypeStruct((8, 128), I32),
            jax.ShapeDtypeStruct((8, 128), I32),
        ],
        in_specs=[spec(pltpu.SMEM), spec(pltpu.VMEM)],
        out_specs=[spec(pltpu.VMEM)] * 4,
        compiler_params=params(),
        cost_estimate=pl.CostEstimate(flops=2 * 10**10, bytes_accessed=10**7, transcendentals=0),
        name="plan_places",
    )(here, labels)


def sort_kernel(here, labels, pos_ref, off_ref, every, x, first, middle, *refs):
    hands, (buf, sums) = refs[:HANDS], refs[HANDS:]
    rows = labels.shape[1]
    blocks = rows // BLK
    cap = rows // 2
    buf[...] = jnp.zeros_like(buf)
    group = 2 * labels[0:1, :] + labels[1:2, :]
    slot = iota((WIDE, BLK), 0)
    more_slot = iota((BLK + 16 - WIDE, BLK), 0) + WIDE
    sums[...] = jnp.zeros_like(sums)
    tails = []
    for b in range(blocks):
        vectors = x.at[pl.ds(b * BLK, BLK)]
        hot = [as_bf((iota((16, BLK), 0) & 3) == group[:, b * BLK : (b + 1) * BLK])]
        bases = []
        ends = []
        places = []
        for kind in (0, 1):
            line = slice(8 * b + kind, 8 * b + kind + 1)
            base = pl.multiple_of(jnp.minimum((off_ref[line, 0:1][0, 0] // 16) * 16, cap), 16)
            bases.append(base)
            ends.append(off_ref[line, 64:65][0, 0])
            places.append(pos_ref[line, :] - base)
            hot.append(as_bf(slot == places[kind]))
        got = dot(jnp.concatenate(hot, axis=0), vectors[...])
        sums[...] += got[0:8]
        got = got[16:].astype(BF)
        buf[pl.ds(bases[0], WIDE), :] += got[:WIDE]
        buf[pl.ds(bases[1], 16), :] += got[WIDE : WIDE + 16]
        buf[pl.ds(bases[1] + 16, WIDE - 16), :] = got[WIDE + 16 :]
        for kind in (0, 1):
            tails.append((b, places[kind], bases[kind], ends[kind] - bases[kind]))

    @pl.when(functools.reduce(jnp.maximum, [size for *_, size in tails]) > WIDE)
    def _():
        for b, place, base, size in tails:

            @pl.when(size > WIDE)
            def _():
                more = dot(as_bf(more_slot == place), x[b * BLK : (b + 1) * BLK, :]).astype(BF)
                buf[pl.ds(base + WIDE, BLK + 16 - WIDE), :] += more

    one, two = here[0], here[1]
    kinds = [every[k : k + 1] for k in range(4)]
    counts = []
    for g in range(4):
        away, miss = jnp.int32(g >> 1) != one, jnp.int32(g & 1) != two
        counts.append(jnp.where(away, jnp.where(miss, kinds[0], kinds[1]), jnp.where(miss, kinds[2], kinds[3])))
    part = cap // 4
    first[0:part, :] = buf[0:part, :]
    first[part:, :] = pack(sums[0:4, :], counts + [kinds[0], kinds[2]], x.shape[1])
    middle[...] = buf[part : 2 * part, :]
    for h, hand in enumerate(hands):
        for turn in range(hand.shape[0] // 16):
            block = 2 * part + 16 * (h + HANDS * turn)
            hand[16 * turn : 16 * turn + 16, :] = buf[block : block + 16, :]


def sort_call(here, labels, pos, off, every, vectors):
    rows, width = vectors.shape
    part = rows // 8
    return pl.pallas_call(
        sort_kernel,
        out_shape=[
            jax.ShapeDtypeStruct((part + 16, width), BF),
            jax.ShapeDtypeStruct((part, width), BF),
            *[jax.ShapeDtypeStruct((2 * part // HANDS, width), BF)] * HANDS,
        ],
        in_specs=[spec(pltpu.SMEM)] + [spec(pltpu.VMEM)] * 5,
        out_specs=[spec(pltpu.VMEM)] * (2 + HANDS),
        scratch_shapes=[pltpu.VMEM((rows // 2 + BLK + 16, width), BF), pltpu.VMEM((8, width), F32)],
        compiler_params=params(),
        cost_estimate=pl.CostEstimate(flops=10**4, bytes_accessed=10**3, transcendentals=0),
        name="sort_leavers",
    )(here, labels, pos, off, every, vectors)


def pack_kernel(step, me, counts, *refs):
    hands, (out, longest, begins) = refs[:HANDS], refs[HANDS:]
    rows = hands[0].shape[0]
    ways = counts.shape[0] // 8
    full = (jnp.maximum(counts[...] - rows * HANDS, 0) + 15) >> 4
    longest_pack = jnp.zeros((1, 128), I32)
    for group in range(ways // HANDS):
        lines = [full[8 * (group * HANDS + h) : 8 * (group * HANDS + h) + 1] for h in range(HANDS)]
        for other in range(HANDS):
            size = jnp.zeros((1, 128), I32)
            for h in range(HANDS):
                size = size + ((lines[other ^ h] + (HANDS - 1 - h)) >> 3)
            longest_pack = jnp.maximum(longest_pack, size)
    per = step // 16
    longest[...] = jnp.broadcast_to(jnp.minimum(longest_pack + per - 1, out.shape[0] // 16) // per, longest.shape)

    def shares(device):
        found = []
        for h in range(HANDS):
            line = pl.ds(pl.multiple_of(8 * (device ^ h), 8), 8)
            blocks = (jnp.maximum(counts[line, :][0:1] - rows * HANDS, 0) + 15) >> 4
            found.append((blocks + (HANDS - 1 - h)) >> 3)
        return found

    out[...] = jnp.zeros_like(out)
    place = jnp.zeros((1, 128), I32)
    for h, size in enumerate(shares(me[0])):
        base = pl.multiple_of(place[0, 0] * 16, 16)
        out[pl.ds(base, rows), :] = hands[h][...]
        place = jnp.minimum(place + size, (h + 1) * (rows // 16))
    place = jnp.zeros((1, 128), I32)
    for h, size in enumerate(shares(me[0] ^ (ways // 2))):
        begins[h : h + 1, :] = place * 16
        place = jnp.minimum(place + size, (h + 1) * (rows // 16))


def pack_call(step, me, counts, hands):
    rows, width = hands[0].shape
    return pl.pallas_call(
        functools.partial(pack_kernel, step),
        out_shape=[
            jax.ShapeDtypeStruct((rows * HANDS, width), BF),
            jax.ShapeDtypeStruct((8, 128), I32),
            jax.ShapeDtypeStruct((8, 128), I32),
        ],
        in_specs=[spec(pltpu.SMEM)] + [spec(pltpu.VMEM)] * (HANDS + 1),
        out_specs=[spec(pltpu.VMEM)] * 3,
        compiler_params=params(),
        cost_estimate=pl.CostEstimate(flops=0, bytes_accessed=10**5, transcendentals=0),
        name="pack_hands",
    )(me, counts, *hands)


def part_kernel(begins, pack_in, *refs):
    hands, sem = refs[:HANDS], refs[HANDS]
    rows = hands[0].shape[0]
    copies = []
    for h, hand in enumerate(hands):
        base = pl.multiple_of((begins[h, 0] // 16) * 16, 16)
        copies.append(pltpu.make_async_copy(pack_in.at[pl.ds(base, rows)], hand, sem.at[h]))
    for copy in copies:
        copy.start()
    for copy in copies:
        copy.wait()


def part_call(begins, pack_in):
    rows, width = pack_in.shape
    return pl.pallas_call(
        part_kernel,
        out_shape=[jax.ShapeDtypeStruct((rows // HANDS, width), BF)] * HANDS,
        in_specs=[spec(pltpu.SMEM), spec(pl.ANY)],
        out_specs=[spec(pl.ANY)] * HANDS,
        scratch_shapes=[pltpu.SemaphoreType.DMA((HANDS,))],
        compiler_params=params(),
        cost_estimate=pl.CostEstimate(flops=0, bytes_accessed=3 * 10**6, transcendentals=0),
        name="part_pack",
    )(begins, pack_in)


def second_send_kernel(off, pos, first, x, second, buf):
    half = second.shape[0] - 16
    buf[...] = jnp.zeros_like(buf)
    slot = iota((WIDE, BLK), 0)
    more_slot = iota((BLK + 16 - WIDE, BLK), 0) + WIDE
    tails = []
    for b in range(x.shape[0] // BLK):
        line = slice(8 * b + 2, 8 * b + 3)
        base = pl.multiple_of(jnp.minimum((off[line, 0:1][0, 0] // 16) * 16, half), 16)
        place = pos[line, :] - base
        got = dot(as_bf(slot == place), x[b * BLK : (b + 1) * BLK, :]).astype(BF)
        buf[pl.ds(base, 16), :] += got[:16]
        buf[pl.ds(base + 16, WIDE - 16), :] = got[16:]
        tails.append((b, place, base, off[line, 64:65][0, 0] - base))

    @pl.when(functools.reduce(jnp.maximum, [size for *_, size in tails]) > WIDE)
    def _():
        for b, place, base, size in tails:

            @pl.when(size > WIDE)
            def _():
                more = dot(as_bf(more_slot == place), x[b * BLK : (b + 1) * BLK, :]).astype(BF)
                buf[pl.ds(base + WIDE, BLK + 16 - WIDE), :] += more

    second[0:half, :] = buf[0:half, :]
    second[half:, :] = first[half:, :]


def second_send_call(off, pos, first, x):
    rows, width = x.shape
    half = rows // 8
    return pl.pallas_call(
        second_send_kernel,
        out_shape=jax.ShapeDtypeStruct((half + 16, width), BF),
        in_specs=[spec(pltpu.VMEM)] * 4,
        out_specs=spec(pltpu.VMEM),
        scratch_shapes=[pltpu.VMEM((half + BLK + 16, width), BF)],
        compiler_params=params(),
        cost_estimate=pl.CostEstimate(flops=10**4, bytes_accessed=10**3, transcendentals=0),
        name="second_send",
    )(off, pos, first, x)


def rank_kernel(off, pos, meta, ranks):
    ranks[...] = jnp.zeros_like(ranks)
    cap = 8 * meta.shape[1]
    line = iota((16, BLK), 0)
    slot = iota((BLK + 128, BLK), 0)
    for b in range(pos.shape[0] // 8):
        rank = pos[8 * b + 4 : 8 * b + 5, :]
        value = jnp.where(line == 0, rank >> 8, jnp.where(line == 1, rank & 255, 1))
        value = jnp.where(rank >= 0, value, 0).astype(F32).astype(BF)
        for kind in (0, 1):
            row = slice(8 * b + kind, 8 * b + kind + 1)
            base = pl.multiple_of(jnp.minimum((off[row, 0:1][0, 0] // 128) * 128, cap), 128)
            ranks[:, pl.ds(base, BLK + 128)] += dot_t(value, as_bf(slot == pos[row, :] - base))[:8]
    seen = ranks[2:3, :cap] > 0.5
    rank = (ranks[0:1, :cap] * 256.0 + ranks[1:2, :cap]).astype(I32)
    goal = jnp.where(seen, rank, 1 << 20)
    line = cap // 8
    for k in range(8):
        meta[k : k + 1, :] = goal[:, k * line : (k + 1) * line]


def rank_call(off, pos):
    cap = pos.shape[0] // 8 * BLK // 2
    return pl.pallas_call(
        rank_kernel,
        out_shape=jax.ShapeDtypeStruct((8, cap // 8), I32),
        in_specs=[spec(pltpu.VMEM)] * 2,
        out_specs=spec(pltpu.VMEM),
        scratch_shapes=[pltpu.VMEM((8, cap + BLK + 128), F32)],
        compiler_params=params(),
        cost_estimate=pl.CostEstimate(flops=10**4, bytes_accessed=10**3, transcendentals=0),
        name="list_ranks",
    )(off, pos)


def own_kernel(pos, x, held):
    same = iota((BLK, BLK), 0) == iota((BLK, BLK), 1)
    start = pl.program_id(0) * held.shape[0]
    for sub in range(held.shape[0] // BLK):
        keep = as_bf(same & (pos[8 * sub + 3 : 8 * sub + 4, :] >= 0))
        held[sub * BLK : (sub + 1) * BLK, :] = dot(keep, x[pl.ds(start + sub * BLK, BLK), :]).astype(BF)


def own_call(pos, x):
    rows, width = x.shape
    return pl.pallas_call(
        own_kernel,
        grid=(rows // 1024,),
        out_shape=jax.ShapeDtypeStruct((rows + rows // 2 + rows // 4, width), BF),
        in_specs=[pl.BlockSpec((8 * 1024 // BLK, BLK), lambda b: (b, 0)), spec(pltpu.VMEM)],
        out_specs=pl.BlockSpec((1024, width), lambda b: (b, 0)),
        compiler_params=params(),
        cost_estimate=pl.CostEstimate(flops=10**4, bytes_accessed=10**3, transcendentals=0),
        name="own_slots",
    )(pos, x)


def scores(x, turned):
    score = dot(x, turned)
    lane = iota(score.shape, 1)
    high = score.astype(BF).astype(F32)
    middle = (score - high).astype(BF).astype(F32)
    terms = jnp.where(lane < 4, high, jnp.where(lane < 8, middle, score - high - middle)).astype(BF)
    lane = iota((16, 128), 1)
    return dot_t(as_bf(((lane & 3) == iota((16, 128), 0)) & (lane < 12)), terms)


def margins(score, shift, first, width):
    return (score[first + 1 : first + 2] - score[first : first + 1] - shift) / width


def put_lines(ref, start, values):
    for k in range(values.shape[1] // 128):
        ref[start + k : start + k + 1, :] = values[:, 128 * k : 128 * (k + 1)]


def centre_kernel(here, total, labels, x_ref, cents, turned, shifts, one, two):
    width = x_ref.shape[1]
    lines = labels.shape[1]

    @pl.when(pl.program_id(0) == 0)
    def _():
        sums, counts = total[0:4, :], total[4:8, :]
        low = (sums[0:1] + sums[1:2]) / (counts[0:1] + counts[1:2])
        high = (sums[2:3] + sums[3:4]) / (counts[2:3] + counts[3:4])
        groups = sums / counts
        cents[0:1, :] = low
        cents[1:2, :] = high
        cents[2:6, :] = groups
        top = here[0] == 1
        left = jnp.where(top, groups[2:3], groups[0:1])
        right = jnp.where(top, groups[3:4], groups[1:2])
        rows = jnp.concatenate([low, high, left, right] * 3 + [jnp.zeros((116, width), F32)], axis=0)
        turned[...] = rows.T.astype(BF)
        for k, (a, b) in enumerate(((low, high), (left, right))):
            shift = 0.5 * (jnp.sum(b * b, axis=1, keepdims=True) - jnp.sum(a * a, axis=1, keepdims=True))
            shifts[k : k + 1, :] = jnp.broadcast_to(shift, (1, 128))

    score = scores(x_ref[pl.ds(pl.program_id(0) * lines, lines), :], turned[...])
    stay = labels[0:1, :] == here[0]
    keep = stay & (labels[1:2, :] == here[1])
    put_lines(one, 0, jnp.where(stay, margins(score, shifts[0:1, 0:1], 0, width), 0.0))
    put_lines(two, 0, jnp.where(keep, margins(score, shifts[1:2, 0:1], 2, width), 0.0))


def centre_call(here, total, labels, vectors):
    rows, width = vectors.shape
    cap = rows // 2
    return pl.pallas_call(
        centre_kernel,
        grid=(rows // 1024,),
        out_shape=[
            jax.ShapeDtypeStruct((6, width), F32),
            jax.ShapeDtypeStruct((width, 128), BF),
            jax.ShapeDtypeStruct((8, 128), F32),
            jax.ShapeDtypeStruct(((rows + cap) // 128, 128), F32),
            jax.ShapeDtypeStruct(((rows + cap + cap // 2) // 128, 128), F32),
        ],
        in_specs=[
            spec(pltpu.SMEM),
            pl.BlockSpec((8, width), lambda b: (0, 0)),
            pl.BlockSpec((2, 1024), lambda b: (0, b)),
            spec(pltpu.VMEM),
        ],
        out_specs=[
            pl.BlockSpec((6, width), lambda b: (0, 0)),
            pl.BlockSpec((width, 128), lambda b: (0, 0)),
            pl.BlockSpec((8, 128), lambda b: (0, 0)),
            pl.BlockSpec((8, 128), lambda b: (b, 0)),
            pl.BlockSpec((8, 128), lambda b: (b, 0)),
        ],
        compiler_params=params(),
        cost_estimate=pl.CostEstimate(flops=10**8, bytes_accessed=10**5, transcendentals=0),
        name="own_margins",
    )(here, total, labels, vectors)


def second_kernel(turned, shifts, second, relay, first, meta, leavers, held_in, two_in, held, two, again, alone, start, goals):
    del held_in, two_in
    half = second.shape[0] - 16
    slots = held.shape[0]
    cap = 2 * slots
    have = count_at(second[half:, :], 5)
    more = count_at(relay[half:, :], 4)
    both = count_at(first[half:, :], 4)
    lane = iota((1, half), 1)
    goal = jnp.where(lane < more, lane + have, -1)
    moved = dot(as_bf(iota((slots, half), 0) == goal), relay[0:half, :]).astype(BF)
    held[0:half, :] = moved[0:half] + second[0:half, :]
    held[half:, :] = moved[half:]
    score = scores(held[...], turned[...])
    width = held.shape[1]
    live = iota((1, slots), 1) < have + more
    put_lines(two, 0, jnp.where(live, margins(score, shifts[1:2, 0:1], 2, width), 0.0))

    score = scores(first[0:half, :], turned[...])
    value = jnp.where(lane < both, margins(score, shifts[0:1, 0:1], 0, width), 0.0)
    high = value.astype(BF).astype(F32)
    middle = (value - high).astype(BF).astype(F32)
    low = value - high - middle
    value = jnp.concatenate([high, middle, low, jnp.ones((1, half), F32), jnp.zeros((12, half), F32)], axis=0).astype(BF)
    place = jnp.concatenate([meta[k : k + 1, :] for k in range(8)], axis=1)
    goal = jnp.where(lane < both, place[:, :half], -1)
    for k in range(cap // BLK):
        hot = as_bf(iota((BLK, half), 0) + k * BLK == goal)
        got = dot_t(value, hot)
        put_lines(again, k * BLK // 128, got[0:1] + got[1:2] + got[2:3])
        free = (iota((1, BLK), 1) + k * BLK < leavers[0:1, 0:1]) & (got[3:4] < 0.5)
        put_lines(alone, k * BLK // 128, jnp.where(free, 1.0, 0.0))
    lines = cap // SLOTS
    lane = iota((lines, cap), 1)
    earlier = (lane < both) | (place < SLOTS * iota((lines, cap), 0))
    begin = jnp.sum(jnp.where(earlier, 1.0, 0.0), axis=1, keepdims=True).astype(I32)
    begin = jnp.minimum((begin >> 7) << 7, cap - SLOTS - 128)
    start[...] = jnp.broadcast_to(begin, start.shape)
    goals[...] = jnp.broadcast_to(jnp.where(iota((1, cap), 1) < both, -1, place), goals.shape)


def second_call(turned, shifts, second, relay, first, meta, leavers, held, two):
    half, width = second.shape
    half -= 16
    cap = 4 * half
    slots = cap // 2
    return pl.pallas_call(
        second_kernel,
        grid=(1,),
        out_shape=[
            jax.ShapeDtypeStruct(held.shape, BF),
            jax.ShapeDtypeStruct(two.shape, F32),
            jax.ShapeDtypeStruct((cap // 128, 128), F32),
            jax.ShapeDtypeStruct((cap // 128, 128), F32),
            jax.ShapeDtypeStruct((cap // SLOTS, 128), I32),
            jax.ShapeDtypeStruct((8, cap), I32),
        ],
        in_specs=[spec(pltpu.VMEM)] * 7 + [spec(pl.ANY)] * 2,
        out_specs=[
            pl.BlockSpec((slots, width), lambda b: (held.shape[0] // slots - 1, 0)),
            pl.BlockSpec((slots // 128, 128), lambda b: (held.shape[0] // slots - 1, 0)),
            pl.BlockSpec((cap // 128, 128), lambda b: (0, 0)),
            pl.BlockSpec((cap // 128, 128), lambda b: (0, 0)),
            pl.BlockSpec((cap // SLOTS, 128), lambda b: (0, 0)),
            pl.BlockSpec((8, cap), lambda b: (0, 0)),
        ],
        input_output_aliases={7: 0, 8: 1},
        compiler_params=params(),
        cost_estimate=pl.CostEstimate(flops=10**8, bytes_accessed=10**5, transcendentals=0),
        name="second_slots",
    )(turned, shifts, second, relay, first, meta, leavers, held, two)


def column_kernel(own, a, b, c, out):
    sums, counts = unpack(own[...])
    for other in (a, b, c):
        s, n = unpack(other[...])
        sums, counts = sums + s, counts + n
    out[0:4, :] = sums
    width = out.shape[1]
    for g in range(4):
        out[4 + g : 5 + g, :] = jnp.broadcast_to(counts[:, 128 * g : 128 * g + 1], (1, width))


def column_call(*pieces):
    width = pieces[0].shape[1]
    return pl.pallas_call(
        column_kernel,
        grid=(1,),
        out_shape=jax.ShapeDtypeStruct((8, width), F32),
        in_specs=[pl.BlockSpec((16, width), functools.partial(lambda last, b: (last, 0), p.shape[0] // 16 - 1)) for p in pieces],
        out_specs=pl.BlockSpec((8, width), lambda b: (0, 0)),
        compiler_params=params(),
        name="column_sums",
    )(*pieces)


def first_kernel(start, turned, shifts, goals, again, alone, first, middle, *refs):
    hands, (held_in, one_in, two_in, held, one, two, x, out, sent) = refs[:HANDS], refs[HANDS:]
    del one_in, two_in, held_in
    part, width = middle.shape
    x[0:part, :] = first[0:part, :]
    x[part : 2 * part, :] = middle[...]
    for h, hand in enumerate(hands):
        for turn in range(hand.shape[0] // 16):
            block = 2 * part + 16 * (h + HANDS * turn)
            x[block : block + 16, :] = hand[16 * turn : 16 * turn + 16, :]
    span = SLOTS + 128
    base = 8 * part
    slot = iota((SLOTS, span), 0)
    group = 4
    stores = []
    for k in range(4 * part // SLOTS):
        begin = pl.multiple_of(start[k, 0], 128)
        hot = as_bf(slot == goals[0:1, pl.ds(begin, span)] - k * SLOTS)
        out[k * SLOTS : (k + 1) * SLOTS, :] = dot(hot, x[pl.ds(begin, span), :]).astype(BF)
        if k % group == group - 1:
            size = group * SLOTS
            lines = pl.ds((k + 1) * SLOTS - size, size)
            to = held.at[pl.ds(base + (k + 1) * SLOTS - size, size)]
            stores.append(pltpu.make_async_copy(out.at[lines], to, sent.at[k // group]))
            stores[-1].start()
            score = scores(out[lines, :], turned[...])
            m_one = margins(score, shifts[0:1, 0:1], 0, width)
            m_two = margins(score, shifts[1:2, 0:1], 2, width)
            for i in range(size // 128):
                line = (k + 1) * SLOTS // 128 - size // 128 + i
                line = slice(line, line + 1)
                lanes = slice(128 * i, 128 * (i + 1))
                one[line, :] = jnp.where(alone[line, :] > 0.5, m_one[:, lanes], again[line, :])
                two[line, :] = jnp.where(alone[line, :] > 0.5, m_two[:, lanes], 0.0)
    for store in stores:
        store.wait()


def first_call(start, turned, shifts, goals, again, alone, first, middle, hands, held, one, two):
    width = held.shape[1]
    cap = goals.shape[1]
    lines = cap // 128
    return pl.pallas_call(
        first_kernel,
        grid=(1,),
        out_shape=[
            jax.ShapeDtypeStruct(held.shape, BF),
            jax.ShapeDtypeStruct(one.shape, F32),
            jax.ShapeDtypeStruct(two.shape, F32),
        ],
        in_specs=[spec(pltpu.SMEM)] + [spec(pltpu.VMEM)] * (HANDS + 7) + [spec(pl.ANY)] * 3,
        out_specs=[
            spec(pl.ANY),
            pl.BlockSpec((lines, 128), lambda k: (2, 0)),
            pl.BlockSpec((lines, 128), lambda k: (2, 0)),
        ],
        scratch_shapes=[
            pltpu.VMEM((cap, width), BF),
            pltpu.VMEM((cap, width), BF),
            pltpu.SemaphoreType.DMA((cap // BLK,)),
        ],
        input_output_aliases={8 + HANDS: 0, 9 + HANDS: 1, 10 + HANDS: 2},
        compiler_params=params(),
        cost_estimate=pl.CostEstimate(flops=3 * 10**9, bytes_accessed=7 * 10**6, transcendentals=0),
        name="first_slots",
    )(start, turned, shifts, goals, again, alone, first, middle, *hands, held, one, two)


def local(vectors, child_labels):
    ways = lax.axis_size("cube")
    top = ways // 2
    nxt = ways // 4
    me = lax.axis_index("cube")
    here = jnp.stack([(me // top) & 1, (me // nxt) & 1]).astype(I32)
    after = lax.optimization_barrier
    pos, off, every, leavers = plan_call(here, child_labels)
    counts = lax.all_gather(leavers, "cube", axis=0, tiled=True)
    first, middle, own, *hands = sort_call(here, child_labels, pos, off, every, vectors)
    first_in = swap(first, top)
    second = second_send_call(off, pos, first, vectors)
    second_in = swap(second, nxt)
    own, second, *hands = after((own, second, *hands))
    hands = [own] + [swap(hand, h + 1) for h, hand in enumerate(hands)]
    after_deal, hands[1] = after((pos, hands[1]))
    meta = rank_call(off, after_deal)
    held = own_call(after_deal, vectors)
    limit = 2 * middle.shape[0]
    step = limit // 32
    held, meta, hands[7] = after((held, meta, hands[7]))
    partner = lax.dynamic_slice_in_dim(counts, 8 * (me ^ top), 8, 0)
    packed, longest, begins = pack_call(step, me.astype(I32)[None], counts, hands)

    def cross(size):
        def branch(rows, first_in, meta):
            got = jnp.pad(swap(rows[:size], top), ((0, limit - size), (0, 0))) if size else jnp.zeros_like(rows)
            return got, swap(first_in, nxt), swap(meta, top)

        return branch

    sizes = range(0, limit + 1, step)
    packed, first_in = after((packed, first_in))
    packed_in, relay, meta_in = lax.switch(longest[0, 0], [cross(size) for size in sizes], packed, first_in, meta)
    middle, packed_in = after((middle, packed_in))
    middle_in = swap(middle, top)
    own, *hands = part_call(begins, packed_in)
    hands = [own] + [swap(hand, h + 1) for h, hand in enumerate(hands)]
    second_in, hands[1] = after((second_in, hands[1]))
    total = column_call(first, second_in, first_in, relay)
    bit = 1
    while bit < nxt:
        total = total + swap(total, bit)
        bit *= 2
    cents, turned, shifts, one, two = centre_call(here, total, child_labels, vectors)
    held, two, again, alone, start, goals = second_call(
        turned, shifts, second_in, relay, first_in, meta_in, partner, held, two
    )
    held, one, two = first_call(
        start, turned, shifts, goals, again, alone, first_in, middle_in, hands, held, one, two
    )
    return held, one.reshape(-1), two.reshape(-1), cents


def solution(mesh):
    return jax.shard_map(
        local,
        mesh=mesh,
        in_specs=(P("cube", None), P(None, "cube")),
        out_specs=(P("cube", None), P("cube"), P("cube"), P()),
        check_vma=False,
    )
```

```python
import functools
import jax
import jax.numpy as jnp
from jax import lax
from jax.experimental import pallas as pl
from jax.experimental.pallas import tpu as pltpu
from jax.sharding import PartitionSpec as P

BF = jnp.bfloat16
F32 = jnp.float32
I32 = jnp.int32
BLK = 256
HANDS = 8
WIDE = BLK // 2 + 16
SLOTS = 128
VMEM_BYTES = 28 * 1024 * 1024


def swap(x, bits):
    return lax.ppermute(x, "cube", [(i, i ^ bits) for i in range(lax.axis_size("cube"))])


def dot(a, b):
    return lax.dot_general(a, b, (((1,), (0,)), ((), ())), preferred_element_type=F32)


def dot_t(a, b):
    return lax.dot_general(a, b, (((1,), (1,)), ((), ())), preferred_element_type=F32)


def iota(shape, dim):
    return lax.broadcasted_iota(I32, shape, dim)


def as_bf(mask):
    return jnp.where(mask, jnp.float32(1), jnp.float32(0)).astype(BF)


def pack(sums, counts, width):
    high = sums.astype(BF).astype(F32)
    middle = (sums - high).astype(BF).astype(F32)
    low = sums - high - middle
    spare = width - 128 * len(counts)
    counts = jnp.concatenate(counts + ([jnp.zeros((1, spare), I32)] if spare else []), axis=1)
    upper, lower = (counts >> 8).astype(F32), (counts & 255).astype(F32)
    return jnp.concatenate([high, middle, low, upper, lower, jnp.zeros((2, width), F32)], axis=0).astype(BF)


def unpack(extra):
    extra = extra.astype(F32)
    sums = extra[0:4] + extra[4:8] + extra[8:12]
    return sums, extra[12:13] * 256.0 + extra[13:14]


def count_at(extra, k):
    extra = extra[12:14, 128 * k : 128 * k + 1].astype(F32)
    return (extra[0:1] * 256.0 + extra[1:2]).astype(I32)


def spec(memory):
    return pl.BlockSpec(memory_space=memory)


def params():
    return pltpu.CompilerParams(vmem_limit_bytes=VMEM_BYTES)


def plan_kernel(here, labels, pos, off_ref, every, leavers):
    rows = labels.shape[1]
    blocks = rows // BLK
    leave = labels[0:1, :] != here[0]
    miss = labels[1:2, :] != here[1]
    code = jnp.where(leave, jnp.where(miss, 0, 1), jnp.where(miss, 2, 3))
    code = jnp.concatenate(
        [jnp.broadcast_to(code[:, b * BLK : (b + 1) * BLK], (8, BLK)) for b in range(blocks)], axis=0
    )
    tall = 8 * blocks
    kind = iota((tall, BLK), 0) & 7
    mask = (code == kind) | ((kind == 4) & (code <= 1))
    maskb = as_bf(mask)
    upper = as_bf(iota((BLK, BLK), 0) <= iota((BLK, BLK), 1))
    before = dot(maskb, upper)
    total = dot(maskb, jnp.ones((BLK, BLK), BF)).astype(BF)
    r, c = iota((tall, tall), 0), iota((tall, tall), 1)
    same = ((r ^ c) & 7) == 0
    earlier = as_bf((same & (c < r)) | (((r & 7) == 1) & ((c & 7) == 0)))
    off = dot(earlier, total)
    pos[...] = jnp.where(mask, (before + off).astype(I32) - 1, -1)
    off_ref[...] = (off + jnp.where(iota((tall, BLK), 1) < 64, 0.0, total.astype(F32)))[:, :128].astype(I32)
    r8, c8 = iota((8, tall), 0), iota((8, tall), 1)
    count = dot(as_bf(r8 == (c8 & 7)), total)[:, :128].astype(I32)
    every[...] = count
    leavers[...] = jnp.broadcast_to(count[4:5], leavers.shape)


def plan_call(here, labels):
    rows = labels.shape[1]
    tall = 8 * rows // BLK
    return pl.pallas_call(
        plan_kernel,
        out_shape=[
            jax.ShapeDtypeStruct((tall, BLK), I32),
            jax.ShapeDtypeStruct((tall, 128), I32),
            jax.ShapeDtypeStruct((8, 128), I32),
            jax.ShapeDtypeStruct((8, 128), I32),
        ],
        in_specs=[spec(pltpu.SMEM), spec(pltpu.VMEM)],
        out_specs=[spec(pltpu.VMEM)] * 4,
        compiler_params=params(),
        cost_estimate=pl.CostEstimate(flops=2 * 10**10, bytes_accessed=10**7, transcendentals=0),
        name="plan_places",
    )(here, labels)


def sort_kernel(here, labels, pos_ref, off_ref, every, x, first, middle, rest, buf, sums):
    rows = labels.shape[1]
    blocks = rows // BLK
    cap = rows // 2
    buf[...] = jnp.zeros_like(buf)
    group = 2 * labels[0:1, :] + labels[1:2, :]
    slot = iota((WIDE, BLK), 0)
    more_slot = iota((BLK + 16 - WIDE, BLK), 0) + WIDE
    sums[...] = jnp.zeros_like(sums)
    tails = []
    for b in range(blocks):
        vectors = x.at[pl.ds(b * BLK, BLK)]
        hot = [as_bf((iota((16, BLK), 0) & 3) == group[:, b * BLK : (b + 1) * BLK])]
        bases = []
        ends = []
        places = []
        for kind in (0, 1):
            line = slice(8 * b + kind, 8 * b + kind + 1)
            base = pl.multiple_of(jnp.minimum((off_ref[line, 0:1][0, 0] // 16) * 16, cap), 16)
            bases.append(base)
            ends.append(off_ref[line, 64:65][0, 0])
            places.append(pos_ref[line, :] - base)
            hot.append(as_bf(slot == places[kind]))
        got = dot(jnp.concatenate(hot, axis=0), vectors[...])
        sums[...] += got[0:8]
        got = got[16:].astype(BF)
        buf[pl.ds(bases[0], WIDE), :] += got[:WIDE]
        buf[pl.ds(bases[1], 16), :] += got[WIDE : WIDE + 16]
        buf[pl.ds(bases[1] + 16, WIDE - 16), :] = got[WIDE + 16 :]
        for kind in (0, 1):
            tails.append((b, places[kind], bases[kind], ends[kind] - bases[kind]))

    @pl.when(functools.reduce(jnp.maximum, [size for *_, size in tails]) > WIDE)
    def _():
        for b, place, base, size in tails:

            @pl.when(size > WIDE)
            def _():
                more = dot(as_bf(more_slot == place), x[b * BLK : (b + 1) * BLK, :]).astype(BF)
                buf[pl.ds(base + WIDE, BLK + 16 - WIDE), :] += more

    one, two = here[0], here[1]
    kinds = [every[k : k + 1] for k in range(4)]
    counts = []
    for g in range(4):
        away, miss = jnp.int32(g >> 1) != one, jnp.int32(g & 1) != two
        counts.append(jnp.where(away, jnp.where(miss, kinds[0], kinds[1]), jnp.where(miss, kinds[2], kinds[3])))
    part = cap // 4
    first[0:part, :] = buf[0:part, :]
    first[part:, :] = pack(sums[0:4, :], counts + [kinds[0], kinds[2]], x.shape[1])
    middle[...] = buf[part : 2 * part, :]
    rest[...] = buf[2 * part : cap, :]


def sort_call(here, labels, pos, off, every, vectors):
    rows, width = vectors.shape
    part = rows // 8
    return pl.pallas_call(
        sort_kernel,
        out_shape=[
            jax.ShapeDtypeStruct((part + 16, width), BF),
            jax.ShapeDtypeStruct((part, width), BF),
            jax.ShapeDtypeStruct((2 * part, width), BF),
        ],
        in_specs=[spec(pltpu.SMEM)] + [spec(pltpu.VMEM)] * 5,
        out_specs=[spec(pltpu.VMEM)] * 3,
        scratch_shapes=[pltpu.VMEM((rows // 2 + BLK + 16, width), BF), pltpu.VMEM((8, width), F32)],
        compiler_params=params(),
        cost_estimate=pl.CostEstimate(flops=8 * 10**9, bytes_accessed=10 * 10**6, transcendentals=0),
        name="sort_leavers",
    )(here, labels, pos, off, every, vectors)


def deal_kernel(rest, own, near, top, far, *hands):
    rows, width = rest.shape
    turns = rows // 16 // HANDS
    counts = jnp.concatenate([ref[0:1, :] for ref in (own, near, top, far)], axis=1)
    counts = jnp.concatenate([counts, jnp.zeros((1, width - 512), I32)], axis=1)
    upper, lower = (counts >> 8).astype(F32), (counts & 255).astype(F32)
    tail = jnp.concatenate([upper, lower, jnp.zeros((14, width), F32)], axis=0).astype(BF)
    for h, hand in enumerate(hands):
        for turn in range(turns):
            block = 16 * (h + HANDS * turn)
            hand[16 * turn : 16 * turn + 16, :] = rest[block : block + 16, :]
        hand[16 * turns :, :] = tail


def deal_call(rest, *counts):
    rows, width = rest.shape
    turns = rows // 16 // HANDS
    return pl.pallas_call(
        deal_kernel,
        out_shape=[jax.ShapeDtypeStruct((16 * turns + 16, width), BF)] * HANDS,
        in_specs=[spec(pltpu.VMEM)] * 5,
        out_specs=[spec(pltpu.VMEM)] * HANDS,
        compiler_params=params(),
        cost_estimate=pl.CostEstimate(flops=0, bytes_accessed=10**5, transcendentals=0),
        name="deal_rest",
    )(rest, *counts)


def pack_kernel(step, *refs):
    hands, (out, longest, begins) = refs[:HANDS], refs[HANDS:]
    rows = hands[0].shape[0] - 16
    out[...] = jnp.zeros_like(out)
    full = []
    for hand in hands:
        count = hand[rows : rows + 2, 0:512].astype(F32)
        count = (count[0:1] * 256.0 + count[1:2]).astype(I32)
        full.append((jnp.maximum(count - rows * HANDS, 0) + 15) >> 4)
    place = jnp.zeros((1, 512), I32)
    for h, hand in enumerate(hands):
        base = pl.multiple_of(place[0, 0] * 16, 16)
        out[pl.ds(base, rows), :] = hand[0:rows, :]
        begins[h : h + 1, :] = place[:, 256:384] * 16
        place = jnp.minimum(place + ((full[h] + (HANDS - 1 - h)) >> 3), (h + 1) * (rows // 16))
    most = jnp.zeros((1, 512), I32)
    for other in range(HANDS):
        size = jnp.zeros((1, 512), I32)
        for h in range(HANDS):
            size = size + ((full[other ^ h] + (HANDS - 1 - h)) >> 3)
        most = jnp.maximum(most, size)
    most = jnp.max(most.astype(F32), axis=1, keepdims=True).astype(I32)
    per = step // 16
    longest[...] = jnp.broadcast_to(jnp.minimum(most + per - 1, out.shape[0] // 16) // per, longest.shape)


def pack_call(step, hands):
    rows, width = hands[0].shape
    rows -= 16
    return pl.pallas_call(
        functools.partial(pack_kernel, step),
        out_shape=[
            jax.ShapeDtypeStruct((rows * HANDS, width), BF),
            jax.ShapeDtypeStruct((8, 128), I32),
            jax.ShapeDtypeStruct((8, 128), I32),
        ],
        in_specs=[spec(pltpu.VMEM)] * HANDS,
        out_specs=[spec(pltpu.VMEM)] * 3,
        compiler_params=params(),
        cost_estimate=pl.CostEstimate(flops=0, bytes_accessed=10**5, transcendentals=0),
        name="pack_hands",
    )(*hands)


def part_kernel(begins, pack_in, *refs):
    hands, sem = refs[:HANDS], refs[HANDS]
    rows = hands[0].shape[0]
    copies = []
    for h, hand in enumerate(hands):
        base = pl.multiple_of((begins[h, 0] // 16) * 16, 16)
        copies.append(pltpu.make_async_copy(pack_in.at[pl.ds(base, rows)], hand, sem.at[h]))
    for copy in copies:
        copy.start()
    for copy in copies:
        copy.wait()


def part_call(begins, pack_in):
    rows, width = pack_in.shape
    return pl.pallas_call(
        part_kernel,
        out_shape=[jax.ShapeDtypeStruct((rows // HANDS, width), BF)] * HANDS,
        in_specs=[spec(pltpu.SMEM), spec(pl.ANY)],
        out_specs=[spec(pl.ANY)] * HANDS,
        scratch_shapes=[pltpu.SemaphoreType.DMA((HANDS,))],
        compiler_params=params(),
        cost_estimate=pl.CostEstimate(flops=0, bytes_accessed=10**5, transcendentals=0),
        name="part_pack",
    )(begins, pack_in)


def second_send_kernel(off, pos, first, x, second, buf):
    half = second.shape[0] - 16
    buf[...] = jnp.zeros_like(buf)
    slot = iota((WIDE, BLK), 0)
    more_slot = iota((BLK + 16 - WIDE, BLK), 0) + WIDE
    tails = []
    for b in range(x.shape[0] // BLK):
        line = slice(8 * b + 2, 8 * b + 3)
        base = pl.multiple_of(jnp.minimum((off[line, 0:1][0, 0] // 16) * 16, half), 16)
        place = pos[line, :] - base
        got = dot(as_bf(slot == place), x[b * BLK : (b + 1) * BLK, :]).astype(BF)
        buf[pl.ds(base, 16), :] += got[:16]
        buf[pl.ds(base + 16, WIDE - 16), :] = got[16:]
        tails.append((b, place, base, off[line, 64:65][0, 0] - base))

    @pl.when(functools.reduce(jnp.maximum, [size for *_, size in tails]) > WIDE)
    def _():
        for b, place, base, size in tails:

            @pl.when(size > WIDE)
            def _():
                more = dot(as_bf(more_slot == place), x[b * BLK : (b + 1) * BLK, :]).astype(BF)
                buf[pl.ds(base + WIDE, BLK + 16 - WIDE), :] += more

    second[0:half, :] = buf[0:half, :]
    second[half:, :] = first[half:, :]


def second_send_call(off, pos, first, x):
    rows, width = x.shape
    half = rows // 8
    return pl.pallas_call(
        second_send_kernel,
        out_shape=jax.ShapeDtypeStruct((half + 16, width), BF),
        in_specs=[spec(pltpu.VMEM)] * 4,
        out_specs=spec(pltpu.VMEM),
        scratch_shapes=[pltpu.VMEM((half + BLK + 16, width), BF)],
        compiler_params=params(),
        cost_estimate=pl.CostEstimate(flops=10**8, bytes_accessed=10**6, transcendentals=0),
        name="second_send",
    )(off, pos, first, x)


def rank_kernel(off, pos, meta, ranks):
    ranks[...] = jnp.zeros_like(ranks)
    cap = 8 * meta.shape[1]
    line = iota((16, BLK), 0)
    slot = iota((BLK + 128, BLK), 0)
    for b in range(pos.shape[0] // 8):
        rank = pos[8 * b + 4 : 8 * b + 5, :]
        value = jnp.where(line == 0, rank >> 8, jnp.where(line == 1, rank & 255, 1))
        value = jnp.where(rank >= 0, value, 0).astype(F32).astype(BF)
        for kind in (0, 1):
            row = slice(8 * b + kind, 8 * b + kind + 1)
            base = pl.multiple_of(jnp.minimum((off[row, 0:1][0, 0] // 128) * 128, cap), 128)
            ranks[:, pl.ds(base, BLK + 128)] += dot_t(value, as_bf(slot == pos[row, :] - base))[:8]
    seen = ranks[2:3, :cap] > 0.5
    rank = (ranks[0:1, :cap] * 256.0 + ranks[1:2, :cap]).astype(I32)
    goal = jnp.where(seen, rank, 1 << 20)
    line = cap // 8
    for k in range(8):
        meta[k : k + 1, :] = goal[:, k * line : (k + 1) * line]


def rank_call(off, pos):
    cap = pos.shape[0] // 8 * BLK // 2
    return pl.pallas_call(
        rank_kernel,
        out_shape=jax.ShapeDtypeStruct((8, cap // 8), I32),
        in_specs=[spec(pltpu.VMEM)] * 2,
        out_specs=spec(pltpu.VMEM),
        scratch_shapes=[pltpu.VMEM((8, cap + BLK + 128), F32)],
        compiler_params=params(),
        cost_estimate=pl.CostEstimate(flops=10**8, bytes_accessed=10**6, transcendentals=0),
        name="list_ranks",
    )(off, pos)


def own_kernel(pos, x, held):
    same = iota((BLK, BLK), 0) == iota((BLK, BLK), 1)
    start = pl.program_id(0) * held.shape[0]
    for sub in range(held.shape[0] // BLK):
        keep = as_bf(same & (pos[8 * sub + 3 : 8 * sub + 4, :] >= 0))
        held[sub * BLK : (sub + 1) * BLK, :] = dot(keep, x[pl.ds(start + sub * BLK, BLK), :]).astype(BF)


def own_call(pos, x):
    rows, width = x.shape
    return pl.pallas_call(
        own_kernel,
        grid=(rows // 1024,),
        out_shape=jax.ShapeDtypeStruct((rows + rows // 2 + rows // 4, width), BF),
        in_specs=[pl.BlockSpec((8 * 1024 // BLK, BLK), lambda b: (b, 0)), spec(pltpu.VMEM)],
        out_specs=pl.BlockSpec((1024, width), lambda b: (b, 0)),
        compiler_params=params(),
        cost_estimate=pl.CostEstimate(flops=10**8, bytes_accessed=10**6, transcendentals=0),
        name="own_slots",
    )(pos, x)


def scores(x, turned):
    score = dot(x, turned)
    lane = iota(score.shape, 1)
    high = score.astype(BF).astype(F32)
    middle = (score - high).astype(BF).astype(F32)
    terms = jnp.where(lane < 4, high, jnp.where(lane < 8, middle, score - high - middle)).astype(BF)
    lane = iota((16, 128), 1)
    return dot_t(as_bf(((lane & 3) == iota((16, 128), 0)) & (lane < 12)), terms)


def margins(score, shift, first, width):
    return (score[first + 1 : first + 2] - score[first : first + 1] - shift) / width


def put_lines(ref, start, values):
    for k in range(values.shape[1] // 128):
        ref[start + k : start + k + 1, :] = values[:, 128 * k : 128 * (k + 1)]


def split(values):
    terms = []
    for value in values:
        high = value.astype(BF).astype(F32)
        middle = (value - high).astype(BF).astype(F32)
        terms += [high, middle, value - high - middle]
    return jnp.concatenate(terms + [jnp.zeros((16 - len(terms), values[0].shape[1]), F32)], axis=0).astype(BF)


def second_kernel(second, relay, first, meta, held_in, held, copy, known, start, twice, bounds, goals):
    del held_in
    half = second.shape[0] - 16
    slots = held.shape[0]
    cap = 2 * slots
    have = count_at(second[half:, :], 5)
    more = count_at(relay[half:, :], 4)
    both = count_at(first[half:, :], 4)
    lane = iota((1, half), 1)
    goal = jnp.where(lane < more, lane + have, -1)
    moved = dot(as_bf(iota((slots, half), 0) == goal), relay[0:half, :]).astype(BF)
    held[0:half, :] = moved[0:half] + second[0:half, :]
    held[half:, :] = moved[half:]
    copy[...] = held[...]
    known[...] = jnp.broadcast_to(jnp.where(iota((8, 1), 0) == 0, have + more, both), known.shape)
    place = jnp.concatenate([meta[k : k + 1, :] for k in range(8)], axis=1)
    lines = cap // SLOTS
    own = iota((1, cap), 1) < both
    edge = SLOTS * iota((lines, cap), 0)
    before = jnp.sum(jnp.where(own | (place < edge), 1.0, 0.0), axis=1, keepdims=True)
    begin = jnp.minimum((before.astype(I32) >> 7) << 7, cap - SLOTS - 128)
    start[...] = jnp.broadcast_to(begin, start.shape)
    before = jnp.sum(jnp.where(own & (place < edge), 1.0, 0.0), axis=1, keepdims=True)
    begin = jnp.minimum((before.astype(I32) >> 7) << 7, half - SLOTS - 128)
    twice[...] = jnp.broadcast_to(begin, twice.shape)
    edge = 2 * SLOTS * iota((lines // 2, cap), 0)
    before = jnp.sum(jnp.where(own | (place < edge), 1.0, 0.0), axis=1, keepdims=True)
    until = jnp.sum(jnp.where(own | (place < edge + 2 * SLOTS), 1.0, 0.0), axis=1, keepdims=True)
    low = jnp.sum(jnp.where(until <= half, 1.0, 0.0), axis=0, keepdims=True).astype(I32)
    high = jnp.sum(jnp.where(before < 2 * half, 1.0, 0.0), axis=0, keepdims=True).astype(I32)
    bounds[...] = jnp.broadcast_to(jnp.where(iota((8, 1), 0) == 0, low, high), bounds.shape)
    goals[...] = jnp.broadcast_to(jnp.where(own, -1, place), goals.shape)


def second_call(second, relay, first, meta, held):
    half, width = second.shape
    half -= 16
    cap = 4 * half
    slots = cap // 2
    return pl.pallas_call(
        second_kernel,
        grid=(1,),
        out_shape=[
            jax.ShapeDtypeStruct(held.shape, BF),
            jax.ShapeDtypeStruct((slots, width), BF),
            jax.ShapeDtypeStruct((8, 128), I32),
            jax.ShapeDtypeStruct((cap // SLOTS, 128), I32),
            jax.ShapeDtypeStruct((cap // SLOTS, 128), I32),
            jax.ShapeDtypeStruct((8, 128), I32),
            jax.ShapeDtypeStruct((8, cap), I32),
        ],
        in_specs=[spec(pltpu.VMEM)] * 4 + [spec(pl.ANY)],
        out_specs=[pl.BlockSpec((slots, width), lambda b: (held.shape[0] // slots - 1, 0))] + [spec(pltpu.VMEM)] * 6,
        input_output_aliases={4: 0},
        compiler_params=params(),
        cost_estimate=pl.CostEstimate(flops=3*10**9, bytes_accessed=10**5, transcendentals=0),
        name="second_slots",
    )(second, relay, first, meta, held)


def centre_kernel(here, twice, total, labels, x, second, first, meta, known, cents, turned, shifts, one, two, again, value, goal):
    rows, width = x.shape
    part = 1024
    sums, counts = total[0:4, :], total[4:8, :]
    low = (sums[0:1] + sums[1:2]) / (counts[0:1] + counts[1:2])
    high = (sums[2:3] + sums[3:4]) / (counts[2:3] + counts[3:4])
    groups = sums / counts
    cents[0:1, :] = low
    cents[1:2, :] = high
    cents[2:6, :] = groups
    top = here[0] == 1
    left = jnp.where(top, groups[2:3], groups[0:1])
    right = jnp.where(top, groups[3:4], groups[1:2])
    columns = jnp.concatenate([low, high, left, right] * 3 + [jnp.zeros((116, width), F32)], axis=0).T.astype(BF)
    turned[...] = columns
    gaps = []
    for k, (a, b) in enumerate(((low, high), (left, right))):
        gaps.append(0.5 * (jnp.sum(b * b, axis=1, keepdims=True) - jnp.sum(a * a, axis=1, keepdims=True)))
        shifts[k : k + 1, :] = jnp.broadcast_to(gaps[k], (1, 128))
    shifts[2:, :] = jnp.zeros((6, 128), F32)
    one[rows // 128 :, :] = jnp.zeros((rows // 256, 128), F32)
    two[rows // 128 : 3 * rows // 256, :] = jnp.zeros((rows // 256, 128), F32)
    stay = labels[0:1, :] == here[0]
    keep = stay & (labels[1:2, :] == here[1])
    for k in range(rows // part):
        lanes = slice(k * part, (k + 1) * part)
        score = scores(x[lanes, :], columns)
        put_lines(one, k * part // 128, jnp.where(stay[:, lanes], margins(score, gaps[0], 0, width), 0.0))
        put_lines(two, k * part // 128, jnp.where(keep[:, lanes], margins(score, gaps[1], 2, width), 0.0))
    score = scores(second[...], columns)
    live = iota((1, second.shape[0]), 1) < known[0:1, 0:1]
    put_lines(two, 3 * rows // 256, jnp.where(live, margins(score, gaps[1], 2, width), 0.0))
    half = first.shape[0] - 16
    both = iota((1, half), 1) < known[1:2, 0:1]
    score = scores(first[0:half, :], columns)
    value[...] = split([jnp.where(both, margins(score, gaps[0], 0, width), 0.0)])
    place = jnp.concatenate([meta[k : k + 1, :] for k in range(half // meta.shape[1])], axis=1)
    goal[...] = jnp.broadcast_to(jnp.where(both, place, -1), goal.shape)
    span = SLOTS + 128
    for k in range(4 * half // SLOTS):
        lanes = pl.ds(pl.multiple_of((twice[k, 0] // 128) * 128, 128), span)
        got = dot_t(value[:, lanes], as_bf(iota((SLOTS, span), 0) + k * SLOTS == goal[0:1, lanes]))
        put_lines(again, k * SLOTS // 128, got[0:1] + got[1:2] + got[2:3])


def centre_call(here, twice, total, labels, vectors, second, first, meta, known):
    rows, width = vectors.shape
    cap = rows // 2
    return pl.pallas_call(
        centre_kernel,
        out_shape=[
            jax.ShapeDtypeStruct((6, width), F32),
            jax.ShapeDtypeStruct((width, 128), BF),
            jax.ShapeDtypeStruct((8, 128), F32),
            jax.ShapeDtypeStruct(((rows + cap) // 128, 128), F32),
            jax.ShapeDtypeStruct(((rows + cap + cap // 2) // 128, 128), F32),
            jax.ShapeDtypeStruct((cap // 128, 128), F32),
        ],
        in_specs=[spec(pltpu.SMEM)] * 2 + [spec(pltpu.VMEM)] * 7,
        out_specs=[spec(pltpu.VMEM)] * 6,
        scratch_shapes=[pltpu.VMEM((16, cap // 4), BF), pltpu.VMEM((8, cap // 4), I32)],
        compiler_params=params(),
        cost_estimate=pl.CostEstimate(flops=10**8, bytes_accessed=10**5, transcendentals=0),
        name="all_margins",
    )(here, twice, total, labels, vectors, second, first, meta, known)


def column_kernel(own, a, b, c, out):
    sums, counts = unpack(own[...])
    for other in (a, b, c):
        s, n = unpack(other[...])
        sums, counts = sums + s, counts + n
    out[0:4, :] = sums
    width = out.shape[1]
    for g in range(4):
        out[4 + g : 5 + g, :] = jnp.broadcast_to(counts[:, 128 * g : 128 * g + 1], (1, width))


def column_call(*pieces):
    width = pieces[0].shape[1]
    return pl.pallas_call(
        column_kernel,
        grid=(1,),
        out_shape=jax.ShapeDtypeStruct((8, width), F32),
        in_specs=[pl.BlockSpec((16, width), functools.partial(lambda last, b: (last, 0), p.shape[0] // 16 - 1)) for p in pieces],
        out_specs=pl.BlockSpec((8, width), lambda b: (0, 0)),
        compiler_params=params(),
        cost_estimate=pl.CostEstimate(flops=0, bytes_accessed=10**5, transcendentals=0),
        name="column_sums",
    )(*pieces)


def first_kernel(late, start, bounds, turned, shifts, goals, again, first, *refs):
    (middle, past, *refs) = refs if late else (None, None, *refs)
    hands, refs = refs[:HANDS], refs[HANDS:]
    held_in, one_in, two_in, held, one, two, values, x, out, sent = refs
    del held_in
    width = first.shape[1]
    part = first.shape[0] - 16
    pairs = 4 * part // (2 * SLOTS)

    def weigh(begin):
        lanes = slice(begin, begin + part)
        score = scores(x[lanes, :], turned[...])
        m_one = margins(score, shifts[0:1, 0:1], 0, width)
        values[:, lanes] = split([m_one, margins(score, shifts[1:2, 0:1], 2, width)])

    reach = 2 * SLOTS
    low = part - reach if late else 0
    x[low:part, :] = first[low:part, :]
    x[part : 2 * part, :] = middle[...] if late else jnp.zeros((part, width), BF)
    for h, hand in enumerate(hands):
        for turn in range(reach // 16 // HANDS if late else hand.shape[0] // 16):
            block = 2 * part + 16 * (h + HANDS * turn)
            x[block : block + 16, :] = hand[16 * turn : 16 * turn + 16, :]
    if late:
        one[...] = one_in[...]
        two[...] = two_in[...]
        values[...] = past[...]
        weigh(part)
    else:
        one[...] = jnp.zeros_like(one)
        two[...] = jnp.zeros_like(two)
        values[:, part : 2 * part] = jnp.zeros((16, part), BF)
        for k in (0, 2, 3):
            weigh(k * part)
    span = SLOTS + 128
    base = 8 * part
    slot = iota((SLOTS, span), 0)

    def store(pair):
        lines = pl.multiple_of(pair * 2 * SLOTS, 2 * SLOTS)
        to = held.at[pl.ds(base + lines, 2 * SLOTS)]
        return pltpu.make_async_copy(out.at[pl.ds(lines, 2 * SLOTS)], to, sent.at[pair])

    def place_block(k):
        lines = pl.multiple_of(k * SLOTS, SLOTS)
        begin = pl.multiple_of((start[k, 0] // 128) * 128, 128)
        hot = as_bf(slot == goals[0:1, pl.ds(begin, span)] - lines)
        out[pl.ds(lines, SLOTS), :] = dot(hot, x[pl.ds(begin, span), :]).astype(BF)
        got = dot_t(values[:, pl.ds(begin, span)], hot)
        line = pl.ds(k, 1)
        one[line, :] = got[0:1] + got[1:2] + got[2:3] + again[line, :]
        two[line, :] = got[3:4] + got[4:5] + got[5:6]

    def place(pair, _):
        for i in range(2):
            place_block(2 * pair + i)
        store(pair).start()
        return 0

    def place_two(step, first_pair):
        for i in range(4):
            place_block(2 * (first_pair + 2 * step) + i)
        for i in range(2):
            store(first_pair + 2 * step + i).start()
        return first_pair

    def finish(pair, _):
        store(pair).wait()
        return 0

    low = jnp.minimum(bounds[0, 0], pairs)
    high = jnp.clip(bounds[1, 0], low, pairs)
    ranges = [(low, high)] if late else [(0, low), (high, pairs)]
    for begin, end in ranges:
        twos = (end - begin) // 2
        lax.fori_loop(0, twos, place_two, begin)
        lax.fori_loop(begin + 2 * twos, end, place, 0)
    for begin, end in ranges:
        lax.fori_loop(begin, end, finish, 0)


def first_call(start, bounds, turned, shifts, goals, again, first, added, hands, held, one, two):
    width = held.shape[1]
    cap = goals.shape[1]
    lines = cap // 128
    late = bool(added)
    pieces = [first, *added, *hands]
    block = pl.BlockSpec((lines, 128), lambda k: (2, 0))
    given = 6 + len(pieces)
    kept = jax.ShapeDtypeStruct((16, cap), BF)
    return pl.pallas_call(
        functools.partial(first_kernel, late),
        grid=(1,),
        out_shape=[
            jax.ShapeDtypeStruct(held.shape, BF),
            jax.ShapeDtypeStruct(one.shape, F32),
            jax.ShapeDtypeStruct(two.shape, F32),
        ]
        + ([] if late else [kept]),
        in_specs=[spec(pltpu.SMEM)] * 2
        + [spec(pltpu.VMEM)] * (given - 2)
        + [spec(pl.ANY)]
        + ([block] * 2 if late else [spec(pl.ANY)] * 2),
        out_specs=[spec(pl.ANY), block, block] + ([] if late else [spec(pltpu.VMEM)]),
        scratch_shapes=([pltpu.VMEM((16, cap), BF)] if late else [])
        + [
            pltpu.VMEM((cap, width), BF),
            pltpu.VMEM((cap, width), BF),
            pltpu.SemaphoreType.DMA((cap // (2 * SLOTS),)),
        ],
        input_output_aliases={given: 0, given + 1: 1, given + 2: 2},
        compiler_params=params(),
        cost_estimate=pl.CostEstimate(flops=10**8, bytes_accessed=10**5, transcendentals=0),
        name="last_slots" if late else "first_slots",
    )(start, bounds, turned, shifts, goals, again, *pieces, held, one, two)


def local(vectors, child_labels):
    ways = lax.axis_size("cube")
    top = ways // 2
    nxt = ways // 4
    me = lax.axis_index("cube")
    here = jnp.stack([(me // top) & 1, (me // nxt) & 1]).astype(I32)
    after = lax.optimization_barrier
    pos, off, every, leavers = plan_call(here, child_labels)
    counts = [leavers] + [swap(leavers, bits) for bits in (nxt, top, top | nxt)]
    first, middle, rest = sort_call(here, child_labels, pos, off, every, vectors)
    first, *counts = after((first, *counts))
    first_in = swap(first, top)
    second = second_send_call(off, pos, first, vectors)
    second_in = swap(second, nxt)
    rest, second = after((rest, second))
    own, *hands = deal_call(rest, *counts)
    hands = [own] + [swap(hand, h + 1) for h, hand in enumerate(hands)]
    after_deal, hands[1] = after((pos, hands[1]))
    meta = rank_call(off, after_deal)
    held = own_call(after_deal, vectors)
    limit = rest.shape[0]
    step = limit // 32
    held, meta, hands[7] = after((held, meta, hands[7]))
    packed, longest, begins = pack_call(step, hands)
    bit = HANDS
    while bit < nxt:
        longest = jnp.maximum(longest, swap(longest, bit))
        bit *= 2

    def cross(size):
        def branch(rows, first_in, meta):
            got = jnp.pad(swap(rows[:size], top), ((0, limit - size), (0, 0))) if size else jnp.zeros_like(rows)
            return got, swap(first_in, nxt), swap(meta, top)

        return branch

    sizes = range(0, limit + 1, step)
    packed, first_in = after((packed, first_in))
    packed_in, relay, meta_in = lax.switch(longest[0, 0], [cross(size) for size in sizes], packed, first_in, meta)
    middle, packed_in = after((middle, packed_in))
    middle_in = swap(middle, top)
    own, *hands = part_call(begins, packed_in)
    hands = [own] + [swap(hand, h + 1) for h, hand in enumerate(hands)]
    second_in, relay, hands[1] = after((second_in, relay, hands[1]))
    held, copy, known, start, twice, bounds, goals = second_call(second_in, relay, first_in, meta_in, held)
    total = column_call(first, second_in, first_in, relay)
    bit = 1
    while bit < nxt:
        other = swap(total, bit)
        if bit == HANDS // 4:
            other, known = after((other, known))
        total = total + other
        bit *= 2
    cents, turned, shifts, one, two, again = centre_call(
        here, twice, total, child_labels, vectors, copy, first_in, meta_in, known
    )
    told = start, bounds, turned, shifts, goals, again, first_in
    held, one, two, values = first_call(*told, (), hands, held, one, two)
    held, one, two = first_call(*told, (middle_in, values), hands, held, one, two)
    return held, one.reshape(-1), two.reshape(-1), cents


def solution(mesh):
    return jax.shard_map(
        local,
        mesh=mesh,
        in_specs=(P("cube", None), P(None, "cube")),
        out_specs=(P("cube", None), P("cube"), P("cube"), P()),
        check_vma=False,
    )
```

```python
import functools
import jax
import jax.numpy as jnp
from jax import lax
from jax.experimental import pallas as pl
from jax.experimental.pallas import tpu as pltpu
from jax.sharding import PartitionSpec as P

BF = jnp.bfloat16
F32 = jnp.float32
I32 = jnp.int32
BLK = 256
HANDS = 8
WIDE = BLK // 2 + 16
SLOTS = 128
VMEM_BYTES = 28 * 1024 * 1024


def swap(x, bits):
    return lax.ppermute(x, "cube", [(i, i ^ bits) for i in range(lax.axis_size("cube"))])


def dot(a, b):
    return lax.dot_general(a, b, (((1,), (0,)), ((), ())), preferred_element_type=F32)


def dot_t(a, b):
    return lax.dot_general(a, b, (((1,), (1,)), ((), ())), preferred_element_type=F32)


def iota(shape, dim):
    return lax.broadcasted_iota(I32, shape, dim)


def as_bf(mask):
    return jnp.where(mask, jnp.float32(1), jnp.float32(0)).astype(BF)


def pack(sums, counts, width):
    high = sums.astype(BF).astype(F32)
    middle = (sums - high).astype(BF).astype(F32)
    low = sums - high - middle
    spare = width - 128 * len(counts)
    counts = jnp.concatenate(counts + ([jnp.zeros((1, spare), I32)] if spare else []), axis=1)
    upper, lower = (counts >> 8).astype(F32), (counts & 255).astype(F32)
    return jnp.concatenate([high, middle, low, upper, lower, jnp.zeros((2, width), F32)], axis=0).astype(BF)


def unpack(extra):
    extra = extra.astype(F32)
    sums = extra[0:4] + extra[4:8] + extra[8:12]
    return sums, extra[12:13] * 256.0 + extra[13:14]


def count_at(extra, k):
    extra = extra[12:14, 128 * k : 128 * k + 1].astype(F32)
    return (extra[0:1] * 256.0 + extra[1:2]).astype(I32)


def spec(memory):
    return pl.BlockSpec(memory_space=memory)


def params():
    return pltpu.CompilerParams(vmem_limit_bytes=VMEM_BYTES)


def plan_kernel(here, labels, pos, off_ref, every, leavers):
    rows = labels.shape[1]
    blocks = rows // BLK
    leave = labels[0:1, :] != here[0]
    miss = labels[1:2, :] != here[1]
    code = jnp.where(leave, jnp.where(miss, 0, 1), jnp.where(miss, 2, 3))
    code = jnp.concatenate(
        [jnp.broadcast_to(code[:, b * BLK : (b + 1) * BLK], (8, BLK)) for b in range(blocks)], axis=0
    )
    tall = 8 * blocks
    kind = iota((tall, BLK), 0) & 7
    mask = (code == kind) | ((kind == 4) & (code <= 1))
    maskb = as_bf(mask)
    upper = as_bf(iota((BLK, BLK), 0) <= iota((BLK, BLK), 1))
    before = dot(maskb, upper)
    total = dot(maskb, jnp.ones((BLK, BLK), BF)).astype(BF)
    r, c = iota((tall, tall), 0), iota((tall, tall), 1)
    same = ((r ^ c) & 7) == 0
    earlier = as_bf((same & (c < r)) | (((r & 7) == 1) & ((c & 7) == 0)))
    off = dot(earlier, total)
    pos[...] = jnp.where(mask, (before + off).astype(I32) - 1, -1)
    off_ref[...] = (off + jnp.where(iota((tall, BLK), 1) < 64, 0.0, total.astype(F32)))[:, :128].astype(I32)
    r8, c8 = iota((8, tall), 0), iota((8, tall), 1)
    count = dot(as_bf(r8 == (c8 & 7)), total)[:, :128].astype(I32)
    every[...] = count
    leavers[...] = jnp.broadcast_to(count[4:5], leavers.shape)


def plan_call(here, labels):
    rows = labels.shape[1]
    tall = 8 * rows // BLK
    return pl.pallas_call(
        plan_kernel,
        out_shape=[
            jax.ShapeDtypeStruct((tall, BLK), I32),
            jax.ShapeDtypeStruct((tall, 128), I32),
            jax.ShapeDtypeStruct((8, 128), I32),
            jax.ShapeDtypeStruct((8, 128), I32),
        ],
        in_specs=[spec(pltpu.SMEM), spec(pltpu.VMEM)],
        out_specs=[spec(pltpu.VMEM)] * 4,
        compiler_params=params(),
        cost_estimate=pl.CostEstimate(flops=2 * 10**10, bytes_accessed=10**7, transcendentals=0),
        name="plan_places",
    )(here, labels)


def sort_kernel(here, labels, pos_ref, off_ref, every, x, first, middle, rest, buf, sums):
    rows = labels.shape[1]
    blocks = rows // BLK
    cap = rows // 2
    buf[...] = jnp.zeros_like(buf)
    group = 2 * labels[0:1, :] + labels[1:2, :]
    slot = iota((WIDE, BLK), 0)
    more_slot = iota((BLK + 16 - WIDE, BLK), 0) + WIDE
    sums[...] = jnp.zeros_like(sums)
    tails = []
    for b in range(blocks):
        vectors = x.at[pl.ds(b * BLK, BLK)]
        hot = [as_bf((iota((16, BLK), 0) & 3) == group[:, b * BLK : (b + 1) * BLK])]
        bases = []
        ends = []
        places = []
        for kind in (0, 1):
            line = slice(8 * b + kind, 8 * b + kind + 1)
            base = pl.multiple_of(jnp.minimum((off_ref[line, 0:1][0, 0] // 16) * 16, cap), 16)
            bases.append(base)
            ends.append(off_ref[line, 64:65][0, 0])
            places.append(pos_ref[line, :] - base)
            hot.append(as_bf(slot == places[kind]))
        got = dot(jnp.concatenate(hot, axis=0), vectors[...])
        sums[...] += got[0:8]
        got = got[16:].astype(BF)
        buf[pl.ds(bases[0], WIDE), :] += got[:WIDE]
        buf[pl.ds(bases[1], 16), :] += got[WIDE : WIDE + 16]
        buf[pl.ds(bases[1] + 16, WIDE - 16), :] = got[WIDE + 16 :]
        for kind in (0, 1):
            tails.append((b, places[kind], bases[kind], ends[kind] - bases[kind]))

    @pl.when(functools.reduce(jnp.maximum, [size for *_, size in tails]) > WIDE)
    def _():
        for b, place, base, size in tails:

            @pl.when(size > WIDE)
            def _():
                more = dot(as_bf(more_slot == place), x[b * BLK : (b + 1) * BLK, :]).astype(BF)
                buf[pl.ds(base + WIDE, BLK + 16 - WIDE), :] += more

    one, two = here[0], here[1]
    kinds = [every[k : k + 1] for k in range(4)]
    counts = []
    for g in range(4):
        away, miss = jnp.int32(g >> 1) != one, jnp.int32(g & 1) != two
        counts.append(jnp.where(away, jnp.where(miss, kinds[0], kinds[1]), jnp.where(miss, kinds[2], kinds[3])))
    part = cap // 4
    first[0:part, :] = buf[0:part, :]
    first[part:, :] = pack(sums[0:4, :], counts + [kinds[0], kinds[2]], x.shape[1])
    middle[...] = buf[part : 2 * part, :]
    rest[...] = buf[2 * part : cap, :]


def sort_call(here, labels, pos, off, every, vectors):
    rows, width = vectors.shape
    part = rows // 8
    return pl.pallas_call(
        sort_kernel,
        out_shape=[
            jax.ShapeDtypeStruct((part + 16, width), BF),
            jax.ShapeDtypeStruct((part, width), BF),
            jax.ShapeDtypeStruct((2 * part, width), BF),
        ],
        in_specs=[spec(pltpu.SMEM)] + [spec(pltpu.VMEM)] * 5,
        out_specs=[spec(pltpu.VMEM)] * 3,
        scratch_shapes=[pltpu.VMEM((rows // 2 + BLK + 16, width), BF), pltpu.VMEM((8, width), F32)],
        compiler_params=params(),
        cost_estimate=pl.CostEstimate(flops=8 * 10**9, bytes_accessed=10 * 10**6, transcendentals=0),
        name="sort_leavers",
    )(here, labels, pos, off, every, vectors)


def deal_kernel(rest, own, near, top, far, *hands):
    rows, width = rest.shape
    turns = rows // 16 // HANDS
    counts = jnp.concatenate([ref[0:1, :] for ref in (own, near, top, far)], axis=1)
    counts = jnp.concatenate([counts, jnp.zeros((1, width - 512), I32)], axis=1)
    upper, lower = (counts >> 8).astype(F32), (counts & 255).astype(F32)
    tail = jnp.concatenate([upper, lower, jnp.zeros((14, width), F32)], axis=0).astype(BF)
    for h, hand in enumerate(hands):
        for turn in range(turns):
            block = 16 * (h + HANDS * turn)
            hand[16 * turn : 16 * turn + 16, :] = rest[block : block + 16, :]
        hand[16 * turns :, :] = tail


def deal_call(rest, *counts):
    rows, width = rest.shape
    turns = rows // 16 // HANDS
    return pl.pallas_call(
        deal_kernel,
        out_shape=[jax.ShapeDtypeStruct((16 * turns + 16, width), BF)] * HANDS,
        in_specs=[spec(pltpu.VMEM)] * 5,
        out_specs=[spec(pltpu.VMEM)] * HANDS,
        compiler_params=params(),
        cost_estimate=pl.CostEstimate(flops=0, bytes_accessed=10**5, transcendentals=0),
        name="deal_rest",
    )(rest, *counts)


def pack_kernel(sizes, *refs):
    hands, (out, longest, begins) = refs[:HANDS], refs[HANDS:]
    rows = hands[0].shape[0] - 16
    out[...] = jnp.zeros_like(out)
    full = []
    for hand in hands:
        count = hand[rows : rows + 2, 0:512].astype(F32)
        count = (count[0:1] * 256.0 + count[1:2]).astype(I32)
        full.append((jnp.maximum(count - rows * HANDS, 0) + 15) >> 4)
    place = jnp.zeros((1, 512), I32)
    for h, hand in enumerate(hands):
        base = pl.multiple_of(place[0, 0] * 16, 16)
        out[pl.ds(base, rows), :] = hand[0:rows, :]
        begins[h : h + 1, :] = place[:, 256:384] * 16
        place = jnp.minimum(place + ((full[h] + (HANDS - 1 - h)) >> 3), (h + 1) * (rows // 16))
    most = jnp.zeros((1, 512), I32)
    for other in range(HANDS):
        size = jnp.zeros((1, 512), I32)
        for h in range(HANDS):
            size = size + ((full[other ^ h] + (HANDS - 1 - h)) >> 3)
        most = jnp.maximum(most, size)
    most = jnp.max(most.astype(F32), axis=1, keepdims=True).astype(I32)
    smaller = sum(jnp.where(most * 16 > size, 1, 0) for size in sizes[:-1])
    longest[...] = jnp.broadcast_to(smaller, longest.shape)


def pack_call(sizes, hands):
    rows, width = hands[0].shape
    rows -= 16
    return pl.pallas_call(
        functools.partial(pack_kernel, sizes),
        out_shape=[
            jax.ShapeDtypeStruct((rows * HANDS, width), BF),
            jax.ShapeDtypeStruct((8, 128), I32),
            jax.ShapeDtypeStruct((8, 128), I32),
        ],
        in_specs=[spec(pltpu.VMEM)] * HANDS,
        out_specs=[spec(pltpu.VMEM)] * 3,
        compiler_params=params(),
        cost_estimate=pl.CostEstimate(flops=0, bytes_accessed=10**5, transcendentals=0),
        name="pack_hands",
    )(*hands)


def part_kernel(begins, pack_in, *refs):
    hands, sem = refs[:HANDS], refs[HANDS]
    rows = hands[0].shape[0]
    copies = []
    for h, hand in enumerate(hands):
        base = pl.multiple_of((begins[h, 0] // 16) * 16, 16)
        copies.append(pltpu.make_async_copy(pack_in.at[pl.ds(base, rows)], hand, sem.at[h]))
    for copy in copies:
        copy.start()
    for copy in copies:
        copy.wait()


def part_call(begins, pack_in):
    rows, width = pack_in.shape
    return pl.pallas_call(
        part_kernel,
        out_shape=[jax.ShapeDtypeStruct((rows // HANDS, width), BF)] * HANDS,
        in_specs=[spec(pltpu.SMEM), spec(pl.ANY)],
        out_specs=[spec(pl.ANY)] * HANDS,
        scratch_shapes=[pltpu.SemaphoreType.DMA((HANDS,))],
        compiler_params=params(),
        cost_estimate=pl.CostEstimate(flops=0, bytes_accessed=3 * 10**6, transcendentals=0),
        name="part_pack",
    )(begins, pack_in)


def second_send_kernel(off, pos, first, x, second, buf):
    half = second.shape[0] - 16
    buf[...] = jnp.zeros_like(buf)
    slot = iota((WIDE, BLK), 0)
    more_slot = iota((BLK + 16 - WIDE, BLK), 0) + WIDE
    tails = []
    for b in range(x.shape[0] // BLK):
        line = slice(8 * b + 2, 8 * b + 3)
        base = pl.multiple_of(jnp.minimum((off[line, 0:1][0, 0] // 16) * 16, half), 16)
        place = pos[line, :] - base
        got = dot(as_bf(slot == place), x[b * BLK : (b + 1) * BLK, :]).astype(BF)
        buf[pl.ds(base, 16), :] += got[:16]
        buf[pl.ds(base + 16, WIDE - 16), :] = got[16:]
        tails.append((b, place, base, off[line, 64:65][0, 0] - base))

    @pl.when(functools.reduce(jnp.maximum, [size for *_, size in tails]) > WIDE)
    def _():
        for b, place, base, size in tails:

            @pl.when(size > WIDE)
            def _():
                more = dot(as_bf(more_slot == place), x[b * BLK : (b + 1) * BLK, :]).astype(BF)
                buf[pl.ds(base + WIDE, BLK + 16 - WIDE), :] += more

    second[0:half, :] = buf[0:half, :]
    second[half:, :] = first[half:, :]


def second_send_call(off, pos, first, x):
    rows, width = x.shape
    half = rows // 8
    return pl.pallas_call(
        second_send_kernel,
        out_shape=jax.ShapeDtypeStruct((half + 16, width), BF),
        in_specs=[spec(pltpu.VMEM)] * 4,
        out_specs=spec(pltpu.VMEM),
        scratch_shapes=[pltpu.VMEM((half + BLK + 16, width), BF)],
        compiler_params=params(),
        cost_estimate=pl.CostEstimate(flops=10**8, bytes_accessed=10**6, transcendentals=0),
        name="second_send",
    )(off, pos, first, x)


def rank_kernel(off, pos, meta, ranks):
    ranks[...] = jnp.zeros_like(ranks)
    cap = 8 * meta.shape[1]
    line = iota((16, BLK), 0)
    slot = iota((BLK + 128, BLK), 0)
    for b in range(pos.shape[0] // 8):
        rank = pos[8 * b + 4 : 8 * b + 5, :]
        value = jnp.where(line == 0, rank >> 8, jnp.where(line == 1, rank & 255, 1))
        value = jnp.where(rank >= 0, value, 0).astype(F32).astype(BF)
        for kind in (0, 1):
            row = slice(8 * b + kind, 8 * b + kind + 1)
            base = pl.multiple_of(jnp.minimum((off[row, 0:1][0, 0] // 128) * 128, cap), 128)
            ranks[:, pl.ds(base, BLK + 128)] += dot_t(value, as_bf(slot == pos[row, :] - base))[:8]
    seen = ranks[2:3, :cap] > 0.5
    rank = (ranks[0:1, :cap] * 256.0 + ranks[1:2, :cap]).astype(I32)
    goal = jnp.where(seen, rank, 1 << 20)
    line = cap // 8
    for k in range(8):
        meta[k : k + 1, :] = goal[:, k * line : (k + 1) * line]


def rank_call(off, pos):
    cap = pos.shape[0] // 8 * BLK // 2
    return pl.pallas_call(
        rank_kernel,
        out_shape=jax.ShapeDtypeStruct((8, cap // 8), I32),
        in_specs=[spec(pltpu.VMEM)] * 2,
        out_specs=spec(pltpu.VMEM),
        scratch_shapes=[pltpu.VMEM((8, cap + BLK + 128), F32)],
        compiler_params=params(),
        cost_estimate=pl.CostEstimate(flops=10**8, bytes_accessed=10**6, transcendentals=0),
        name="list_ranks",
    )(off, pos)


def own_kernel(pos, x, held):
    same = iota((BLK, BLK), 0) == iota((BLK, BLK), 1)
    start = pl.program_id(0) * held.shape[0]
    for sub in range(held.shape[0] // BLK):
        keep = as_bf(same & (pos[8 * sub + 3 : 8 * sub + 4, :] >= 0))
        held[sub * BLK : (sub + 1) * BLK, :] = dot(keep, x[pl.ds(start + sub * BLK, BLK), :]).astype(BF)


def own_call(pos, x):
    rows, width = x.shape
    return pl.pallas_call(
        own_kernel,
        grid=(rows // 1024,),
        out_shape=jax.ShapeDtypeStruct((rows + rows // 2 + rows // 4, width), BF),
        in_specs=[pl.BlockSpec((8 * 1024 // BLK, BLK), lambda b: (b, 0)), spec(pltpu.VMEM)],
        out_specs=pl.BlockSpec((1024, width), lambda b: (b, 0)),
        compiler_params=params(),
        cost_estimate=pl.CostEstimate(flops=10**8, bytes_accessed=10**6, transcendentals=0),
        name="own_slots",
    )(pos, x)


def scores(x, turned):
    score = dot(x, turned)
    lane = iota(score.shape, 1)
    high = score.astype(BF).astype(F32)
    middle = (score - high).astype(BF).astype(F32)
    terms = jnp.where(lane < 4, high, jnp.where(lane < 8, middle, score - high - middle)).astype(BF)
    lane = iota((16, 128), 1)
    return dot_t(as_bf(((lane & 3) == iota((16, 128), 0)) & (lane < 12)), terms)


def margins(score, shift, first, width):
    return (score[first + 1 : first + 2] - score[first : first + 1] - shift) / width


def put_lines(ref, start, values):
    for k in range(values.shape[1] // 128):
        ref[start + k : start + k + 1, :] = values[:, 128 * k : 128 * (k + 1)]


def centre_kernel(here, total, labels, x_ref, cents, turned, shifts, one, two):
    width = x_ref.shape[1]
    lines = labels.shape[1]

    @pl.when(pl.program_id(0) == 0)
    def _():
        sums, counts = total[0:4, :], total[4:8, :]
        low = (sums[0:1] + sums[1:2]) / (counts[0:1] + counts[1:2])
        high = (sums[2:3] + sums[3:4]) / (counts[2:3] + counts[3:4])
        groups = sums / counts
        cents[0:1, :] = low
        cents[1:2, :] = high
        cents[2:6, :] = groups
        top = here[0] == 1
        left = jnp.where(top, groups[2:3], groups[0:1])
        right = jnp.where(top, groups[3:4], groups[1:2])
        rows = jnp.concatenate([low, high, left, right] * 3 + [jnp.zeros((116, width), F32)], axis=0)
        turned[...] = rows.T.astype(BF)
        for k, (a, b) in enumerate(((low, high), (left, right))):
            shift = 0.5 * (jnp.sum(b * b, axis=1, keepdims=True) - jnp.sum(a * a, axis=1, keepdims=True))
            shifts[k : k + 1, :] = jnp.broadcast_to(shift, (1, 128))

    score = scores(x_ref[pl.ds(pl.program_id(0) * lines, lines), :], turned[...])
    stay = labels[0:1, :] == here[0]
    keep = stay & (labels[1:2, :] == here[1])
    put_lines(one, 0, jnp.where(stay, margins(score, shifts[0:1, 0:1], 0, width), 0.0))
    put_lines(two, 0, jnp.where(keep, margins(score, shifts[1:2, 0:1], 2, width), 0.0))


def centre_call(here, total, labels, vectors):
    rows, width = vectors.shape
    cap = rows // 2
    return pl.pallas_call(
        centre_kernel,
        grid=(rows // 1024,),
        out_shape=[
            jax.ShapeDtypeStruct((6, width), F32),
            jax.ShapeDtypeStruct((width, 128), BF),
            jax.ShapeDtypeStruct((8, 128), F32),
            jax.ShapeDtypeStruct(((rows + cap) // 128, 128), F32),
            jax.ShapeDtypeStruct(((rows + cap + cap // 2) // 128, 128), F32),
        ],
        in_specs=[
            spec(pltpu.SMEM),
            pl.BlockSpec((8, width), lambda b: (0, 0)),
            pl.BlockSpec((2, 1024), lambda b: (0, b)),
            spec(pltpu.VMEM),
        ],
        out_specs=[
            pl.BlockSpec((6, width), lambda b: (0, 0)),
            pl.BlockSpec((width, 128), lambda b: (0, 0)),
            pl.BlockSpec((8, 128), lambda b: (0, 0)),
            pl.BlockSpec((8, 128), lambda b: (b, 0)),
            pl.BlockSpec((8, 128), lambda b: (b, 0)),
        ],
        compiler_params=params(),
        cost_estimate=pl.CostEstimate(flops=3*10**9, bytes_accessed=10**5, transcendentals=0),
        name="own_margins",
    )(here, total, labels, vectors)


def second_kernel(turned, shifts, second, relay, first, meta, leavers, held_in, two_in, held, two, again, alone, start, goals):
    del held_in, two_in
    half = second.shape[0] - 16
    slots = held.shape[0]
    cap = 2 * slots
    have = count_at(second[half:, :], 5)
    more = count_at(relay[half:, :], 4)
    both = count_at(first[half:, :], 4)
    lane = iota((1, half), 1)
    goal = jnp.where(lane < more, lane + have, -1)
    moved = dot(as_bf(iota((slots, half), 0) == goal), relay[0:half, :]).astype(BF)
    held[0:half, :] = moved[0:half] + second[0:half, :]
    held[half:, :] = moved[half:]
    score = scores(held[...], turned[...])
    width = held.shape[1]
    live = iota((1, slots), 1) < have + more
    put_lines(two, 0, jnp.where(live, margins(score, shifts[1:2, 0:1], 2, width), 0.0))

    score = scores(first[0:half, :], turned[...])
    value = jnp.where(lane < both, margins(score, shifts[0:1, 0:1], 0, width), 0.0)
    high = value.astype(BF).astype(F32)
    middle = (value - high).astype(BF).astype(F32)
    low = value - high - middle
    value = jnp.concatenate([high, middle, low, jnp.ones((1, half), F32), jnp.zeros((12, half), F32)], axis=0).astype(BF)
    place = jnp.concatenate([meta[k : k + 1, :] for k in range(8)], axis=1)
    goal = jnp.where(lane < both, place[:, :half], -1)
    for k in range(cap // BLK):
        hot = as_bf(iota((BLK, half), 0) + k * BLK == goal)
        got = dot_t(value, hot)
        put_lines(again, k * BLK // 128, got[0:1] + got[1:2] + got[2:3])
        free = (iota((1, BLK), 1) + k * BLK < leavers[0:1, 0:1]) & (got[3:4] < 0.5)
        put_lines(alone, k * BLK // 128, jnp.where(free, 1.0, 0.0))
    lines = cap // SLOTS
    lane = iota((lines, cap), 1)
    earlier = (lane < both) | (place < SLOTS * iota((lines, cap), 0))
    begin = jnp.sum(jnp.where(earlier, 1.0, 0.0), axis=1, keepdims=True).astype(I32)
    begin = jnp.minimum((begin >> 7) << 7, cap - SLOTS - 128)
    start[...] = jnp.broadcast_to(begin, start.shape)
    goals[...] = jnp.broadcast_to(jnp.where(iota((1, cap), 1) < both, -1, place), goals.shape)


def second_call(turned, shifts, second, relay, first, meta, leavers, held, two):
    half, width = second.shape
    half -= 16
    cap = 4 * half
    slots = cap // 2
    return pl.pallas_call(
        second_kernel,
        grid=(1,),
        out_shape=[
            jax.ShapeDtypeStruct(held.shape, BF),
            jax.ShapeDtypeStruct(two.shape, F32),
            jax.ShapeDtypeStruct((cap // 128, 128), F32),
            jax.ShapeDtypeStruct((cap // 128, 128), F32),
            jax.ShapeDtypeStruct((cap // SLOTS, 128), I32),
            jax.ShapeDtypeStruct((8, cap), I32),
        ],
        in_specs=[spec(pltpu.VMEM)] * 7 + [spec(pl.ANY)] * 2,
        out_specs=[
            pl.BlockSpec((slots, width), lambda b: (held.shape[0] // slots - 1, 0)),
            pl.BlockSpec((slots // 128, 128), lambda b: (held.shape[0] // slots - 1, 0)),
            pl.BlockSpec((cap // 128, 128), lambda b: (0, 0)),
            pl.BlockSpec((cap // 128, 128), lambda b: (0, 0)),
            pl.BlockSpec((cap // SLOTS, 128), lambda b: (0, 0)),
            pl.BlockSpec((8, cap), lambda b: (0, 0)),
        ],
        input_output_aliases={7: 0, 8: 1},
        compiler_params=params(),
        cost_estimate=pl.CostEstimate(flops=1*10**9, bytes_accessed=10**5, transcendentals=0),
        name="second_slots",
    )(turned, shifts, second, relay, first, meta, leavers, held, two)


def column_kernel(own, a, b, c, out):
    sums, counts = unpack(own[...])
    for other in (a, b, c):
        s, n = unpack(other[...])
        sums, counts = sums + s, counts + n
    out[0:4, :] = sums
    width = out.shape[1]
    for g in range(4):
        out[4 + g : 5 + g, :] = jnp.broadcast_to(counts[:, 128 * g : 128 * g + 1], (1, width))


def column_call(*pieces):
    width = pieces[0].shape[1]
    return pl.pallas_call(
        column_kernel,
        grid=(1,),
        out_shape=jax.ShapeDtypeStruct((8, width), F32),
        in_specs=[pl.BlockSpec((16, width), functools.partial(lambda last, b: (last, 0), p.shape[0] // 16 - 1)) for p in pieces],
        out_specs=pl.BlockSpec((8, width), lambda b: (0, 0)),
        compiler_params=params(),
        name="column_sums",
    )(*pieces)


def first_kernel(start, turned, shifts, goals, again, alone, first, middle, *refs):
    hands, (held_in, one_in, two_in, held, one, two, x, out, sent) = refs[:HANDS], refs[HANDS:]
    del one_in, two_in, held_in
    part, width = middle.shape
    x[0:part, :] = first[0:part, :]
    x[part : 2 * part, :] = middle[...]
    for h, hand in enumerate(hands):
        for turn in range(hand.shape[0] // 16):
            block = 2 * part + 16 * (h + HANDS * turn)
            x[block : block + 16, :] = hand[16 * turn : 16 * turn + 16, :]
    span = SLOTS + 128
    base = 8 * part
    slot = iota((SLOTS, span), 0)
    group = 4
    stores = []
    for k in range(4 * part // SLOTS):
        begin = pl.multiple_of(start[k, 0], 128)
        hot = as_bf(slot == goals[0:1, pl.ds(begin, span)] - k * SLOTS)
        out[k * SLOTS : (k + 1) * SLOTS, :] = dot(hot, x[pl.ds(begin, span), :]).astype(BF)
        if k % group == group - 1:
            size = group * SLOTS
            lines = pl.ds((k + 1) * SLOTS - size, size)
            to = held.at[pl.ds(base + (k + 1) * SLOTS - size, size)]
            stores.append(pltpu.make_async_copy(out.at[lines], to, sent.at[k // group]))
            stores[-1].start()
            score = scores(out[lines, :], turned[...])
            m_one = margins(score, shifts[0:1, 0:1], 0, width)
            m_two = margins(score, shifts[1:2, 0:1], 2, width)
            for i in range(size // 128):
                line = (k + 1) * SLOTS // 128 - size // 128 + i
                line = slice(line, line + 1)
                lanes = slice(128 * i, 128 * (i + 1))
                one[line, :] = jnp.where(alone[line, :] > 0.5, m_one[:, lanes], again[line, :])
                two[line, :] = jnp.where(alone[line, :] > 0.5, m_two[:, lanes], 0.0)
    for store in stores:
        store.wait()


def first_call(start, turned, shifts, goals, again, alone, first, middle, hands, held, one, two):
    width = held.shape[1]
    cap = goals.shape[1]
    lines = cap // 128
    return pl.pallas_call(
        first_kernel,
        grid=(1,),
        out_shape=[
            jax.ShapeDtypeStruct(held.shape, BF),
            jax.ShapeDtypeStruct(one.shape, F32),
            jax.ShapeDtypeStruct(two.shape, F32),
        ],
        in_specs=[spec(pltpu.SMEM)] + [spec(pltpu.VMEM)] * (HANDS + 7) + [spec(pl.ANY)] * 3,
        out_specs=[
            spec(pl.ANY),
            pl.BlockSpec((lines, 128), lambda k: (2, 0)),
            pl.BlockSpec((lines, 128), lambda k: (2, 0)),
        ],
        scratch_shapes=[
            pltpu.VMEM((cap, width), BF),
            pltpu.VMEM((cap, width), BF),
            pltpu.SemaphoreType.DMA((cap // BLK,)),
        ],
        input_output_aliases={8 + HANDS: 0, 9 + HANDS: 1, 10 + HANDS: 2},
        compiler_params=params(),
        cost_estimate=pl.CostEstimate(flops=3 * 10**9, bytes_accessed=7 * 10**6, transcendentals=0),
        name="first_slots",
    )(start, turned, shifts, goals, again, alone, first, middle, *hands, held, one, two)


def local(vectors, child_labels):
    ways = lax.axis_size("cube")
    top = ways // 2
    nxt = ways // 4
    me = lax.axis_index("cube")
    here = jnp.stack([(me // top) & 1, (me // nxt) & 1]).astype(I32)
    after = lax.optimization_barrier
    pos, off, every, leavers = plan_call(here, child_labels)
    counts = [leavers] + [swap(leavers, bits) for bits in (nxt, top, top | nxt)]
    first, middle, rest = sort_call(here, child_labels, pos, off, every, vectors)
    first, *counts = after((first, *counts))
    first_in = swap(first, top)
    second = second_send_call(off, pos, first, vectors)
    second_in = swap(second, nxt)
    rest, second = after((rest, second))
    own, *hands = deal_call(rest, *counts)
    hands = [own] + [swap(hand, h + 1) for h, hand in enumerate(hands)]
    after_deal, hands[1] = after((pos, hands[1]))
    meta = rank_call(off, after_deal)
    held = own_call(after_deal, vectors)
    limit = rest.shape[0]
    unit = limit // 32
    sizes = [n * unit for n in (0, 4, 8, 12, 14, *range(16, 28), 28, 30, 32)]
    held, meta, hands[7] = after((held, meta, hands[7]))
    packed, longest, begins = pack_call(sizes, hands)
    bit = HANDS
    while bit < nxt:
        longest = jnp.maximum(longest, swap(longest, bit))
        bit *= 2

    def cross(size):
        def branch(rows, first_in, meta):
            got = jnp.pad(swap(rows[:size], top), ((0, limit - size), (0, 0))) if size else jnp.zeros_like(rows)
            return got, swap(first_in, nxt), swap(meta, top)

        return branch

    packed, first_in = after((packed, first_in))
    packed_in, relay, meta_in = lax.switch(longest[0, 0], [cross(size) for size in sizes], packed, first_in, meta)
    middle, packed_in = after((middle, packed_in))
    middle_in = swap(middle, top)
    own, *hands = part_call(begins, packed_in)
    hands = [own] + [swap(hand, h + 1) for h, hand in enumerate(hands)]
    second_in, hands[1] = after((second_in, hands[1]))
    total = column_call(first, second_in, first_in, relay)
    bit = 1
    while bit < nxt:
        total = total + swap(total, bit)
        bit *= 2
    cents, turned, shifts, one, two = centre_call(here, total, child_labels, vectors)
    held, two, again, alone, start, goals = second_call(
        turned, shifts, second_in, relay, first_in, meta_in, counts[2], held, two
    )
    held, one, two = first_call(
        start, turned, shifts, goals, again, alone, first_in, middle_in, hands, held, one, two
    )
    return held, one.reshape(-1), two.reshape(-1), cents


def solution(mesh):
    return jax.shard_map(
        local,
        mesh=mesh,
        in_specs=(P("cube", None), P(None, "cube")),
        out_specs=(P("cube", None), P("cube"), P("cube"), P()),
        check_vma=False,
    )
```
